32 devices in a mesh: dx: 4 (over x, core), dy: 4 (over z), solid: 2 (over y).
Axes of the slice: x: 2, y: 2, z: 4, core: 2. Of those that a mesh axis runs over, the one named last changes fastest.
Arguments:
- velocity: float32 [3, 4, 4, 4, 4, 16, 256], P(None, None, None, None, 'dx', 'dy', 'solid'), may hold values from -6 to 6
- viscosity: float32 [4, 16, 256], P('dx', 'dy', 'solid'), may hold values from 0.5 to 4
- cell_config: int32 [4, 16, 256], P('dx', 'dy', 'solid'), may hold values from 0 to 7
- constraint_offsets: float32 [8, 64, 64], replicated, may hold values from -0.24 to 0.24
- slot_cells: int32 [4, 8, 64], P('dx', ('dy', 'solid')), may hold values from -1 to 511, as said below
- point_coords: float32 [3, 4, 8, 64], P(None, 'dx', ('dy', 'solid')), may hold values from 0 to 1
- strain_offsets: float32 [3, 3, 4, 8, 64], P(None, None, 'dx', ('dy', 'solid')), may hold values from -1.5 to 1.5
- solid_velocity: float32 [3, 4, 8, 64], P(None, 'dx', ('dy', 'solid')), may hold values from -6 to 6
Outputs:
- fluid_out: float32 [3, 4, 4, 4, 4, 16, 256], P(None, None, None, None, 'dx', 'dy', 'solid')
- new_deform: float32 [3, 3, 4, 8, 64], P(None, None, 'dx', ('dy', 'solid'))
The draws below stay inside these ranges and needn't reach their ends.
Inputs may be any that keep to these rules, and one draw needn't show every extreme that they name: `slot_cells`: an entry is -1 for an empty slot, else a cell of the owner numbered with x slowest and z fastest. Slots h * 8 to (h + 1) * 8 - 1 of owner o hold the points that device h keeps.
All inputs are finite; a program needn't handle non-finite values.
Results may differ from the reference program's by a relative error of at most 0.0003.
Values sent between devices are 32-bit elements; how exact they have to be, the bound alone decides.
No kernel may reach another device: no remote copies, remote signals or barrier semaphores. Data moves between devices by JAX's collectives and lax.ppermute only.
A program may use at most 64 MiB of HBM per device.

```python
import math
import jax
import jax.numpy as jnp
import numpy as np
from jax import lax

CX = 1
CY = 4
CZ = 128
CAP = 8
NCONF = 8
GROUP = 8
SLOTS = 64
CELLS = 512
NCX = 4
NCY = 16
NCZ = 256
N_DX = 4
N_DY = 4
N_SOLID = 2


def draw_slot_cells(key, part):
    keys = jax.random.split(jax.random.fold_in(key, 11), 5)
    cells = jax.random.randint(keys[0], (N_DX, GROUP, SLOTS), 0, CELLS)
    level = jax.random.randint(keys[1], (N_DX, GROUP, 1), 2, 9)
    roll = jax.random.randint(keys[2], (N_DX, GROUP, SLOTS), 0, 8)
    live = roll < level
    full_owner = jax.random.randint(keys[3], (N_DX, 1, 1), 0, GROUP)
    full_holder = jax.random.randint(keys[4], (N_DX, 1, 1), 0, GROUP)
    owners = jnp.arange(GROUP)[None, :, None]
    slots = jnp.arange(SLOTS)[None, None, :]
    in_full = (owners == full_owner) & (slots // CAP == full_holder)
    live = live | in_full
    empty_one = (owners == (full_owner + 1) % GROUP) & (slots == 0)
    live = live & jnp.logical_not(empty_one)
    top_one = (owners == full_owner) & (slots == full_holder * CAP)
    cells = jnp.where(top_one, CELLS - 1, cells)
    return jnp.where(live, cells, -1).astype(jnp.int32)


def touch_ends(values, rng, low, top_value):
    longest = values.shape.index(max(values.shape))
    spots = []
    for shift in (0, 1):
        where = [jax.random.randint(jax.random.fold_in(rng, axis), (), 0, length) for axis, length in enumerate(values.shape)]
        where[longest] = (where[longest] + shift) % values.shape[longest]
        spots.append(tuple(where))
    return values.at[spots[0]].set(low).at[spots[1]].set(top_value)


def levels(own_key, dims, pieces, low, top_value):
    gain, own = 1.0, jax.random.fold_in(own_key, 6)
    for position, shards_of in pieces:
        draws = jnp.exp(jax.random.uniform(jax.random.fold_in(own, position), (shards_of,), jnp.float32, low / len(pieces), top_value / len(pieces)))
        gain = gain * jnp.repeat(draws, dims[position] // shards_of).reshape([-1 if axis == position else 1 for axis in range(len(dims))])
    return gain


def gaussian(key, extent, width, reach, cuts=(), kind=jnp.bfloat16):
    gain = levels(key, extent, cuts, -0.22, 0.18) if cuts else 1.0
    drawn = jax.random.normal(key, extent, jnp.float32) * width * gain
    return jnp.minimum(jnp.maximum(drawn, -reach), reach).astype(kind)


def setup_inputs(seed: int = 0) -> dict:
    seeds = jax.random.split(jax.random.key(seed), 9)
    velocity = gaussian(seeds[0], (3, 4, 4, 4, NCX, NCY, NCZ), 1.0, 6.0, ((4, 4), (5, 4), (6, 2)), jnp.float32)
    viscosity = jnp.clip(jnp.exp(math.log(4.0) - 2.0794415 * jax.random.uniform(seeds[1], (NCX, NCY, NCZ), jnp.float32) ** levels(seeds[1], (NCX, NCY, NCZ), ((0, 4), (1, 4), (2, 2)), -0.2, 0.2)), 0.5, 4.0)
    cell_config = touch_ends(jax.random.randint(seeds[2], (NCX, NCY, NCZ), 0, NCONF), jax.random.fold_in(seeds[2], 1), 0, NCONF - 1).astype(jnp.int32)
    constraint_offsets = gaussian(seeds[3], (NCONF, 64, 64), 0.04, 0.24, (), jnp.float32)
    slot_cells = draw_slot_cells(jax.random.fold_in(seeds[8], 71), 0)
    point_coords = jnp.clip(1.0 * jax.random.uniform(seeds[5], (3, N_DX, GROUP, SLOTS), jnp.float32) ** levels(seeds[5], (3, N_DX, GROUP, SLOTS), ((1, 4), (2, 8)), -0.2, 0.2), 0.0, 1.0)
    strain_offsets = gaussian(seeds[6], (3, 3, N_DX, GROUP, SLOTS), 0.3, 1.5, ((2, 4), (3, 8)), jnp.float32)
    solid_velocity = gaussian(seeds[7], (3, N_DX, GROUP, SLOTS), 1.0, 6.0, ((1, 4), (2, 8)), jnp.float32)
    return dict(velocity=velocity, viscosity=viscosity, cell_config=cell_config, constraint_offsets=constraint_offsets, slot_cells=slot_cells, point_coords=point_coords, strain_offsets=strain_offsets, solid_velocity=solid_velocity)


PRECISE = lax.Precision.HIGHEST
TIME_STEP = 0.05
SPRING_RATE = 2.0
PENALTY = 4.0
STIFFNESS = np.array([[2.0, -1.0, 0.0, 0.0], [-1.0, 2.0, -1.0, 0.0], [0.0, -1.0, 2.0, -1.0], [0.0, 0.0, -1.0, 2.0]])
NODE_POINTS = (0.0, 1.0 / 3.0, 2.0 / 3.0, 1.0)


def lagrange(coord):
    values = []
    slopes = []
    for which in range(4):
        others = [NODE_POINTS[j] for j in range(4) if j != which]
        denom = 1.0
        for other in others:
            denom = denom * (NODE_POINTS[which] - other)
        first = coord - others[0]
        second = coord - others[1]
        third = coord - others[2]
        values.append(first * second * third / denom)
        slopes.append((second * third + first * third + first * second) / denom)
    return jnp.stack(values), jnp.stack(slopes)


def constrain(flat, config, offsets, transpose):
    eye = jnp.eye(64, dtype=flat.dtype)
    result = jnp.zeros_like(flat)
    for which in range(NCONF):
        matrix = eye + offsets[which]
        form = 'ji,mjn->min' if transpose else 'ij,mjn->min'
        product = jnp.einsum(form, matrix, flat, precision=PRECISE)
        result = result + jnp.where(config == which, product, 0.0)
    return result


def operate(field, padded, viscosity):
    stiff = jnp.asarray(STIFFNESS, field.dtype)
    lap = jnp.einsum('ia,kabcxyz->kibcxyz', stiff, field, precision=PRECISE)
    lap = lap + jnp.einsum('ib,kabcxyz->kaicxyz', stiff, field, precision=PRECISE)
    lap = lap + jnp.einsum('ic,kabcxyz->kabixyz', stiff, field, precision=PRECISE)
    result = field + viscosity * lap
    lower_x = padded[:, :, :, :, :-2, 1:-1, 1:-1]
    upper_x = padded[:, :, :, :, 2:, 1:-1, 1:-1]
    result = result.at[:, 0].add(PENALTY * (field[:, 0] - lower_x[:, 3]))
    result = result.at[:, 3].add(PENALTY * (field[:, 3] - upper_x[:, 0]))
    lower_y = padded[:, :, :, :, 1:-1, :-2, 1:-1]
    upper_y = padded[:, :, :, :, 1:-1, 2:, 1:-1]
    result = result.at[:, :, 0].add(PENALTY * (field[:, :, 0] - lower_y[:, :, 3]))
    result = result.at[:, :, 3].add(PENALTY * (field[:, :, 3] - upper_y[:, :, 0]))
    lower_z = padded[:, :, :, :, 1:-1, 1:-1, :-2]
    upper_z = padded[:, :, :, :, 1:-1, 1:-1, 2:]
    result = result.at[:, :, :, 0].add(PENALTY * (field[:, :, :, 0] - lower_z[:, :, :, 3]))
    result = result.at[:, :, :, 3].add(PENALTY * (field[:, :, :, 3] - upper_z[:, :, :, 0]))
    return result


def evaluate(gathered, coords):
    field = gathered.reshape(3, 4, 4, 4, -1)
    value_x, slope_x = lagrange(coords[0])
    value_y, slope_y = lagrange(coords[1])
    value_z, slope_z = lagrange(coords[2])
    along_zp = jnp.einsum('kabcs,cs->kabs', field, value_z, precision=PRECISE)
    along_zd = jnp.einsum('kabcs,cs->kabs', field, slope_z, precision=PRECISE)
    plain = jnp.einsum('kabs,bs->kas', along_zp, value_y, precision=PRECISE)
    dery = jnp.einsum('kabs,bs->kas', along_zp, slope_y, precision=PRECISE)
    derz = jnp.einsum('kabs,bs->kas', along_zd, value_y, precision=PRECISE)
    vel = jnp.einsum('kas,as->ks', plain, value_x, precision=PRECISE)
    grad_x = jnp.einsum('kas,as->ks', plain, slope_x, precision=PRECISE)
    grad_y = jnp.einsum('kas,as->ks', dery, value_x, precision=PRECISE)
    grad_z = jnp.einsum('kas,as->ks', derz, value_x, precision=PRECISE)
    return vel, jnp.stack([grad_x, grad_y, grad_z], axis=1)


def solid_update(vel, grad, strain, motion):
    eye = jnp.eye(3, dtype=strain.dtype)[:, :, None]
    deform = eye + strain
    moved = deform + TIME_STEP * jnp.einsum('kjs,jls->kls', grad, deform, precision=PRECISE)
    stress = jnp.einsum('kls,mls->kms', moved, moved, precision=PRECISE) - eye
    drag = SPRING_RATE * (motion - vel)
    return moved, stress, drag


def spread_nodes(stress, drag, coords):
    value_x, slope_x = lagrange(coords[0])
    value_y, slope_y = lagrange(coords[1])
    value_z, slope_z = lagrange(coords[2])
    shape_x = jnp.einsum('as,bs,cs->abcs', slope_x, value_y, value_z, precision=PRECISE)
    shape_y = jnp.einsum('as,bs,cs->abcs', value_x, slope_y, value_z, precision=PRECISE)
    shape_z = jnp.einsum('as,bs,cs->abcs', value_x, value_y, slope_z, precision=PRECISE)
    whole = jnp.einsum('as,bs,cs->abcs', value_x, value_y, value_z, precision=PRECISE)
    nodal = jnp.einsum('ks,abcs->kabcs', stress[:, 0], shape_x, precision=PRECISE)
    nodal = nodal + jnp.einsum('ks,abcs->kabcs', stress[:, 1], shape_y, precision=PRECISE)
    nodal = nodal + jnp.einsum('ks,abcs->kabcs', stress[:, 2], shape_z, precision=PRECISE)
    nodal = jnp.einsum('ks,abcs->kabcs', drag, whole, precision=PRECISE) - nodal
    return nodal.reshape(192, -1)


def slot_work(items):
    block, targets, coords, strain, motion = items
    live = targets >= 0
    safe = jnp.where(live, targets, 0).astype(jnp.int32)
    gathered = jnp.where(live[None, :], jnp.take(block, safe, axis=1), 0.0)
    vel, grad = evaluate(gathered, coords)
    moved, stress, drag = solid_update(vel, grad, strain, motion)
    nodal = jnp.where(live[None, :], spread_nodes(stress, drag, coords), 0.0)
    force = jnp.zeros_like(block).at[:, safe].add(nodal)
    return force, moved


def reference(velocity, viscosity, cell_config, constraint_offsets, slot_cells, point_coords, strain_offsets, solid_velocity):
    shape = velocity.shape
    count = NCX * NCY * NCZ
    config = cell_config.reshape(count)
    flat = constrain(velocity.reshape(3, 64, count), config, constraint_offsets, False)
    constrained = flat.reshape(shape)
    padded = jnp.pad(constrained, ((0, 0), (0, 0), (0, 0), (0, 0), (1, 1), (1, 1), (1, 1)))
    applied = operate(constrained, padded, viscosity)
    owned = constrained.reshape(3, 4, 4, 4, N_DX, CX, N_DY, CY, N_SOLID, CZ)
    owned = owned.transpose(4, 6, 8, 0, 1, 2, 3, 5, 7, 9).reshape(N_DX * GROUP, 192, CELLS)
    targets = slot_cells.reshape(N_DX * GROUP, SLOTS)
    coords = point_coords.transpose(1, 2, 0, 3).reshape(N_DX * GROUP, 3, SLOTS)
    strain = strain_offsets.reshape(3, 3, N_DX, GROUP, GROUP, CAP).transpose(2, 4, 0, 1, 3, 5)
    strain = strain.reshape(N_DX * GROUP, 3, 3, SLOTS)
    motion = solid_velocity.reshape(3, N_DX, GROUP, GROUP, CAP).transpose(1, 3, 0, 2, 4)
    motion = motion.reshape(N_DX * GROUP, 3, SLOTS)
    force, moved = lax.map(slot_work, (owned, targets, coords, strain, motion))
    force = force.reshape(N_DX, N_DY, N_SOLID, 3, 4, 4, 4, CX, CY, CZ)
    force = force.transpose(3, 4, 5, 6, 0, 7, 1, 8, 2, 9).reshape(3, 64, count)
    total = applied.reshape(3, 64, count) - force
    fluid_out = constrain(total, config, constraint_offsets, True).reshape(shape)
    new_deform = moved.reshape(N_DX, GROUP, 3, 3, GROUP, CAP).transpose(2, 3, 0, 4, 1, 5)
    new_deform = new_deform.reshape(3, 3, N_DX, GROUP, SLOTS)
    return fluid_out, new_deform
```

```python
import functools

import jax
import jax.numpy as jnp
from jax import lax
from jax.experimental import pallas as pl
from jax.experimental.pallas import tpu as pltpu
from jax.sharding import PartitionSpec as P

TIME_STEP = 0.05
SPRING_RATE = 2.0
PENALTY = 4.0
NODE_POINTS = (0.0, 1.0 / 3.0, 2.0 / 3.0, 1.0)
F32, BF16 = jnp.float32, jnp.bfloat16
VMEM_LIMIT = 24 * 1024 * 1024


def iota(shape, dim):
    return lax.broadcasted_iota(jnp.int32, shape, dim)


def split(x):
    high = x.astype(BF16)
    low = (x - high.astype(F32)).astype(BF16)
    return high, low


def dot(a, b, dims=((1,), (0,))):
    return lax.dot_general(a, b, (dims, ((), ())), preferred_element_type=F32)


def lagrange(coord):
    values = []
    slopes = []
    for which in range(4):
        others = [NODE_POINTS[j] for j in range(4) if j != which]
        denom = 1.0
        for other in others:
            denom = denom * (NODE_POINTS[which] - other)
        scale = 1.0 / denom
        first = coord - others[0]
        second = coord - others[1]
        third = coord - others[2]
        values.append(first * second * third * scale)
        slopes.append((second * third + first * third + first * second) * scale)
    return values, slopes


def spread_rows(parts, dim, lanes):
    wide = [jnp.broadcast_to(p, (8, lanes)) for p in parts]
    if dim == 0:
        return jnp.concatenate([wide[a] for a in (0, 0, 1, 1, 2, 2, 3, 3)], axis=0)
    row = iota((8, lanes), 0)
    if dim == 1:
        even = jnp.where(row < 4, wide[0], wide[1])
        odd = jnp.where(row < 4, wide[2], wide[3])
        return jnp.concatenate([even, odd] * 4, axis=0)
    c = row & 3
    block = jnp.where(c == 0, wide[0], jnp.where(c == 1, wide[1], jnp.where(c == 2, wide[2], wide[3])))
    return jnp.concatenate([block] * 8, axis=0)


def shapes_of(xi, lanes):
    out = []
    for dim in range(3):
        values, slopes = lagrange(xi[dim])
        out.append((spread_rows(values, dim, lanes), spread_rows(slopes, dim, lanes)))
    return out


def one_hot(slots, cells):
    lanes = slots.shape[1]
    return jnp.where(iota((cells, lanes), 0) == slots, 1.0, 0.0).astype(BF16)


def configured(product, config, nconf):
    rows = product.shape[0] // nconf
    chosen = product[:rows]
    for which in range(1, nconf):
        chosen = jnp.where(config == which, product[which * rows : (which + 1) * rows], chosen)
    return chosen


def constrain(matrix, split_ref, config_rows, add, store, nconf, nodes, comps, blocks, lanes):
    step = 2 if blocks % 2 == 0 else 1
    for k in range(comps):
        for first in range(0, blocks, step):
            col = (k * blocks + first) * lanes
            product = dot(matrix, split_ref[:, col : col + step * lanes])
            for i in range(step):
                piece = product[:, i * lanes : (i + 1) * lanes]
                y = first + i
                store(k, y, add(k, y) + configured(piece, config_rows[y], nconf))


def put_split(ref, col, lanes, nodes, value):
    high, low = split(value)
    ref[0:nodes, col : col + lanes] = high
    ref[nodes : 2 * nodes, col : col + lanes] = low
    ref[2 * nodes : 3 * nodes, col : col + lanes] = high


def before(
    dims, axes,
    v_ref, config_ref, offset_ref, slot_ref, xi_ref, strain_ref, motion_ref,
    con_ref, talk_ref, xa_ref, xb_ref, ya_ref, yb_ref, zb_ref,
    rhs_ref, field_ref,
):
    comps, nodes, cx, cy, cz, nconf, slots, has_zb = dims
    blocks = cx * cy
    me_x, me_y, me_z = (lax.axis_index(a) for a in axes)
    even_x, even_y, even_z = (me_x % 2 == 0, me_y % 2 == 0, me_z % 2 == 0)
    high, low = split(offset_ref[...])
    matrix = jnp.concatenate([high, high, low], axis=1)
    config_rows = [config_ref[y : y + 1, :] for y in range(blocks)]

    def load(k, y):
        return v_ref[pl.ds(k * nodes * blocks + y, nodes, stride=blocks), :]

    for k in range(comps):
        for y in range(blocks):
            put_split(rhs_ref, (k * blocks + y) * cz, cz, nodes, load(k, y))

    def store(k, y, value):
        field_ref[(y * comps + k) * nodes : (y * comps + k + 1) * nodes, :] = value
        part, rest = split(value)
        row = 2 * k * nodes
        con_ref[row : row + nodes, y * cz : (y + 1) * cz] = part
        con_ref[row + nodes : row + 2 * nodes, y * cz : (y + 1) * cz] = rest

    constrain(matrix, rhs_ref, config_rows, load, store, nconf, nodes, comps, blocks, cz)

    face = nodes // 4
    for k in range(comps):
        for y in range(cy):
            low_row = (y * comps + k) * nodes
            up_row = (((cx - 1) * cy + y) * comps + k + 1) * nodes
            lower = field_ref[low_row : low_row + face, :]
            upper = field_ref[up_row - face : up_row, :]
            cells = slice(y * cz, (y + 1) * cz)
            xa_ref[k * face : (k + 1) * face, cells] = jnp.where(even_x, upper, lower)
            xb_ref[k * face : (k + 1) * face, cells] = jnp.where(even_x, lower, upper)
        for a in range(4):
            into = k * face + a * 4
            for x in range(cx):
                first = (x * cy * comps + k) * nodes + a * face
                last = ((x * cy + cy - 1) * comps + k) * nodes + a * face
                lower = field_ref[first : first + 4, :]
                upper = field_ref[last + 12 : last + 16, :]
                ya_ref[into : into + 4, x * cz : (x + 1) * cz] = jnp.where(even_y, upper, lower)
                yb_ref[into : into + 4, x * cz : (x + 1) * cz] = jnp.where(even_y, lower, upper)
    rows = comps * face
    lane = iota((rows, 128), 1)
    pack_a = jnp.zeros((rows, 128), F32)
    pack_b = jnp.zeros((rows, 128), F32)
    for y in range(blocks):
        first = y * comps * nodes
        lower = pltpu.roll(field_ref[pl.ds(first, rows, stride=4), :], y, axis=1)
        upper = pltpu.roll(field_ref[pl.ds(first + 3, rows, stride=4), :], (y + 1) % cz, axis=1)
        pack_a = jnp.where(lane == y, jnp.where(even_z, upper, lower), pack_a)
        if has_zb:
            pack_b = jnp.where(lane == y, jnp.where(even_z, lower, upper), pack_b)
    talk_ref[24 : 24 + rows, 0:128] = pack_a
    if has_zb:
        zb_ref[...] = pack_b
    else:
        zb_ref[...] = jnp.zeros_like(zb_ref)

    lanes = talk_ref.shape[1]
    repeat = lanes // slots
    targets = jnp.concatenate([slot_ref[...]] * repeat, axis=1)
    xi = [jnp.concatenate([xi_ref[j]] * repeat, axis=1) for j in range(3)]
    chosen = dot(con_ref[...], one_hot(targets, blocks * cz))
    (px, dx), (py, dy), (pz, dz) = shapes_of(xi, lanes)
    whole = py * pz
    along = (px * whole, dx * whole, px * dy * pz, px * py * dz)
    for k in range(comps):
        row = 2 * k * nodes
        local = chosen[row : row + nodes] + chosen[row + nodes : row + 2 * nodes]
        talk_ref[k : k + 1, :] = jnp.sum(local * along[0], axis=0, keepdims=True)
        for j in range(3):
            at = 3 + 3 * k + j
            talk_ref[at : at + 1, :] = jnp.sum(local * along[1 + j], axis=0, keepdims=True)
    for i in range(9):
        talk_ref[12 + i : 13 + i, :] = jnp.concatenate([strain_ref[i]] * repeat, axis=1)
    for i in range(3):
        talk_ref[21 + i : 22 + i, :] = jnp.concatenate([motion_ref[i]] * repeat, axis=1)


def solid(vel, grad, strain, motion):
    deform = [strain[3 * j + l] + (1.0 if j == l else 0.0) for j in range(3) for l in range(3)]
    moved = []
    for k in range(3):
        for l in range(3):
            change = sum(grad[3 * k + j] * deform[3 * j + l] for j in range(3))
            moved.append(deform[3 * k + l] + TIME_STEP * change)
    stress = [
        sum(moved[3 * k + l] * moved[3 * m + l] for l in range(3)) - (1.0 if k == m else 0.0)
        for k in range(3) for m in range(3)
    ]
    drag = [SPRING_RATE * (motion[k] - vel[k]) for k in range(3)]
    return moved, stress, drag


def node_tables():
    i, j = iota((64, 64), 0), iota((64, 64), 1)
    digits = [((i >> s) & 3, (j >> s) & 3) for s in (4, 2, 0)]
    same = [p == q for p, q in digits]
    lap = jnp.zeros((64, 64), F32)
    swaps = []
    for d in range(3):
        others = same[(d + 1) % 3] & same[(d + 2) % 3]
        p, q = digits[d]
        line = jnp.where(p == q, 2.0, jnp.where((p - q == 1) | (q - p == 1), -1.0, 0.0))
        lap = lap + jnp.where(others, line, 0.0)
        swaps.append(jnp.where(others & (((p == 0) & (q == 3)) | ((p == 3) & (q == 0))), 1.0, 0.0))
    return jnp.concatenate([lap, swaps[2], swaps[1]], axis=0).astype(BF16)


def after(
    dims, axes, sizes,
    con_ref, viscosity_ref, config_ref, offset_ref, slot_ref, xi_ref, strain_ref, motion_ref,
    talk_ref, parts_ref, xa_ref, xb_ref, ya_ref, yb_ref, za_ref, zb_ref,
    out_ref, deform_ref,
    rhs_ref, total_ref, z_ref,
):
    comps, nodes, cx, cy, cz, nconf, slots, has_zb = dims
    blocks = cx * cy
    face = nodes // 4
    row_x = cy * cz
    index = [lax.axis_index(a) for a in axes]
    even = [i % 2 == 0 for i in index]
    open_b = [jnp.where(e, i > 0, i < n - 1) for e, i, n in zip(even, index, sizes, strict=True)]
    open_b = [jnp.where(o, 1.0, 0.0) for o in open_b]

    def sides(d, a, b):
        b = b * open_b[d]
        return jnp.where(even[d], b, a), jnp.where(even[d], a, b)

    lanes = talk_ref.shape[1]
    repeat = lanes // slots
    targets = jnp.concatenate([slot_ref[...]] * repeat, axis=1)
    xi = [jnp.concatenate([xi_ref[j]] * repeat, axis=1) for j in range(3)]
    own = [talk_ref[i : i + 1, :] for i in range(24)]
    got = [parts_ref[i : i + 1, :] for i in range(24)]
    _, stress, drag = solid(own[0:3], own[3:12], got[12:21], got[21:24])
    moved, _, _ = solid(got[0:3], got[3:12], own[12:21], own[21:24])
    for i in range(9):
        deform_ref[i] = moved[i][:, :slots]
    (px, dx), (py, dy), (pz, dz) = shapes_of(xi, lanes)
    flat_yz, flat_dyz, flat_ydz = py * pz, dy * pz, py * dz
    basis = (px * flat_yz, dx * flat_yz, px * flat_dyz, px * flat_ydz)
    hot = one_hot(targets, blocks * cz)
    lane_half = iota((nodes, lanes), 1) < slots

    table = node_tables()
    table = jnp.concatenate([table, table], axis=1)
    row = iota((nodes, cz), 0)
    a, b, c = (row >> 4) & 3, (row >> 2) & 3, row & 3
    def ends(p):
        return jnp.where((p == 0) | (p == 3), PENALTY, 0.0)
    keep = 1.0 + ends(a) + ends(b) + ends(c)
    lane = iota((nodes, cz), 1)
    z_low, z_up = sides(2, za_ref[24 : 24 + comps * face, 0:128], zb_ref[...])
    z_ref[pl.ds(0, comps * face, stride=4), :] = z_low
    z_ref[pl.ds(3, comps * face, stride=4), :] = z_up

    for k in range(comps):
        force = drag[k] * basis[0]
        for j in range(3):
            force = force - stress[3 * k + j] * basis[1 + j]
        high, low = split(force)
        if repeat == 2:
            pieces = jnp.where(lane_half, high.astype(F32), low.astype(F32)).astype(BF16)
            spread = dot(pieces, hot, ((1,), (1,)))
        else:
            spread = dot(high, hot, ((1,), (1,))) + dot(low, hot, ((1,), (1,)))
        pair = con_ref[2 * k * nodes : 2 * (k + 1) * nodes, :]
        ops = dot(table, pair)
        y_low, y_up = sides(1, ya_ref[k * face : (k + 1) * face, :], yb_ref[k * face : (k + 1) * face, :])
        x_low, x_up = sides(0, xa_ref[k * face : (k + 1) * face, :], xb_ref[k * face : (k + 1) * face, :])
        z_face = z_ref[k * nodes : (k + 1) * nodes, :]
        for y in range(blocks):
            x_at, y_at = y // cy, y % cy
            cells = slice(y * cz, (y + 1) * cz)
            value = pair[:nodes, cells].astype(F32) + pair[nodes:, cells].astype(F32)
            total = keep * value + viscosity_ref[y : y + 1, :] * ops[0:nodes, cells] - spread[:, cells]
            moved_z = ops[nodes : 2 * nodes, cells]
            below = jnp.where(lane == 0, pltpu.roll(z_face, (cz - y) % cz, axis=1), pltpu.roll(moved_z, 1, axis=1))
            above = jnp.where(lane == cz - 1, pltpu.roll(z_face, (cz - 1 - y) % cz, axis=1), pltpu.roll(moved_z, cz - 1, axis=1))
            near = jnp.where(c == 0, below, jnp.where(c == 3, above, 0.0))
            if y_at > 0:
                below = ops[2 * nodes : 3 * nodes, (y - 1) * cz : y * cz]
            else:
                low_face = y_low[:, x_at * cz : (x_at + 1) * cz]
                below = jnp.concatenate([low_face[4 * (i // 4) : 4 * (i // 4) + 4] for i in range(16)], axis=0)
            if y_at < cy - 1:
                above = ops[2 * nodes : 3 * nodes, (y + 1) * cz : (y + 2) * cz]
            else:
                up_face = y_up[:, x_at * cz : (x_at + 1) * cz]
                above = jnp.concatenate([up_face[4 * (i // 4) : 4 * (i // 4) + 4] for i in range(16)], axis=0)
            near = near + jnp.where(b == 0, below, jnp.where(b == 3, above, 0.0))
            total = total - PENALTY * near
            plane = slice(y_at * cz, (y_at + 1) * cz)
            if x_at > 0:
                other = slice((y - cy) * cz, (y - cy + 1) * cz)
                below = pair[nodes - face : nodes, other].astype(F32) + pair[2 * nodes - face :, other].astype(F32)
            else:
                below = x_low[:, plane]
            if x_at < cx - 1:
                other = slice((y + cy) * cz, (y + cy + 1) * cz)
                above = pair[:face, other].astype(F32) + pair[nodes : nodes + face, other].astype(F32)
            else:
                above = x_up[:, plane]
            total = jnp.concatenate(
                [total[:face] - PENALTY * below, total[face : nodes - face], total[nodes - face :] - PENALTY * above],
                axis=0,
            )
            total_ref[k * nodes : (k + 1) * nodes, cells] = total
            put_split(rhs_ref, (k * blocks + y) * cz, cz, nodes, total)

    turned = jnp.concatenate([offset_ref[w * nodes : (w + 1) * nodes, :].T for w in range(nconf)], axis=0)
    high, low = split(turned)
    matrix = jnp.concatenate([high, high, low], axis=1)
    config_rows = [config_ref[y : y + 1, :] for y in range(blocks)]

    def add(k, y):
        return total_ref[k * nodes : (k + 1) * nodes, y * cz : (y + 1) * cz]

    def store(k, y, value):
        out_ref[pl.ds(k * nodes * blocks + y, nodes, stride=blocks), :] = value

    constrain(matrix, rhs_ref, config_rows, add, store, nconf, nodes, comps, blocks, cz)


def swap(x, axis, stage):
    n = lax.axis_size(axis)
    pairs = [(i, i + 1) for i in range(stage, n - 1, 2)]
    if not pairs:
        return jnp.zeros_like(x)
    return lax.ppermute(x, axis, pairs + [(j, i) for i, j in pairs])


def shards(
    mesh_sizes,
    velocity,
    viscosity,
    cell_config,
    constraint_offsets,
    slot_cells,
    point_coords,
    strain_offsets,
    solid_velocity,
):
    axes = ("dx", "dy", "solid")
    comps, cx, cy, cz = velocity.shape[0], *velocity.shape[4:]
    nodes = velocity.shape[1] * velocity.shape[2] * velocity.shape[3]
    blocks = cx * cy
    nconf = constraint_offsets.shape[0]
    slots = slot_cells.shape[-1]
    n_dx, n_dy, n_solid = mesh_sizes
    has_zb = n_solid > 2
    dims = (comps, nodes, cx, cy, cz, nconf, slots, has_zb)
    face_rows = comps * nodes // 4
    lanes = max(slots, 128)

    v = velocity.reshape(comps * nodes * blocks, cz)
    visc = viscosity.reshape(blocks, cz)
    config = cell_config.reshape(blocks, cz)
    offsets = constraint_offsets.reshape(nconf * nodes, nodes)
    targets = slot_cells.reshape(1, slots)
    xi = point_coords.reshape(3, 1, slots)
    strain = strain_offsets.reshape(9, 1, slots)
    motion = solid_velocity.reshape(3, 1, slots)

    vmem = pl.BlockSpec(memory_space=pltpu.VMEM)
    params = pltpu.CompilerParams(vmem_limit_bytes=VMEM_LIMIT)
    face_z = jax.ShapeDtypeStruct((face_rows, 128), F32)
    face_y = jax.ShapeDtypeStruct((face_rows, cx * cz), F32)
    face_x = jax.ShapeDtypeStruct((face_rows, cy * cz), F32)
    con, talk, xa, xb, ya, yb, zb = pl.pallas_call(
        functools.partial(before, dims, axes),
        out_shape=(
            jax.ShapeDtypeStruct((2 * comps * nodes, blocks * cz), BF16),
            jax.ShapeDtypeStruct((24 + face_rows, lanes), F32),
            face_x, face_x, face_y, face_y, face_z,
        ),
        in_specs=[vmem] * 7,
        out_specs=(vmem,) * 7,
        scratch_shapes=[
            pltpu.VMEM((3 * nodes, comps * blocks * cz), BF16),
            pltpu.VMEM((blocks * comps * nodes, cz), F32),
        ],
        compiler_params=params,
        name="before",
    )(v, config, offsets, targets, xi, strain, motion)

    if (n_dy, n_solid, slots) == (4, 2, 64):
        got_s = swap(talk, "solid", 0)
        got_xa = swap(xa, "dx", 0)
        pair = jnp.where(iota((24, 128), 1) < 64, talk[:24], got_s[:24])
        send_a = jnp.concatenate([ya, pair], axis=0)
        got_a = swap(send_a, "dy", 0)
        got_xb = swap(xb, "dx", 1)
        send_b = jnp.concatenate([yb, pair, got_a[face_rows:]], axis=0)
        got_b = lax.ppermute(send_b, "dy", [(i, 3 - i) for i in range(4)])
        four = [pair, got_a[face_rows:], got_b[face_rows : face_rows + 24], got_b[face_rows + 24 :]]
        me_y, me_s = lax.axis_index("dy"), lax.axis_index("solid")
        me = me_y * 2 + me_s
        parts = jnp.zeros((24, 8, 8), F32)
        for flip, block in zip((0, 1, 3, 2), four, strict=True):
            for half in range(2):
                source = (me_y ^ flip) * 2 + (me_s ^ half)
                piece = lax.dynamic_slice(block, (0, half * 64 + me * 8), (24, 8))
                parts = lax.dynamic_update_slice(parts, piece[:, None, :], (0, source, 0))
        parts = parts.reshape(24, 64)
        parts = jnp.concatenate([parts, parts], axis=1)
        got_ya, got_yb = got_a[:face_rows], got_b[:face_rows]
        got_za, got_zb = got_s, zb
    else:
        got_xa, got_xb = swap(xa, "dx", 0), swap(xb, "dx", 1)
        got_ya, got_yb = swap(ya, "dy", 0), swap(yb, "dy", 1)
        got_za, got_zb = swap(talk, "solid", 0), swap(zb, "solid", 1)
        parts = lax.all_to_all(talk[:24, :slots], ("dy", "solid"), split_axis=1, concat_axis=1, tiled=True)
        parts = jnp.concatenate([parts] * (lanes // slots), axis=1)

    out, deform = pl.pallas_call(
        functools.partial(after, dims, axes, mesh_sizes),
        out_shape=(
            jax.ShapeDtypeStruct(v.shape, F32),
            jax.ShapeDtypeStruct((9, 1, slots), F32),
        ),
        in_specs=[vmem] * 16,
        out_specs=(vmem,) * 2,
        scratch_shapes=[
            pltpu.VMEM((3 * nodes, comps * blocks * cz), BF16),
            pltpu.VMEM((comps * nodes, blocks * cz), F32),
            pltpu.VMEM((comps * nodes, 128), F32),
        ],
        compiler_params=params,
        name="after",
    )(con, visc, config, offsets, targets, xi, strain, motion,
      talk, parts, got_xa, got_xb, got_ya, got_yb, got_za, got_zb)
    return out.reshape(velocity.shape), deform.reshape(strain_offsets.shape)


def solution(mesh):
    sizes = tuple(mesh.shape[a] for a in ("dx", "dy", "solid"))
    return jax.shard_map(
        functools.partial(shards, sizes),
        mesh=mesh,
        in_specs=(
            P(None, None, None, None, "dx", "dy", "solid"),
            P("dx", "dy", "solid"),
            P("dx", "dy", "solid"),
            P(),
            P("dx", ("dy", "solid"), None),
            P(None, "dx", ("dy", "solid"), None),
            P(None, None, "dx", ("dy", "solid"), None),
            P(None, "dx", ("dy", "solid"), None),
        ),
        out_specs=(
            P(None, None, None, None, "dx", "dy", "solid"),
            P(None, None, "dx", ("dy", "solid"), None),
        ),
        check_vma=False,
    )
```

```python
import functools

import jax
import jax.numpy as jnp
from jax import lax
from jax.experimental import pallas as pl
from jax.experimental.pallas import tpu as pltpu
from jax.sharding import PartitionSpec as P

TIME_STEP = 0.05
SPRING_RATE = 2.0
PENALTY = 4.0
NODE_POINTS = (0.0, 1.0 / 3.0, 2.0 / 3.0, 1.0)
F32, BF16 = jnp.float32, jnp.bfloat16
VMEM_LIMIT = 24 * 1024 * 1024


def iota(shape, dim):
    return lax.broadcasted_iota(jnp.int32, shape, dim)


def split(x):
    high = x.astype(BF16)
    low = (x - high.astype(F32)).astype(BF16)
    return high, low


def dot(a, b, dims=((1,), (0,))):
    return lax.dot_general(a, b, (dims, ((), ())), preferred_element_type=F32)


def lagrange(coord):
    values = []
    slopes = []
    for which in range(4):
        others = [NODE_POINTS[j] for j in range(4) if j != which]
        denom = 1.0
        for other in others:
            denom = denom * (NODE_POINTS[which] - other)
        scale = 1.0 / denom
        first = coord - others[0]
        second = coord - others[1]
        third = coord - others[2]
        values.append(first * second * third * scale)
        slopes.append((second * third + first * third + first * second) * scale)
    return values, slopes


def spread_rows(parts, dim, lanes):
    wide = [jnp.broadcast_to(p, (8, lanes)) for p in parts]
    if dim == 0:
        return jnp.concatenate([wide[a] for a in (0, 0, 1, 1, 2, 2, 3, 3)], axis=0)
    row = iota((8, lanes), 0)
    if dim == 1:
        even = jnp.where(row < 4, wide[0], wide[1])
        odd = jnp.where(row < 4, wide[2], wide[3])
        return jnp.concatenate([even, odd] * 4, axis=0)
    c = row & 3
    block = jnp.where(c == 0, wide[0], jnp.where(c == 1, wide[1], jnp.where(c == 2, wide[2], wide[3])))
    return jnp.concatenate([block] * 8, axis=0)


def shapes_of(xi, lanes):
    out = []
    for dim in range(3):
        values, slopes = lagrange(xi[dim])
        out.append((spread_rows(values, dim, lanes), spread_rows(slopes, dim, lanes)))
    return out


def one_hot(slots, cells):
    lanes = slots.shape[1]
    return jnp.where(iota((cells, lanes), 0) == slots, 1.0, 0.0).astype(BF16)


def configured(product, config, nconf):
    rows = product.shape[0] // nconf
    chosen = product[:rows]
    for which in range(1, nconf):
        chosen = jnp.where(config == which, product[which * rows : (which + 1) * rows], chosen)
    return chosen


def constrain(matrix, split_ref, config_rows, add, store, nconf, nodes, comps, blocks, lanes):
    step = 2 if blocks % 2 == 0 else 1
    for k in range(comps):
        for first in range(0, blocks, step):
            col = (k * blocks + first) * lanes
            product = dot(matrix, split_ref[:, col : col + step * lanes])
            for i in range(step):
                piece = product[:, i * lanes : (i + 1) * lanes]
                y = first + i
                store(k, y, add(k, y) + configured(piece, config_rows[y], nconf))


def put_split(ref, col, lanes, nodes, value):
    high, low = split(value)
    ref[0:nodes, col : col + lanes] = high
    ref[nodes : 2 * nodes, col : col + lanes] = low
    ref[2 * nodes : 3 * nodes, col : col + lanes] = high


def fetch(pairs, sems):
    copies = [pltpu.make_async_copy(src, dst, sems.at[i]) for i, (src, dst) in enumerate(pairs)]
    for copy in copies:
        copy.start()
    return copies


def begin(
    dims,
    v_hbm, config_hbm, offset_hbm, slot_hbm, xi_hbm, strain_hbm, motion_hbm, viscosity_hbm,
    talk_ref, rhs_ref, matrix_ref, hot_ref, basis_ref, config_ref, offset_ref, viscosity_ref,
    v_ref, slot_ref, xi_ref, strain_ref, motion_ref, column_ref, end_ref, sems,
):
    comps, nodes, cx, cy, cz, nconf, slots, lanes = dims
    blocks = cx * cy
    cells = blocks * cz
    face = nodes // 4
    copies = fetch(
        [(slot_hbm, slot_ref), (xi_hbm, xi_ref), (strain_hbm, strain_ref), (motion_hbm, motion_ref),
         (config_hbm, config_ref), (offset_hbm, offset_ref), (v_hbm, v_ref), (viscosity_hbm, viscosity_ref)],
        sems,
    )
    for copy in copies:
        copy.wait()

    lane = iota((1, lanes), 1)
    targets = jnp.concatenate([slot_ref[...], jnp.full((1, lanes - slots), -1, jnp.int32)], axis=1)
    for y in range(blocks):
        targets = jnp.where(lane == lanes - 2 * blocks + y, y * cz, targets)
        targets = jnp.where(lane == lanes - blocks + y, (y + 1) * cz - 1, targets)
    hot = one_hot(targets, cells)
    hot_ref[...] = hot
    high, low = split(offset_ref[...])
    matrix = jnp.concatenate([high, high, low], axis=1)
    matrix_ref[...] = matrix
    for k in range(comps):
        for y in range(blocks):
            value = v_ref[pl.ds(k * nodes * blocks + y, nodes, stride=blocks), :]
            put_split(rhs_ref, (k * blocks + y) * cz, cz, nodes, value)
    config = jnp.concatenate([config_ref[y : y + 1, :] for y in range(blocks)], axis=1)
    config = dot(jnp.broadcast_to(config.astype(F32), (16, cells)).astype(BF16), hot)[0:1, :]

    raw = []
    for k in range(comps):
        both = dot(rhs_ref[0 : 2 * nodes, k * cells : (k + 1) * cells], hot)
        raw.append(both[:nodes] + both[nodes:])
        put_split(column_ref, k * lanes, lanes, nodes, raw[k])
    product = dot(matrix, column_ref[...])

    xi = [jnp.concatenate([xi_ref[j], jnp.zeros((1, lanes - slots), F32)], axis=1) for j in range(3)]
    (px, dx), (py, dy), (pz, dz) = shapes_of(xi, lanes)
    whole = py * pz
    along = (px * whole, dx * whole, px * dy * pz, px * py * dz)
    for j in range(4):
        basis_ref[j * nodes : (j + 1) * nodes, :] = along[j]
    for k in range(comps):
        piece = product[:, k * lanes : (k + 1) * lanes]
        local = raw[k] + configured(piece, config, nconf)
        talk_ref[k : k + 1, :] = jnp.sum(local * along[0], axis=0, keepdims=True)
        for j in range(3):
            at = 3 + 3 * k + j
            talk_ref[at : at + 1, :] = jnp.sum(local * along[1 + j], axis=0, keepdims=True)
        ends = local[:, lanes - 128 :]
        ends = jnp.where(iota((nodes, 128), 1) < 128 - blocks, ends, pltpu.roll(ends, nodes - 3, axis=0))
        end_ref[k * nodes : (k + 1) * nodes, :] = ends
    talk_ref[24 : 24 + comps * face, lanes - 128 :] = end_ref[pl.ds(0, comps * face, stride=4), :]
    for i in range(9):
        talk_ref[12 + i : 13 + i, 0:slots] = strain_ref[i]
    for i in range(3):
        talk_ref[21 + i : 22 + i, 0:slots] = motion_ref[i]
    if 2 * slots == lanes:
        twice = talk_ref[0:24, :]
        talk_ref[0:24, :] = jnp.where(iota((24, lanes), 1) < slots, twice, pltpu.roll(twice, slots, axis=1))


def local(
    dims, axes,
    rhs_ref, matrix_ref, config_ref,
    con_ref, xa_ref, xb_ref, ya_ref, yb_ref,
    field_ref,
):
    comps, nodes, cx, cy, cz, nconf, slots, lanes = dims
    blocks = cx * cy
    me_x, me_y = lax.axis_index(axes[0]), lax.axis_index(axes[1])
    even_x, even_y = me_x % 2 == 0, me_y % 2 == 0
    config_rows = [config_ref[y : y + 1, :] for y in range(blocks)]

    def load(k, y):
        cells = slice((k * blocks + y) * cz, (k * blocks + y + 1) * cz)
        return rhs_ref[0:nodes, cells].astype(F32) + rhs_ref[nodes : 2 * nodes, cells].astype(F32)

    def store(k, y, value):
        field_ref[(y * comps + k) * nodes : (y * comps + k + 1) * nodes, :] = value
        part, rest = split(value)
        row = 2 * k * nodes
        con_ref[row : row + nodes, y * cz : (y + 1) * cz] = part
        con_ref[row + nodes : row + 2 * nodes, y * cz : (y + 1) * cz] = rest

    constrain(matrix_ref[...], rhs_ref, config_rows, load, store, nconf, nodes, comps, blocks, cz)

    face = nodes // 4
    for k in range(comps):
        for y in range(cy):
            low_row = (y * comps + k) * nodes
            up_row = (((cx - 1) * cy + y) * comps + k + 1) * nodes
            lower = field_ref[low_row : low_row + face, :]
            upper = field_ref[up_row - face : up_row, :]
            cells = slice(y * cz, (y + 1) * cz)
            xa_ref[k * face : (k + 1) * face, cells] = jnp.where(even_x, upper, lower)
            xb_ref[k * face : (k + 1) * face, cells] = jnp.where(even_x, lower, upper)
        for a in range(4):
            into = k * face + a * 4
            for x in range(cx):
                first = (x * cy * comps + k) * nodes + a * face
                last = ((x * cy + cy - 1) * comps + k) * nodes + a * face
                lower = field_ref[first : first + 4, :]
                upper = field_ref[last + 12 : last + 16, :]
                ya_ref[into : into + 4, x * cz : (x + 1) * cz] = jnp.where(even_y, upper, lower)
                yb_ref[into : into + 4, x * cz : (x + 1) * cz] = jnp.where(even_y, lower, upper)


def solid(vel, grad, strain, motion):
    deform = [strain[3 * j + l] + (1.0 if j == l else 0.0) for j in range(3) for l in range(3)]
    moved = []
    for k in range(3):
        for l in range(3):
            change = sum(grad[3 * k + j] * deform[3 * j + l] for j in range(3))
            moved.append(deform[3 * k + l] + TIME_STEP * change)
    stress = [
        sum(moved[3 * k + l] * moved[3 * m + l] for l in range(3)) - (1.0 if k == m else 0.0)
        for k in range(3) for m in range(3)
    ]
    drag = [SPRING_RATE * (motion[k] - vel[k]) for k in range(3)]
    return moved, stress, drag


def node_tables():
    i, j = iota((64, 64), 0), iota((64, 64), 1)
    digits = [((i >> s) & 3, (j >> s) & 3) for s in (4, 2, 0)]
    same = [p == q for p, q in digits]
    lap = jnp.zeros((64, 64), F32)
    swaps = []
    for d in range(3):
        others = same[(d + 1) % 3] & same[(d + 2) % 3]
        p, q = digits[d]
        line = jnp.where(p == q, 2.0, jnp.where((p - q == 1) | (q - p == 1), -1.0, 0.0))
        lap = lap + jnp.where(others, line, 0.0)
        swaps.append(jnp.where(others & (((p == 0) & (q == 3)) | ((p == 3) & (q == 0))), 1.0, 0.0))
    return jnp.concatenate([lap, swaps[2], swaps[1]], axis=0).astype(BF16)


def sides(even, open_b, a, b):
    b = jnp.where(open_b, b, 0.0)
    return jnp.where(even, b, a), jnp.where(even, a, b)


def place(axis, n):
    index = lax.axis_index(axis)
    even = index % 2 == 0
    return even, jnp.where(even, index, n - 1 - index) > 0


def middle(
    dims, axes, sizes,
    con_ref, viscosity_ref, offset_ref, xa_ref, xb_ref, za_ref, zb_ref,
    total_ref, matrix_ref,
    z_ref,
):
    comps, nodes, cx, cy, cz, nconf, slots, lanes = dims
    blocks = cx * cy
    face = nodes // 4
    even_x, open_x = place(axes[0], sizes[0])
    even_z, open_z = place(axes[2], sizes[2])

    table = node_tables()
    table = jnp.concatenate([table, table], axis=1)
    row = iota((nodes, cz), 0)
    a, b, c = (row >> 4) & 3, (row >> 2) & 3, row & 3

    def ends(p):
        return jnp.where((p == 0) | (p == 3), PENALTY, 0.0)

    keep = 1.0 + ends(a) + ends(b) + ends(c)
    lane = iota((nodes, cz), 1)
    ends_at = slice(za_ref.shape[1] - 128, za_ref.shape[1])
    z_low, z_up = sides(even_z, open_z, za_ref[24 : 24 + comps * face, ends_at], zb_ref[24 : 24 + comps * face, ends_at])
    z_ref[pl.ds(0, comps * face, stride=4), :] = z_low
    z_ref[pl.ds(3, comps * face, stride=4), :] = z_up

    for k in range(comps):
        pair = con_ref[2 * k * nodes : 2 * (k + 1) * nodes, :]
        ops = dot(table, pair)
        rows = slice(k * face, (k + 1) * face)
        x_low, x_up = sides(even_x, open_x, xa_ref[rows, :], xb_ref[rows, :])
        z_face = z_ref[k * nodes : (k + 1) * nodes, :]
        for y in range(blocks):
            x_at, y_at = y // cy, y % cy
            cells = slice(y * cz, (y + 1) * cz)
            value = pair[:nodes, cells].astype(F32) + pair[nodes:, cells].astype(F32)
            total = keep * value + viscosity_ref[y : y + 1, :] * ops[0:nodes, cells]
            moved_z = ops[nodes : 2 * nodes, cells]
            below = jnp.where(lane == 0, pltpu.roll(z_face, (blocks - y) % cz, axis=1), pltpu.roll(moved_z, 1, axis=1))
            above = jnp.where(
                lane == cz - 1, pltpu.roll(z_face, (2 * blocks - 1 - y) % cz, axis=1), pltpu.roll(moved_z, cz - 1, axis=1)
            )
            near = jnp.where(c == 0, below, jnp.where(c == 3, above, 0.0))
            if y_at > 0:
                near = near + jnp.where(b == 0, ops[2 * nodes : 3 * nodes, (y - 1) * cz : y * cz], 0.0)
            if y_at < cy - 1:
                near = near + jnp.where(b == 3, ops[2 * nodes : 3 * nodes, (y + 1) * cz : (y + 2) * cz], 0.0)
            total = total - PENALTY * near
            plane = slice(y_at * cz, (y_at + 1) * cz)
            if x_at > 0:
                other = slice((y - cy) * cz, (y - cy + 1) * cz)
                below = pair[nodes - face : nodes, other].astype(F32) + pair[2 * nodes - face :, other].astype(F32)
            else:
                below = x_low[:, plane]
            if x_at < cx - 1:
                other = slice((y + cy) * cz, (y + cy + 1) * cz)
                above = pair[:face, other].astype(F32) + pair[nodes : nodes + face, other].astype(F32)
            else:
                above = x_up[:, plane]
            total_ref[k * nodes : (k + 1) * nodes, cells] = jnp.concatenate(
                [total[:face] - PENALTY * below, total[face : nodes - face], total[nodes - face :] - PENALTY * above],
                axis=0,
            )

    turned = jnp.concatenate([offset_ref[w * nodes : (w + 1) * nodes, :].T for w in range(nconf)], axis=0)
    high, low = split(turned)
    matrix_ref[...] = jnp.concatenate([high, high, low], axis=1)


def widen(face, nodes):
    return jnp.concatenate([face[4 * (i // 4) : 4 * (i // 4) + 4] for i in range(nodes // 4)], axis=0)


def gather_parts(refs, axes):
    me_y, me_s = lax.axis_index(axes[1]), lax.axis_index(axes[2])
    me = me_y * 2 + me_s
    lane = iota((24, 128), 1) >> 3
    parts = jnp.zeros((24, 128), F32)
    for flip, ref in enumerate(refs):
        block = ref[0:24, :]
        for half in range(2):
            source = (me_y ^ flip) * 2 + (me_s ^ half)
            shift = (source - me) * 8 + (128 - 64 * half)
            parts = jnp.where(lane == source, pltpu.roll(block, shift & 127, axis=1), parts)
    return parts + pltpu.roll(parts, 64, axis=1)


def after(
    dims, axes, sizes, fast,
    total_ref, matrix_ref, config_ref, hot_ref, basis_ref, talk_ref, ya_ref, yb_ref, *refs,
):
    if fast:
        refs = (refs[0], ya_ref, refs[1], yb_ref, *refs[2:])
        ya_ref, yb_ref = ya_ref.at[24:, :], yb_ref.at[24:, :]
    *part_refs, out_hbm, deform_ref, rhs_ref, total2_ref, out_ref, sems = refs
    comps, nodes, cx, cy, cz, nconf, slots, lanes = dims
    blocks = cx * cy
    face = nodes // 4
    even_y, open_y = place(axes[1], sizes[1])

    parts = gather_parts(part_refs, axes) if fast else part_refs[0][...]
    own = [talk_ref[i : i + 1, :] for i in range(24)]
    got = [parts[i : i + 1, :] for i in range(24)]
    _, stress, drag = solid(own[0:3], own[3:12], got[12:21], got[21:24])
    moved, _, _ = solid(got[0:3], got[3:12], own[12:21], own[21:24])
    for i in range(9):
        deform_ref[i] = moved[i][:, :slots]
    hot = hot_ref[...]
    basis = [basis_ref[j * nodes : (j + 1) * nodes, :] for j in range(4)]
    row = iota((nodes, cz), 0)
    b = (row >> 2) & 3
    live = iota((nodes, lanes), 1) < slots
    highs, lows = [], []
    for k in range(comps):
        force = drag[k] * basis[0]
        for j in range(3):
            force = force - stress[3 * k + j] * basis[1 + j]
        high, low = split(jnp.where(live, force, 0.0))
        highs.append(high)
        lows.append(low)
    spreads = dot(jnp.concatenate(highs + lows, axis=0), hot, ((1,), (1,)))

    for k in range(comps):
        other = (comps + k) * nodes
        spread = spreads[k * nodes : (k + 1) * nodes] + spreads[other : other + nodes]
        rows = slice(k * face, (k + 1) * face)
        y_low, y_up = sides(even_y, open_y, ya_ref[rows, :], yb_ref[rows, :])
        for y in range(blocks):
            x_at, y_at = y // cy, y % cy
            cells = slice(y * cz, (y + 1) * cz)
            total = total_ref[k * nodes : (k + 1) * nodes, cells] - spread[:, cells]
            plane = slice(x_at * cz, (x_at + 1) * cz)
            if y_at == 0:
                total = total - jnp.where(b == 0, PENALTY * widen(y_low[:, plane], nodes), 0.0)
            if y_at == cy - 1:
                total = total - jnp.where(b == 3, PENALTY * widen(y_up[:, plane], nodes), 0.0)
            total2_ref[k * nodes : (k + 1) * nodes, cells] = total
            put_split(rhs_ref, (k * blocks + y) * cz, cz, nodes, total)

    config_rows = [config_ref[y : y + 1, :] for y in range(blocks)]

    def add(k, y):
        return total2_ref[k * nodes : (k + 1) * nodes, y * cz : (y + 1) * cz]

    copies = []

    def store(k, y, value):
        out_ref[pl.ds(k * nodes * blocks + y, nodes, stride=blocks), :] = value
        if y == blocks - 1:
            done = slice(k * nodes * blocks, (k + 1) * nodes * blocks)
            copies.append(pltpu.make_async_copy(out_ref.at[done, :], out_hbm.at[done, :], sems.at[k]))
            copies[-1].start()

    constrain(matrix_ref[...], rhs_ref, config_rows, add, store, nconf, nodes, comps, blocks, cz)
    for copy in copies:
        copy.wait()


def swap(x, axis, stage):
    n = lax.axis_size(axis)
    pairs = [(i, i + 1) for i in range(stage, n - 1, 2)]
    if not pairs:
        return jnp.zeros_like(x)
    return lax.ppermute(x, axis, pairs + [(j, i) for i, j in pairs])


def flip(x, axis, bits):
    return lax.ppermute(x, axis, [(i, i ^ bits) for i in range(lax.axis_size(axis))])


def shards(
    mesh_sizes,
    velocity,
    viscosity,
    cell_config,
    constraint_offsets,
    slot_cells,
    point_coords,
    strain_offsets,
    solid_velocity,
):
    axes = ("dx", "dy", "solid")
    comps, cx, cy, cz = velocity.shape[0], *velocity.shape[4:]
    nodes = velocity.shape[1] * velocity.shape[2] * velocity.shape[3]
    blocks = cx * cy
    nconf = constraint_offsets.shape[0]
    slots = slot_cells.shape[-1]
    n_dx, n_dy, n_solid = mesh_sizes
    face_rows = comps * nodes // 4
    lanes = pl.cdiv(slots + 2 * blocks, 128) * 128
    dims = (comps, nodes, cx, cy, cz, nconf, slots, lanes)

    v = velocity.reshape(comps * nodes * blocks, cz)
    visc = viscosity.reshape(blocks, cz)
    config = cell_config.reshape(blocks, cz)
    offsets = constraint_offsets.reshape(nconf * nodes, nodes)
    targets = slot_cells.reshape(1, slots)
    xi = point_coords.reshape(3, 1, slots)
    strain = strain_offsets.reshape(9, 1, slots)
    motion = solid_velocity.reshape(3, 1, slots)

    vmem = pl.BlockSpec(memory_space=pltpu.VMEM)
    hbm = pl.BlockSpec(memory_space=pltpu.HBM)
    params = pltpu.CompilerParams(vmem_limit_bytes=VMEM_LIMIT)
    cells = blocks * cz
    face_y = jax.ShapeDtypeStruct((face_rows, cx * cz), F32)
    face_x = jax.ShapeDtypeStruct((face_rows, cy * cz), F32)
    def shape(*size, dtype=F32):
        return jax.ShapeDtypeStruct(size, dtype)

    def estimate(columns):
        return pl.CostEstimate(flops=2 * 6 * nconf * nodes * nodes * columns, bytes_accessed=1_000_000, transcendentals=0)

    talk, rhs, matrix, hot, basis, config, offsets, visc = pl.pallas_call(
        functools.partial(begin, dims),
        out_shape=(
            shape(24 + face_rows, lanes),
            shape(3 * nodes, comps * cells, dtype=BF16),
            shape(nconf * nodes, 3 * nodes, dtype=BF16),
            shape(cells, lanes, dtype=BF16),
            shape(4 * nodes, lanes),
            shape(*config.shape, dtype=config.dtype),
            shape(*offsets.shape),
            shape(*visc.shape),
        ),
        in_specs=[hbm] * 8,
        out_specs=(vmem,) * 8,
        scratch_shapes=[
            pltpu.VMEM(v.shape, F32),
            pltpu.VMEM(targets.shape, targets.dtype),
            pltpu.VMEM(xi.shape, F32),
            pltpu.VMEM(strain.shape, F32),
            pltpu.VMEM(motion.shape, F32),
            pltpu.VMEM((3 * nodes, comps * lanes), BF16),
            pltpu.VMEM((comps * nodes, 128), F32),
            pltpu.SemaphoreType.DMA((8,)),
        ],
        compiler_params=params,
        name="begin",
    )(*(pltpu.with_memory_space_constraint(x, pltpu.HBM) for x in (v, config, offsets, targets, xi, strain, motion, visc)))

    con, xa, xb, ya, yb = pl.pallas_call(
        functools.partial(local, dims, axes),
        out_shape=(shape(2 * comps * nodes, cells, dtype=BF16), face_x, face_x, face_y, face_y),
        in_specs=[vmem] * 3,
        out_specs=(vmem,) * 5,
        scratch_shapes=[pltpu.VMEM((blocks * comps * nodes, cz), F32)],
        compiler_params=params,
        cost_estimate=estimate(comps * cells),
        name="local",
    )(rhs, matrix, config)

    fast = (n_dx, n_dy, n_solid, slots) == (4, 4, 2, 64)
    if fast:
        got_s = swap(talk, "solid", 0)
        got_xa = swap(xa, "dx", 0)
        got_xb = flip(xb, "dx", 3)
        pair = jnp.where(iota((24, 128), 1) < 64, talk[:24], got_s[:24])
        got_3 = flip(jnp.concatenate([pair, yb, pair[:8]], axis=0), "dy", 3)
        got_2 = flip(pair, "dy", 2)
        got_1 = flip(jnp.concatenate([pair, ya], axis=0), "dy", 1)
        parts = [pair, got_2]
        got_ya, got_yb = got_1, got_3
        got_za, got_zb = got_s, got_s
    else:
        got_xa, got_xb = swap(xa, "dx", 0), swap(xb, "dx", 1)
        got_ya, got_yb = swap(ya, "dy", 0), swap(yb, "dy", 1)
        got_za, got_zb = swap(talk, "solid", 0), swap(talk, "solid", 1)
        parts = lax.all_to_all(talk[:24, :slots], ("dy", "solid"), split_axis=1, concat_axis=1, tiled=True)
        parts = [jnp.pad(parts, ((0, 0), (0, lanes - slots)))]

    total, matrix = pl.pallas_call(
        functools.partial(middle, dims, axes, mesh_sizes),
        out_shape=(
            jax.ShapeDtypeStruct((comps * nodes, cells), F32),
            jax.ShapeDtypeStruct((nconf * nodes, 3 * nodes), BF16),
        ),
        in_specs=[vmem] * 7,
        out_specs=(vmem,) * 2,
        scratch_shapes=[pltpu.VMEM((comps * nodes, 128), F32)],
        compiler_params=params,
        cost_estimate=estimate(comps * cells),
        name="middle",
    )(con, visc, offsets, got_xa, got_xb, got_za, got_zb)

    out, deform = pl.pallas_call(
        functools.partial(after, dims, axes, mesh_sizes, fast),
        out_shape=(
            jax.ShapeDtypeStruct(v.shape, F32),
            jax.ShapeDtypeStruct((9, 1, slots), F32),
        ),
        in_specs=[vmem] * (8 + len(parts)),
        out_specs=(hbm, vmem),
        scratch_shapes=[
            pltpu.VMEM((3 * nodes, comps * cells), BF16),
            pltpu.VMEM((comps * nodes, cells), F32),
            pltpu.VMEM(v.shape, F32),
            pltpu.SemaphoreType.DMA((comps,)),
        ],
        compiler_params=params,
        name="after",
    )(total, matrix, config, hot, basis, talk, got_ya, got_yb, *parts)
    return out.reshape(velocity.shape), deform.reshape(strain_offsets.shape)


def solution(mesh):
    sizes = tuple(mesh.shape[a] for a in ("dx", "dy", "solid"))
    return jax.shard_map(
        functools.partial(shards, sizes),
        mesh=mesh,
        in_specs=(
            P(None, None, None, None, "dx", "dy", "solid"),
            P("dx", "dy", "solid"),
            P("dx", "dy", "solid"),
            P(),
            P("dx", ("dy", "solid"), None),
            P(None, "dx", ("dy", "solid"), None),
            P(None, None, "dx", ("dy", "solid"), None),
            P(None, "dx", ("dy", "solid"), None),
        ),
        out_specs=(
            P(None, None, None, None, "dx", "dy", "solid"),
            P(None, None, "dx", ("dy", "solid"), None),
        ),
        check_vma=False,
    )
```

```python
import functools

import jax
import jax.numpy as jnp
from jax import lax
from jax.experimental import pallas as pl
from jax.experimental.pallas import tpu as pltpu
from jax.sharding import PartitionSpec as P

TIME_STEP = 0.05
SPRING_RATE = 2.0
PENALTY = 4.0
NODE_POINTS = (0.0, 1.0 / 3.0, 2.0 / 3.0, 1.0)
F32, BF16 = jnp.float32, jnp.bfloat16
VMEM_LIMIT = 24 * 1024 * 1024


def iota(shape, dim):
    return lax.broadcasted_iota(jnp.int32, shape, dim)


def split(x):
    high = x.astype(BF16)
    low = (x - high.astype(F32)).astype(BF16)
    return high, low


def dot(a, b, dims=((1,), (0,))):
    return lax.dot_general(a, b, (dims, ((), ())), preferred_element_type=F32)


def lagrange(coord):
    values = []
    slopes = []
    for which in range(4):
        others = [NODE_POINTS[j] for j in range(4) if j != which]
        denom = 1.0
        for other in others:
            denom = denom * (NODE_POINTS[which] - other)
        scale = 1.0 / denom
        first = coord - others[0]
        second = coord - others[1]
        third = coord - others[2]
        values.append(first * second * third * scale)
        slopes.append((second * third + first * third + first * second) * scale)
    return values, slopes


def spread_rows(parts, dim, lanes):
    wide = [jnp.broadcast_to(p, (8, lanes)) for p in parts]
    if dim == 0:
        return jnp.concatenate([wide[a] for a in (0, 0, 1, 1, 2, 2, 3, 3)], axis=0)
    row = iota((8, lanes), 0)
    if dim == 1:
        even = jnp.where(row < 4, wide[0], wide[1])
        odd = jnp.where(row < 4, wide[2], wide[3])
        return jnp.concatenate([even, odd] * 4, axis=0)
    c = row & 3
    block = jnp.where(c == 0, wide[0], jnp.where(c == 1, wide[1], jnp.where(c == 2, wide[2], wide[3])))
    return jnp.concatenate([block] * 8, axis=0)


def shapes_of(xi, lanes):
    out = []
    for dim in range(3):
        values, slopes = lagrange(xi[dim])
        out.append((spread_rows(values, dim, lanes), spread_rows(slopes, dim, lanes)))
    return out


def one_hot(slots, cells):
    lanes = slots.shape[1]
    return jnp.where(iota((cells, lanes), 0) == slots, 1.0, 0.0).astype(BF16)


def configured(product, config, nconf):
    rows = product.shape[0] // nconf
    chosen = product[:rows]
    for which in range(1, nconf):
        chosen = jnp.where(config == which, product[which * rows : (which + 1) * rows], chosen)
    return chosen


def constrain(matrix, split_ref, config_rows, add, store, nconf, nodes, comps, blocks, lanes):
    step = 2 if blocks % 2 == 0 else 1
    for k in range(comps):
        for first in range(0, blocks, step):
            col = (k * blocks + first) * lanes
            product = dot(matrix, split_ref[:, col : col + step * lanes])
            for i in range(step):
                piece = product[:, i * lanes : (i + 1) * lanes]
                y = first + i
                store(k, y, add(k, y) + configured(piece, config_rows[y], nconf))


def put_split(ref, col, lanes, nodes, value):
    high, low = split(value)
    ref[0:nodes, col : col + lanes] = high
    ref[nodes : 2 * nodes, col : col + lanes] = low
    ref[2 * nodes : 3 * nodes, col : col + lanes] = high


def fetch(pairs, sems):
    copies = [pltpu.make_async_copy(src, dst, sems.at[i]) for i, (src, dst) in enumerate(pairs)]
    for copy in copies:
        copy.start()
    return copies


def begin(
    dims, axes, fast,
    v_hbm, config_hbm, offset_hbm, slot_hbm, xi_hbm, strain_hbm, motion_hbm, viscosity_hbm,
    talk_ref, own_ref, rhs_ref, matrix_ref, hot_ref, basis_ref, config_ref, offset_ref, viscosity_ref,
    v_ref, slot_ref, xi_ref, strain_ref, motion_ref, column_ref, end_ref, sems,
):
    comps, nodes, cx, cy, cz, nconf, slots, lanes = dims
    blocks = cx * cy
    cells = blocks * cz
    face = nodes // 4
    small = [(slot_hbm, slot_ref), (config_hbm, config_ref), (xi_hbm, xi_ref)]
    late = [(strain_hbm, strain_ref), (motion_hbm, motion_ref), (viscosity_hbm, viscosity_ref)]
    pairs = small + [(v_hbm, v_ref)] + [(offset_hbm, offset_ref)] + late
    copies = fetch(pairs, sems)

    def wait(count):
        for _ in range(count):
            copies.pop(0).wait()

    wait(3)
    lane = iota((1, lanes), 1)
    targets = jnp.concatenate([slot_ref[...], jnp.full((1, lanes - slots), -1, jnp.int32)], axis=1)
    for y in range(blocks):
        targets = jnp.where(lane == lanes - 2 * blocks + y, y * cz, targets)
        targets = jnp.where(lane == lanes - blocks + y, (y + 1) * cz - 1, targets)
    hot = one_hot(targets, cells)
    hot_ref[...] = hot
    wait(len(copies))
    config = jnp.concatenate([config_ref[y : y + 1, :] for y in range(blocks)], axis=1)
    config = dot(jnp.broadcast_to(config.astype(F32), (16, cells)).astype(BF16), hot)[0:1, :]
    high, low = split(offset_ref[...])
    matrix = jnp.concatenate([high, high, low], axis=1)
    matrix_ref[...] = matrix
    raw = []
    for k in range(comps):
        for y in range(blocks):
            value = v_ref[pl.ds(k * nodes * blocks + y, nodes, stride=blocks), :]
            put_split(rhs_ref, (k * blocks + y) * cz, cz, nodes, value)
        both = dot(rhs_ref[0 : 2 * nodes, k * cells : (k + 1) * cells], hot)
        raw.append(both[:nodes] + both[nodes:])
        put_split(column_ref, k * lanes, lanes, nodes, raw[k])
    product = dot(matrix, column_ref[...])

    xi = [jnp.concatenate([xi_ref[j], jnp.zeros((1, lanes - slots), F32)], axis=1) for j in range(3)]
    (px, dx), (py, dy), (pz, dz) = shapes_of(xi, lanes)
    whole = py * pz
    along = (px * whole, dx * whole, px * dy * pz, px * py * dz)
    for j in range(4):
        basis_ref[j * nodes : (j + 1) * nodes, :] = along[j]
    for k in range(comps):
        piece = product[:, k * lanes : (k + 1) * lanes]
        local = raw[k] + configured(piece, config, nconf)
        own_ref[k : k + 1, :] = jnp.sum(local * along[0], axis=0, keepdims=True)
        for j in range(3):
            at = 3 + 3 * k + j
            own_ref[at : at + 1, :] = jnp.sum(local * along[1 + j], axis=0, keepdims=True)
        ends = local[:, lanes - 128 :]
        ends = jnp.where(iota((nodes, 128), 1) < 128 - blocks, ends, pltpu.roll(ends, nodes - 3, axis=0))
        end_ref[k * nodes : (k + 1) * nodes, :] = ends
    for i in range(9):
        own_ref[12 + i : 13 + i, 0:slots] = strain_ref[i]
    for i in range(3):
        own_ref[21 + i : 22 + i, 0:slots] = motion_ref[i]

    half = comps * face // 2
    ends = end_ref[pl.ds(0, 2 * half, stride=4), :]
    lane = iota((half, 128), 1)
    ends = jnp.where(lane < 128 - 2 * blocks, pltpu.roll(ends[:half], 128 - 2 * blocks, axis=1), ends[half:])
    last = jnp.where(lane < 128 - 4 * blocks, own_ref[:, lanes - 128 :], ends)
    if fast:
        last = pltpu.roll(last, lax.axis_index(axes[2]) * slots, axis=1)
    elif lanes > 128:
        talk_ref[:, : lanes - 128] = own_ref[:, : lanes - 128]
    talk_ref[:, lanes - 128 :] = last


def local(
    dims, axes,
    rhs_ref, matrix_ref, config_ref,
    con_ref, xa_ref, xb_ref, ya_ref, yb_ref,
    field_ref,
):
    comps, nodes, cx, cy, cz, nconf, slots, lanes = dims
    blocks = cx * cy
    me_x, me_y = lax.axis_index(axes[0]), lax.axis_index(axes[1])
    even_x, even_y = me_x % 2 == 0, me_y % 2 == 0
    config_rows = [config_ref[y : y + 1, :] for y in range(blocks)]

    def load(k, y):
        cells = slice((k * blocks + y) * cz, (k * blocks + y + 1) * cz)
        return rhs_ref[0:nodes, cells].astype(F32) + rhs_ref[nodes : 2 * nodes, cells].astype(F32)

    def store(k, y, value):
        field_ref[(y * comps + k) * nodes : (y * comps + k + 1) * nodes, :] = value
        part, rest = split(value)
        row = 2 * k * nodes
        con_ref[row : row + nodes, y * cz : (y + 1) * cz] = part
        con_ref[row + nodes : row + 2 * nodes, y * cz : (y + 1) * cz] = rest

    constrain(matrix_ref[...], rhs_ref, config_rows, load, store, nconf, nodes, comps, blocks, cz)

    face = nodes // 4
    for k in range(comps):
        for y in range(cy):
            low_row = (y * comps + k) * nodes
            up_row = (((cx - 1) * cy + y) * comps + k + 1) * nodes
            lower = field_ref[low_row : low_row + face, :]
            upper = field_ref[up_row - face : up_row, :]
            cells = slice(y * cz, (y + 1) * cz)
            xa_ref[k * face : (k + 1) * face, cells] = jnp.where(even_x, upper, lower)
            xb_ref[k * face : (k + 1) * face, cells] = jnp.where(even_x, lower, upper)
        for a in range(4):
            into = k * face + a * 4
            for x in range(cx):
                first = (x * cy * comps + k) * nodes + a * face
                last = ((x * cy + cy - 1) * comps + k) * nodes + a * face
                lower = field_ref[first : first + 4, :]
                upper = field_ref[last + 12 : last + 16, :]
                ya_ref[into : into + 4, x * cz : (x + 1) * cz] = jnp.where(even_y, upper, lower)
                yb_ref[into : into + 4, x * cz : (x + 1) * cz] = jnp.where(even_y, lower, upper)


def solid(vel, grad, strain, motion):
    deform = [strain[3 * j + l] + (1.0 if j == l else 0.0) for j in range(3) for l in range(3)]
    moved = []
    for k in range(3):
        for l in range(3):
            change = sum(grad[3 * k + j] * deform[3 * j + l] for j in range(3))
            moved.append(deform[3 * k + l] + TIME_STEP * change)
    stress = [
        sum(moved[3 * k + l] * moved[3 * m + l] for l in range(3)) - (1.0 if k == m else 0.0)
        for k in range(3) for m in range(3)
    ]
    drag = [SPRING_RATE * (motion[k] - vel[k]) for k in range(3)]
    return moved, stress, drag


def node_tables():
    i, j = iota((64, 64), 0), iota((64, 64), 1)
    digits = [((i >> s) & 3, (j >> s) & 3) for s in (4, 2, 0)]
    same = [p == q for p, q in digits]
    lap = jnp.zeros((64, 64), F32)
    swaps = []
    for d in range(3):
        others = same[(d + 1) % 3] & same[(d + 2) % 3]
        p, q = digits[d]
        line = jnp.where(p == q, 2.0, jnp.where((p - q == 1) | (q - p == 1), -1.0, 0.0))
        lap = lap + jnp.where(others, line, 0.0)
        swaps.append(jnp.where(others & (((p == 0) & (q == 3)) | ((p == 3) & (q == 0))), 1.0, 0.0))
    return jnp.concatenate([lap, swaps[2], swaps[1]], axis=0).astype(BF16)


def sides(even, open_b, a, b):
    b = jnp.where(open_b, b, 0.0)
    return jnp.where(even, b, a), jnp.where(even, a, b)


def place(axis, n):
    index = lax.axis_index(axis)
    even = index % 2 == 0
    return even, jnp.where(even, index, n - 1 - index) > 0


def middle(
    dims, axes, sizes, fast,
    con_ref, viscosity_ref, offset_ref, xa_ref, xb_ref, za_ref, zb_ref,
    total_ref, matrix_ref,
    z_ref,
):
    comps, nodes, cx, cy, cz, nconf, slots, lanes = dims
    blocks = cx * cy
    face = nodes // 4
    even_x, open_x = place(axes[0], sizes[0])
    even_z, open_z = place(axes[2], sizes[2])

    table = node_tables()
    table = jnp.concatenate([table, table], axis=1)
    row = iota((nodes, cz), 0)
    a, b, c = (row >> 4) & 3, (row >> 2) & 3, row & 3

    def ends(p):
        return jnp.where((p == 0) | (p == 3), PENALTY, 0.0)

    keep = 1.0 + ends(a) + ends(b) + ends(c)
    lane = iota((nodes, cz), 1)

    def ends_of(ref):
        last = ref[:, lanes - 128 :]
        if fast:
            last = pltpu.roll(last, (lax.axis_index(axes[2]) + 1) % 2 * slots, axis=1)
        return jnp.concatenate([pltpu.roll(last, 2 * blocks, axis=1), last], axis=0)

    z_a = ends_of(za_ref)
    z_low, z_up = sides(even_z, open_z, z_a, z_a if fast else ends_of(zb_ref))
    z_ref[pl.ds(0, comps * face, stride=4), :] = z_low
    z_ref[pl.ds(3, comps * face, stride=4), :] = z_up

    for k in range(comps):
        pair = con_ref[2 * k * nodes : 2 * (k + 1) * nodes, :]
        ops = dot(table, pair)
        rows = slice(k * face, (k + 1) * face)
        x_low, x_up = sides(even_x, open_x, xa_ref[rows, :], xb_ref[rows, :])
        z_face = z_ref[k * nodes : (k + 1) * nodes, :]
        for y in range(blocks):
            x_at, y_at = y // cy, y % cy
            cells = slice(y * cz, (y + 1) * cz)
            value = pair[:nodes, cells].astype(F32) + pair[nodes:, cells].astype(F32)
            total = keep * value + viscosity_ref[y : y + 1, :] * ops[0:nodes, cells]
            moved_z = ops[nodes : 2 * nodes, cells]
            below = jnp.where(lane == 0, pltpu.roll(z_face, (blocks - y) % cz, axis=1), pltpu.roll(moved_z, 1, axis=1))
            above = jnp.where(
                lane == cz - 1, pltpu.roll(z_face, (2 * blocks - 1 - y) % cz, axis=1), pltpu.roll(moved_z, cz - 1, axis=1)
            )
            near = jnp.where(c == 0, below, jnp.where(c == 3, above, 0.0))
            if y_at > 0:
                near = near + jnp.where(b == 0, ops[2 * nodes : 3 * nodes, (y - 1) * cz : y * cz], 0.0)
            if y_at < cy - 1:
                near = near + jnp.where(b == 3, ops[2 * nodes : 3 * nodes, (y + 1) * cz : (y + 2) * cz], 0.0)
            total = total - PENALTY * near
            plane = slice(y_at * cz, (y_at + 1) * cz)
            if x_at > 0:
                other = slice((y - cy) * cz, (y - cy + 1) * cz)
                below = pair[nodes - face : nodes, other].astype(F32) + pair[2 * nodes - face :, other].astype(F32)
            else:
                below = x_low[:, plane]
            if x_at < cx - 1:
                other = slice((y + cy) * cz, (y + cy + 1) * cz)
                above = pair[:face, other].astype(F32) + pair[nodes : nodes + face, other].astype(F32)
            else:
                above = x_up[:, plane]
            total_ref[k * nodes : (k + 1) * nodes, cells] = jnp.concatenate(
                [total[:face] - PENALTY * below, total[face : nodes - face], total[nodes - face :] - PENALTY * above],
                axis=0,
            )

    turned = jnp.concatenate([offset_ref[w * nodes : (w + 1) * nodes, :].T for w in range(nconf)], axis=0)
    high, low = split(turned)
    matrix_ref[...] = jnp.concatenate([high, high, low], axis=1)


def widen(face, nodes):
    return jnp.concatenate([face[4 * (i // 4) : 4 * (i // 4) + 4] for i in range(nodes // 4)], axis=0)


def gather_parts(refs, axes):
    me_y, me_s = lax.axis_index(axes[1]), lax.axis_index(axes[2])
    me = me_y * 2 + me_s
    lane = iota((24, 128), 1) >> 3
    parts = jnp.zeros((24, 128), F32)
    for flip, ref in enumerate(refs):
        block = ref[0:24, :]
        for half in range(2):
            source = (me_y ^ flip) * 2 + half
            shift = (source - me) * 8 + (128 - 64 * half)
            parts = jnp.where(lane == source, pltpu.roll(block, shift & 127, axis=1), parts)
    return parts + pltpu.roll(parts, 64, axis=1)


def after(
    dims, axes, sizes, fast,
    total_ref, matrix_ref, config_ref, hot_ref, basis_ref, own_ref, ya_ref, yb_ref, *refs,
):
    if fast:
        refs = (refs[0], ya_ref, refs[1], yb_ref, *refs[2:])
        ya_ref, yb_ref = ya_ref.at[24:, :], yb_ref.at[24:, :]
    *part_refs, out_hbm, deform_hbm, rhs_ref, total2_ref, out_ref, deform_ref, sems = refs
    comps, nodes, cx, cy, cz, nconf, slots, lanes = dims
    blocks = cx * cy
    face = nodes // 4
    even_y, open_y = place(axes[1], sizes[1])

    parts = gather_parts(part_refs, axes) if fast else part_refs[0][...]
    own = [own_ref[i : i + 1, :] for i in range(24)]
    got = [parts[i : i + 1, :] for i in range(24)]
    _, stress, drag = solid(own[0:3], own[3:12], got[12:21], got[21:24])
    moved, _, _ = solid(got[0:3], got[3:12], own[12:21], own[21:24])
    for i in range(9):
        deform_ref[i] = moved[i][:, :slots]
    copies = [pltpu.make_async_copy(deform_ref, deform_hbm, sems.at[4 * comps])]
    copies[0].start()
    hot = hot_ref[...]
    basis = [basis_ref[j * nodes : (j + 1) * nodes, :] for j in range(4)]
    row = iota((nodes, cz), 0)
    b = (row >> 2) & 3
    live = iota((nodes, lanes), 1) < slots
    highs, lows = [], []
    for k in range(comps):
        force = drag[k] * basis[0]
        for j in range(3):
            force = force - stress[3 * k + j] * basis[1 + j]
        high, low = split(jnp.where(live, force, 0.0))
        highs.append(high)
        lows.append(low)
    spreads = dot(jnp.concatenate(highs + lows, axis=0), hot, ((1,), (1,)))

    for k in range(comps):
        other = (comps + k) * nodes
        spread = spreads[k * nodes : (k + 1) * nodes] + spreads[other : other + nodes]
        rows = slice(k * face, (k + 1) * face)
        y_low, y_up = sides(even_y, open_y, ya_ref[rows, :], yb_ref[rows, :])
        for y in range(blocks):
            x_at, y_at = y // cy, y % cy
            cells = slice(y * cz, (y + 1) * cz)
            total = total_ref[k * nodes : (k + 1) * nodes, cells] - spread[:, cells]
            plane = slice(x_at * cz, (x_at + 1) * cz)
            if y_at == 0:
                total = total - jnp.where(b == 0, PENALTY * widen(y_low[:, plane], nodes), 0.0)
            if y_at == cy - 1:
                total = total - jnp.where(b == 3, PENALTY * widen(y_up[:, plane], nodes), 0.0)
            total2_ref[k * nodes : (k + 1) * nodes, cells] = total
            put_split(rhs_ref, (k * blocks + y) * cz, cz, nodes, total)

    config_rows = [config_ref[y : y + 1, :] for y in range(blocks)]

    def add(k, y):
        return total2_ref[k * nodes : (k + 1) * nodes, y * cz : (y + 1) * cz]

    def store(k, y, value):
        out_ref[pl.ds(k * nodes * blocks + y, nodes, stride=blocks), :] = value
        if y == blocks - 1:
            step = nodes * blocks // 4
            for i in range(4 * k, 4 * k + 4):
                done = slice(i * step, (i + 1) * step)
                copies.append(pltpu.make_async_copy(out_ref.at[done, :], out_hbm.at[done, :], sems.at[i]))
                copies[-1].start()

    constrain(matrix_ref[...], rhs_ref, config_rows, add, store, nconf, nodes, comps, blocks, cz)
    for copy in copies:
        copy.wait()


def swap(x, axis, stage):
    n = lax.axis_size(axis)
    pairs = [(i, i + 1) for i in range(stage, n - 1, 2)]
    if not pairs:
        return jnp.zeros_like(x)
    return lax.ppermute(x, axis, pairs + [(j, i) for i, j in pairs])


def flip(x, axis, bits):
    return lax.ppermute(x, axis, [(i, i ^ bits) for i in range(lax.axis_size(axis))])


def shards(
    mesh_sizes,
    velocity,
    viscosity,
    cell_config,
    constraint_offsets,
    slot_cells,
    point_coords,
    strain_offsets,
    solid_velocity,
):
    axes = ("dx", "dy", "solid")
    comps, cx, cy, cz = velocity.shape[0], *velocity.shape[4:]
    nodes = velocity.shape[1] * velocity.shape[2] * velocity.shape[3]
    blocks = cx * cy
    nconf = constraint_offsets.shape[0]
    slots = slot_cells.shape[-1]
    n_dx, n_dy, n_solid = mesh_sizes
    face_rows = comps * nodes // 4
    lanes = pl.cdiv(slots + 4 * blocks, 128) * 128
    dims = (comps, nodes, cx, cy, cz, nconf, slots, lanes)

    v = velocity.reshape(comps * nodes * blocks, cz)
    visc = viscosity.reshape(blocks, cz)
    config = cell_config.reshape(blocks, cz)
    offsets = constraint_offsets.reshape(nconf * nodes, nodes)
    targets = slot_cells.reshape(1, slots)
    xi = point_coords.reshape(3, 1, slots)
    strain = strain_offsets.reshape(9, 1, slots)
    motion = solid_velocity.reshape(3, 1, slots)

    vmem = pl.BlockSpec(memory_space=pltpu.VMEM)
    hbm = pl.BlockSpec(memory_space=pltpu.HBM)
    params = pltpu.CompilerParams(vmem_limit_bytes=VMEM_LIMIT)
    cells = blocks * cz
    face_y = jax.ShapeDtypeStruct((face_rows, cx * cz), F32)
    face_x = jax.ShapeDtypeStruct((face_rows, cy * cz), F32)
    def shape(*size, dtype=F32):
        return jax.ShapeDtypeStruct(size, dtype)

    def estimate(columns):
        return pl.CostEstimate(flops=2 * 6 * nconf * nodes * nodes * columns, bytes_accessed=1_000_000, transcendentals=0)

    fast = (n_dx, n_dy, n_solid, slots, lanes) == (4, 4, 2, 64, 128)
    talk, own, rhs, matrix, hot, basis, config, offsets, visc = pl.pallas_call(
        functools.partial(begin, dims, axes, fast),
        out_shape=(
            shape(24, lanes),
            shape(24, lanes),
            shape(3 * nodes, comps * cells, dtype=BF16),
            shape(nconf * nodes, 3 * nodes, dtype=BF16),
            shape(cells, lanes, dtype=BF16),
            shape(4 * nodes, lanes),
            shape(*config.shape, dtype=config.dtype),
            shape(*offsets.shape),
            shape(*visc.shape),
        ),
        in_specs=[hbm] * 8,
        out_specs=(vmem,) * 9,
        scratch_shapes=[
            pltpu.VMEM(v.shape, F32),
            pltpu.VMEM(targets.shape, targets.dtype),
            pltpu.VMEM(xi.shape, F32),
            pltpu.VMEM(strain.shape, F32),
            pltpu.VMEM(motion.shape, F32),
            pltpu.VMEM((3 * nodes, comps * lanes), BF16),
            pltpu.VMEM((comps * nodes, 128), F32),
            pltpu.SemaphoreType.DMA((8,)),
        ],
        compiler_params=params,
        name="begin",
    )(*(pltpu.with_memory_space_constraint(x, pltpu.HBM) for x in (v, config, offsets, targets, xi, strain, motion, visc)))

    con, xa, xb, ya, yb = pl.pallas_call(
        functools.partial(local, dims, axes),
        out_shape=(shape(2 * comps * nodes, cells, dtype=BF16), face_x, face_x, face_y, face_y),
        in_specs=[vmem] * 3,
        out_specs=(vmem,) * 5,
        scratch_shapes=[pltpu.VMEM((blocks * comps * nodes, cz), F32)],
        compiler_params=params,
        cost_estimate=estimate(comps * cells),
        name="local",
    )(rhs, matrix, config)

    if fast:
        got_s = swap(talk, "solid", 0)
        got_xa = swap(xa, "dx", 0)
        got_xb = flip(xb, "dx", 3)
        mine = (iota((24, 128), 1) >= 64) == (lax.axis_index("solid") == 1)
        pair = jnp.where(mine, talk, got_s)
        got_3 = flip(jnp.concatenate([pair, yb, pair[:8]], axis=0), "dy", 3)
        got_2 = flip(jnp.concatenate([pair, yb[:8]], axis=0), "dy", 2)
        got_1 = flip(jnp.concatenate([pair, ya], axis=0), "dy", 1)
        parts = [pair, got_2]
        got_ya, got_yb = got_1, got_3
        got_za, got_zb = got_s, got_s
    else:
        got_xa, got_xb = swap(xa, "dx", 0), swap(xb, "dx", 1)
        got_ya, got_yb = swap(ya, "dy", 0), swap(yb, "dy", 1)
        got_za, got_zb = swap(talk, "solid", 0), swap(talk, "solid", 1)
        parts = lax.all_to_all(talk[:, :slots], ("dy", "solid"), split_axis=1, concat_axis=1, tiled=True)
        parts = [jnp.pad(parts, ((0, 0), (0, lanes - slots)))]

    total, matrix = pl.pallas_call(
        functools.partial(middle, dims, axes, mesh_sizes, fast),
        out_shape=(
            jax.ShapeDtypeStruct((comps * nodes, cells), F32),
            jax.ShapeDtypeStruct((nconf * nodes, 3 * nodes), BF16),
        ),
        in_specs=[vmem] * 7,
        out_specs=(vmem,) * 2,
        scratch_shapes=[pltpu.VMEM((comps * nodes, 128), F32)],
        compiler_params=params,
        cost_estimate=estimate(comps * cells),
        name="middle",
    )(con, visc, offsets, got_xa, got_xb, got_za, got_zb)

    out, deform = pl.pallas_call(
        functools.partial(after, dims, axes, mesh_sizes, fast),
        out_shape=(
            jax.ShapeDtypeStruct(v.shape, F32),
            jax.ShapeDtypeStruct((9, 1, slots), F32),
        ),
        in_specs=[vmem] * (8 + len(parts)),
        out_specs=(hbm, hbm),
        scratch_shapes=[
            pltpu.VMEM((3 * nodes, comps * cells), BF16),
            pltpu.VMEM((comps * nodes, cells), F32),
            pltpu.VMEM(v.shape, F32),
            pltpu.VMEM(strain.shape, F32),
            pltpu.SemaphoreType.DMA((4 * comps + 1,)),
        ],
        compiler_params=params,
        name="after",
    )(total, matrix, config, hot, basis, own, got_ya, got_yb, *parts)
    return out.reshape(velocity.shape), deform.reshape(strain_offsets.shape)


def solution(mesh):
    sizes = tuple(mesh.shape[a] for a in ("dx", "dy", "solid"))
    return jax.shard_map(
        functools.partial(shards, sizes),
        mesh=mesh,
        in_specs=(
            P(None, None, None, None, "dx", "dy", "solid"),
            P("dx", "dy", "solid"),
            P("dx", "dy", "solid"),
            P(),
            P("dx", ("dy", "solid"), None),
            P(None, "dx", ("dy", "solid"), None),
            P(None, None, "dx", ("dy", "solid"), None),
            P(None, "dx", ("dy", "solid"), None),
        ),
        out_specs=(
            P(None, None, None, None, "dx", "dy", "solid"),
            P(None, None, "dx", ("dy", "solid"), None),
        ),
        check_vma=False,
    )
```

```python
import functools

import jax
import jax.numpy as jnp
from jax import lax
from jax.experimental import pallas as pl
from jax.experimental.pallas import tpu as pltpu
from jax.sharding import PartitionSpec as P

TIME_STEP = 0.05
SPRING_RATE = 2.0
PENALTY = 4.0
NODE_POINTS = (0.0, 1.0 / 3.0, 2.0 / 3.0, 1.0)
F32, BF16 = jnp.float32, jnp.bfloat16
VMEM_LIMIT = 24 * 1024 * 1024


def iota(shape, dim):
    return lax.broadcasted_iota(jnp.int32, shape, dim)


def split(x):
    high = x.astype(BF16)
    low = (x - high.astype(F32)).astype(BF16)
    return high, low


def dot(a, b, dims=((1,), (0,))):
    return lax.dot_general(a, b, (dims, ((), ())), preferred_element_type=F32)


def lagrange(coord):
    values = []
    slopes = []
    for which in range(4):
        others = [NODE_POINTS[j] for j in range(4) if j != which]
        denom = 1.0
        for other in others:
            denom = denom * (NODE_POINTS[which] - other)
        scale = 1.0 / denom
        first = coord - others[0]
        second = coord - others[1]
        third = coord - others[2]
        values.append(first * second * third * scale)
        slopes.append((second * third + first * third + first * second) * scale)
    return values, slopes


def spread_rows(parts, dim, lanes):
    wide = [jnp.broadcast_to(p, (8, lanes)) for p in parts]
    if dim == 0:
        return jnp.concatenate([wide[a] for a in (0, 0, 1, 1, 2, 2, 3, 3)], axis=0)
    row = iota((8, lanes), 0)
    if dim == 1:
        even = jnp.where(row < 4, wide[0], wide[1])
        odd = jnp.where(row < 4, wide[2], wide[3])
        return jnp.concatenate([even, odd] * 4, axis=0)
    c = row & 3
    block = jnp.where(c == 0, wide[0], jnp.where(c == 1, wide[1], jnp.where(c == 2, wide[2], wide[3])))
    return jnp.concatenate([block] * 8, axis=0)


def shapes_of(xi, lanes):
    out = []
    for dim in range(3):
        values, slopes = lagrange(xi[dim])
        out.append((spread_rows(values, dim, lanes), spread_rows(slopes, dim, lanes)))
    return out


def one_hot(slots, cells):
    lanes = slots.shape[1]
    return jnp.where(iota((cells, lanes), 0) == slots, 1.0, 0.0).astype(BF16)


def configured(product, config, nconf):
    rows = product.shape[0] // nconf
    chosen = product[:rows]
    for which in range(1, nconf):
        chosen = jnp.where(config == which, product[which * rows : (which + 1) * rows], chosen)
    return chosen


def tripled(high, low):
    return jnp.concatenate([high, low, high], axis=0)


def constrain(matrix, columns, config_rows, store, nconf, comps, blocks, lanes):
    step = 2 if blocks % 2 == 0 else 1
    for k in range(comps):
        for first in range(0, blocks, step):
            values, parts = columns(k, range(first, first + step))
            product = dot(matrix, parts)
            for i in range(step):
                piece = product[:, i * lanes : (i + 1) * lanes]
                store(k, first + i, values[i] + configured(piece, config_rows[first + i], nconf))


def fetch(pairs, sems):
    copies = [pltpu.make_async_copy(src, dst, sems.at[i]) for i, (src, dst) in enumerate(pairs)]
    for copy in copies:
        copy.start()
    return copies


def plain_matrix(offsets):
    high, low = split(offsets)
    return jnp.concatenate([high, high, low], axis=1)


def turned_matrix(offsets, nconf, nodes):
    turned = jnp.concatenate([offsets[w * nodes : (w + 1) * nodes, :].T for w in range(nconf)], axis=0)
    high, low = split(turned)
    return jnp.concatenate([high, high, low], axis=1)


def begin(
    dims, axes, fast,
    v_hbm, config_hbm, offset_hbm, slot_hbm, xi_hbm, strain_hbm, motion_hbm, viscosity_hbm,
    talk_ref, own_ref, split_ref, matrix_ref, hot_ref, weight_ref, config_ref, offset_ref, viscosity_ref,
    v_ref, slot_ref, xi_ref, strain_ref, motion_ref, sems,
):
    comps, nodes, cx, cy, cz, nconf, slots, lanes = dims
    blocks = cx * cy
    cells = blocks * cz
    copies = fetch(
        [(v_hbm, v_ref), (offset_hbm, offset_ref), (slot_hbm, slot_ref), (config_hbm, config_ref), (xi_hbm, xi_ref),
         (strain_hbm, strain_ref), (motion_hbm, motion_ref), (viscosity_hbm, viscosity_ref)],
        sems,
    )

    for copy in copies[2:5]:
        copy.wait()
    lane = iota((1, lanes), 1)
    targets = jnp.concatenate([slot_ref[...], jnp.full((1, lanes - slots), -1, jnp.int32)], axis=1)
    for y in range(blocks):
        targets = jnp.where(lane == lanes - 2 * blocks + y, y * cz, targets)
        targets = jnp.where(lane == lanes - blocks + y, (y + 1) * cz - 1, targets)
    hot = one_hot(targets, cells)
    hot_ref[...] = hot
    config = jnp.concatenate([config_ref[y : y + 1, :] for y in range(blocks)], axis=1)
    config = dot(jnp.broadcast_to(config.astype(F32), (16, cells)).astype(BF16), hot)[0:1, :]

    xi = [jnp.concatenate([xi_ref[j], jnp.zeros((1, lanes - slots), F32)], axis=1) for j in range(3)]
    (px, dx), (py, dy), (pz, dz) = shapes_of(xi, lanes)
    whole = py * pz
    basis = (px * whole, dx * whole, px * dy * pz, px * py * dz)
    for copy in copies[:2] + copies[5:]:
        copy.wait()
    raw = []
    for k in range(comps):
        row = 2 * k * nodes
        for y in range(blocks):
            high, low = split(v_ref[pl.ds(k * nodes * blocks + y, nodes, stride=blocks), :])
            at = slice(y * cz, (y + 1) * cz)
            split_ref[row : row + nodes, at] = high
            split_ref[row + nodes : row + 2 * nodes, at] = low
        both = dot(split_ref[row : row + 2 * nodes, :], hot)
        raw.append(both[:nodes] + both[nodes:])
    matrix = turned_matrix(offset_ref[...], nconf, nodes)
    matrix_ref[...] = matrix
    product = dot(matrix, jnp.concatenate([tripled(*split(p)) for p in basis], axis=1))
    weights = []
    for j in range(4):
        weights.append(basis[j] + configured(product[:, j * lanes : (j + 1) * lanes], config, nconf))
        weight_ref[j * nodes : (j + 1) * nodes, :] = weights[j]

    for k in range(comps):
        own_ref[k : k + 1, :] = jnp.sum(raw[k] * weights[0], axis=0, keepdims=True)
        for j in range(3):
            at = 3 + 3 * k + j
            own_ref[at : at + 1, :] = jnp.sum(raw[k] * weights[1 + j], axis=0, keepdims=True)
    for i in range(9):
        own_ref[12 + i : 13 + i, 0:slots] = strain_ref[i]
    for i in range(3):
        own_ref[21 + i : 22 + i, 0:slots] = motion_ref[i]

    count = comps * nodes // 24
    wide = 2 * blocks
    ends = jnp.concatenate([r[:, lanes - 128 :] for r in raw], axis=0)
    lane = iota((24, 128), 1)
    last = own_ref[:, lanes - 128 :]
    for g in range(count):
        start = 128 - (count - g) * wide
        group = pltpu.roll(ends[24 * g : 24 * (g + 1)], (start + wide) % 128, axis=1)
        last = jnp.where(lane >= start, group, last)
    last = jnp.concatenate([last, jnp.broadcast_to(config[:, lanes - 128 :], (8, 128))], axis=0)
    if fast:
        last = pltpu.roll(last, lax.axis_index(axes[2]) * slots, axis=1)
    elif lanes > 128:
        talk_ref[0:24, : lanes - 128] = own_ref[:, : lanes - 128]
    talk_ref[:, lanes - 128 :] = last


def local(
    dims, axes,
    split_ref, offset_ref, config_ref,
    con_ref, xa_ref, xb_ref, ya_ref, yb_ref,
    field_ref,
):
    comps, nodes, cx, cy, cz, nconf, slots, lanes = dims
    blocks = cx * cy
    me_x, me_y = lax.axis_index(axes[0]), lax.axis_index(axes[1])
    even_x, even_y = me_x % 2 == 0, me_y % 2 == 0
    config_rows = [config_ref[y : y + 1, :] for y in range(blocks)]

    def columns(k, ys):
        at = slice(ys[0] * cz, (ys[-1] + 1) * cz)
        high = split_ref[2 * k * nodes : (2 * k + 1) * nodes, at]
        low = split_ref[(2 * k + 1) * nodes : (2 * k + 2) * nodes, at]
        value = high.astype(F32) + low.astype(F32)
        return [value[:, i * cz : (i + 1) * cz] for i in range(len(ys))], tripled(high, low)

    def store(k, y, value):
        field_ref[(y * comps + k) * nodes : (y * comps + k + 1) * nodes, :] = value
        part, rest = split(value)
        row = 2 * k * nodes
        con_ref[row : row + nodes, y * cz : (y + 1) * cz] = part
        con_ref[row + nodes : row + 2 * nodes, y * cz : (y + 1) * cz] = rest

    constrain(plain_matrix(offset_ref[...]), columns, config_rows, store, nconf, comps, blocks, cz)

    face = nodes // 4
    for k in range(comps):
        for y in range(cy):
            low_row = (y * comps + k) * nodes
            up_row = (((cx - 1) * cy + y) * comps + k + 1) * nodes
            lower = field_ref[low_row : low_row + face, :]
            upper = field_ref[up_row - face : up_row, :]
            cells = slice(y * cz, (y + 1) * cz)
            xa_ref[k * face : (k + 1) * face, cells] = jnp.where(even_x, upper, lower)
            xb_ref[k * face : (k + 1) * face, cells] = jnp.where(even_x, lower, upper)
        for a in range(4):
            into = k * face + a * 4
            for x in range(cx):
                first = (x * cy * comps + k) * nodes + a * face
                last = ((x * cy + cy - 1) * comps + k) * nodes + a * face
                lower = field_ref[first : first + 4, :]
                upper = field_ref[last + 12 : last + 16, :]
                ya_ref[into : into + 4, x * cz : (x + 1) * cz] = jnp.where(even_y, upper, lower)
                yb_ref[into : into + 4, x * cz : (x + 1) * cz] = jnp.where(even_y, lower, upper)


def solid(vel, grad, strain, motion):
    deform = [strain[3 * j + l] + (1.0 if j == l else 0.0) for j in range(3) for l in range(3)]
    moved = []
    for k in range(3):
        for l in range(3):
            change = sum(grad[3 * k + j] * deform[3 * j + l] for j in range(3))
            moved.append(deform[3 * k + l] + TIME_STEP * change)
    stress = [
        sum(moved[3 * k + l] * moved[3 * m + l] for l in range(3)) - (1.0 if k == m else 0.0)
        for k in range(3) for m in range(3)
    ]
    drag = [SPRING_RATE * (motion[k] - vel[k]) for k in range(3)]
    return moved, stress, drag


def node_tables():
    i, j = iota((64, 64), 0), iota((64, 64), 1)
    digits = [((i >> s) & 3, (j >> s) & 3) for s in (4, 2, 0)]
    same = [p == q for p, q in digits]
    lap = jnp.zeros((64, 64), F32)
    swaps = []
    for d in range(3):
        others = same[(d + 1) % 3] & same[(d + 2) % 3]
        p, q = digits[d]
        line = jnp.where(p == q, 2.0, jnp.where((p - q == 1) | (q - p == 1), -1.0, 0.0))
        lap = lap + jnp.where(others, line, 0.0)
        swaps.append(jnp.where(others & (((p == 0) & (q == 3)) | ((p == 3) & (q == 0))), 1.0, 0.0))
    return jnp.concatenate([lap, swaps[2], swaps[1]], axis=0).astype(BF16)


def sides(even, open_b, a, b):
    b = jnp.where(open_b, b, 0.0)
    return jnp.where(even, b, a), jnp.where(even, a, b)


def place(axis, n):
    index = lax.axis_index(axis)
    even = index % 2 == 0
    return even, jnp.where(even, index, n - 1 - index) > 0


def middle(
    dims, axes, sizes, fast,
    za_ref, con_ref, viscosity_ref, offset_ref, matrix_ref, config_ref, xa_ref, xb_ref, zb_ref,
    total_ref,
):
    comps, nodes, cx, cy, cz, nconf, slots, lanes = dims
    blocks = cx * cy
    face = nodes // 4
    even_x, open_x = place(axes[0], sizes[0])
    even_z, open_z = place(axes[2], sizes[2])

    table = node_tables()
    table = jnp.concatenate([table, table], axis=1)
    row = iota((nodes, cz), 0)
    a, b, c = (row >> 4) & 3, (row >> 2) & 3, row & 3

    def ends(p):
        return jnp.where((p == 0) | (p == 3), PENALTY, 0.0)

    keep = 1.0 + ends(a) + ends(b) + ends(c)
    lane = iota((nodes, cz), 1)
    count = comps * nodes // 24
    wide = 2 * blocks
    plain = plain_matrix(offset_ref[...])

    def ends_of(ref):
        last = ref[:, lanes - 128 :]
        if fast:
            last = pltpu.roll(last, (lax.axis_index(axes[2]) + 1) % 2 * slots, axis=1)
        config = pltpu.roll(last[24:32], wide, axis=1)
        groups = [pltpu.roll(last[0:24], (count - g) * wide, axis=1) for g in range(count)]
        rows = jnp.concatenate(groups, axis=0)
        raw = rows[:nodes]
        spread_config = config[0:1]
        for k in range(1, comps):
            here = lane >= k * wide
            raw = jnp.where(here, pltpu.roll(rows[k * nodes : (k + 1) * nodes], k * wide, axis=1), raw)
            spread_config = jnp.where(here[0:1], pltpu.roll(config, k * wide, axis=1)[0:1], spread_config)
        raw = jnp.where(lane < comps * wide, raw, 0.0)
        return raw + configured(dot(plain, tripled(*split(raw))), spread_config, nconf)

    z_a = ends_of(za_ref)
    z_low, z_up = sides(even_z, open_z, z_a, z_a if fast else ends_of(zb_ref))
    z_low, z_up = pltpu.roll(z_low, nodes - 3, axis=0), pltpu.roll(z_up, 3, axis=0)
    config_rows = [config_ref[y : y + 1, :] for y in range(blocks)]
    matrix = matrix_ref[...]

    for k in range(comps):
        pair = con_ref[2 * k * nodes : 2 * (k + 1) * nodes, :]
        ops = dot(table, pair)
        rows = slice(k * face, (k + 1) * face)
        x_low, x_up = sides(even_x, open_x, xa_ref[rows, :], xb_ref[rows, :])
        values = []
        for y in range(blocks):
            x_at, y_at = y // cy, y % cy
            cells = slice(y * cz, (y + 1) * cz)
            value = pair[:nodes, cells].astype(F32) + pair[nodes:, cells].astype(F32)
            total = keep * value + viscosity_ref[y : y + 1, :] * ops[0:nodes, cells]
            moved_z = ops[nodes : 2 * nodes, cells]
            below = jnp.where(lane == 0, pltpu.roll(z_low, cz - k * wide - blocks - y, axis=1), pltpu.roll(moved_z, 1, axis=1))
            above = jnp.where(
                lane == cz - 1, pltpu.roll(z_up, cz - 1 - k * wide - y, axis=1), pltpu.roll(moved_z, cz - 1, axis=1)
            )
            near = jnp.where(c == 0, below, jnp.where(c == 3, above, 0.0))
            if y_at > 0:
                near = near + jnp.where(b == 0, ops[2 * nodes : 3 * nodes, (y - 1) * cz : y * cz], 0.0)
            if y_at < cy - 1:
                near = near + jnp.where(b == 3, ops[2 * nodes : 3 * nodes, (y + 1) * cz : (y + 2) * cz], 0.0)
            total = total - PENALTY * near
            plane = slice(y_at * cz, (y_at + 1) * cz)
            if x_at > 0:
                other = slice((y - cy) * cz, (y - cy + 1) * cz)
                below = pair[nodes - face : nodes, other].astype(F32) + pair[2 * nodes - face :, other].astype(F32)
            else:
                below = x_low[:, plane]
            if x_at < cx - 1:
                other = slice((y + cy) * cz, (y + cy + 1) * cz)
                above = pair[:face, other].astype(F32) + pair[nodes : nodes + face, other].astype(F32)
            else:
                above = x_up[:, plane]
            total = jnp.concatenate(
                [total[:face] - PENALTY * below, total[face : nodes - face], total[nodes - face :] - PENALTY * above],
                axis=0,
            )
            values.append(total)
        inner = [y for y in range(blocks) if 0 < y % cy < cy - 1]
        if inner:
            product = dot(matrix, tripled(*split(jnp.concatenate([values[y] for y in inner], axis=1))))
            for i, y in enumerate(inner):
                values[y] = values[y] + configured(product[:, i * cz : (i + 1) * cz], config_rows[y], nconf)
        for y in range(blocks):
            total_ref[k * nodes : (k + 1) * nodes, y * cz : (y + 1) * cz] = values[y]


def widen(face, nodes):
    return jnp.concatenate([face[4 * (i // 4) : 4 * (i // 4) + 4] for i in range(nodes // 4)], axis=0)


def gather_parts(refs, axes):
    me_y, me_s = lax.axis_index(axes[1]), lax.axis_index(axes[2])
    me = me_y * 2 + me_s
    lane = iota((24, 128), 1) >> 3
    parts = jnp.zeros((24, 128), F32)
    for flip, ref in enumerate(refs):
        block = ref[0:24, :]
        for half in range(2):
            source = (me_y ^ flip) * 2 + half
            shift = (source - me) * 8 + (128 - 64 * half)
            parts = jnp.where(lane == source, pltpu.roll(block, shift & 127, axis=1), parts)
    return parts + pltpu.roll(parts, 64, axis=1)


def after(
    dims, axes, sizes, fast,
    total_ref, yb_ref, *refs,
):
    if fast:
        got_2, ya_ref, pair_ref, *refs = refs
        refs = (*refs[:5], pair_ref, ya_ref, got_2, yb_ref, *refs[5:])
    else:
        ya_ref, parts_ref, *refs = refs
        refs = (*refs[:5], parts_ref, *refs[5:])
    matrix_ref, config_ref, hot_ref, weight_ref, own_ref, *refs = refs
    if fast:
        ya_ref, yb_ref = ya_ref.at[24:, :], yb_ref.at[24:, :]
    *part_refs, out_hbm, deform_hbm, out_ref, deform_ref, sems = refs
    comps, nodes, cx, cy, cz, nconf, slots, lanes = dims
    blocks = cx * cy
    face = nodes // 4
    even_y, open_y = place(axes[1], sizes[1])

    parts = gather_parts(part_refs, axes) if fast else part_refs[0][...]
    own = [own_ref[i : i + 1, :] for i in range(24)]
    got = [parts[i : i + 1, :] for i in range(24)]
    _, stress, drag = solid(own[0:3], own[3:12], got[12:21], got[21:24])
    moved, _, _ = solid(got[0:3], got[3:12], own[12:21], own[21:24])
    for i in range(9):
        deform_ref[i] = moved[i][:, :slots]
    copies = [pltpu.make_async_copy(deform_ref, deform_hbm, sems.at[4 * comps])]
    copies[0].start()
    hot = hot_ref[...]
    basis = [weight_ref[j * nodes : (j + 1) * nodes, :] for j in range(4)]
    row = iota((nodes, cz), 0)
    b = (row >> 2) & 3
    live = iota((nodes, lanes), 1) < slots
    highs, lows = [], []
    for k in range(comps):
        force = drag[k] * basis[0]
        for j in range(3):
            force = force - stress[3 * k + j] * basis[1 + j]
        high, low = split(jnp.where(live, force, 0.0))
        highs.append(high)
        lows.append(low)
    spreads = dot(jnp.concatenate(highs + lows, axis=0), hot, ((1,), (1,)))

    config_rows = [config_ref[y : y + 1, :] for y in range(blocks)]
    matrix = matrix_ref[...]
    step = nodes * blocks // 4
    outer = [y for y in range(blocks) if y % cy in (0, cy - 1)]
    for k in range(comps):
        rows = slice(k * face, (k + 1) * face)
        y_low, y_up = sides(even_y, open_y, ya_ref[rows, :], yb_ref[rows, :])
        values = [total_ref[k * nodes : (k + 1) * nodes, y * cz : (y + 1) * cz] for y in range(blocks)]
        for y in outer:
            plane = slice(y // cy * cz, (y // cy + 1) * cz)
            if y % cy == 0:
                values[y] = values[y] - jnp.where(b == 0, PENALTY * widen(y_low[:, plane], nodes), 0.0)
            if y % cy == cy - 1:
                values[y] = values[y] - jnp.where(b == 3, PENALTY * widen(y_up[:, plane], nodes), 0.0)
        product = dot(matrix, tripled(*split(jnp.concatenate([values[y] for y in outer], axis=1))))
        for i, y in enumerate(outer):
            values[y] = values[y] + configured(product[:, i * cz : (i + 1) * cz], config_rows[y], nconf)
        for y in range(blocks):
            cells = slice(y * cz, (y + 1) * cz)
            for part in (k, comps + k):
                values[y] = values[y] - spreads[part * nodes : (part + 1) * nodes, cells]
            out_ref[pl.ds(k * nodes * blocks + y, nodes, stride=blocks), :] = values[y]
        for i in range(4 * k, 4 * k + 4):
            done = slice(i * step, (i + 1) * step)
            copies.append(pltpu.make_async_copy(out_ref.at[done, :], out_hbm.at[done, :], sems.at[i]))
            copies[-1].start()
    for copy in copies:
        copy.wait()


def swap(x, axis, stage):
    n = lax.axis_size(axis)
    pairs = [(i, i + 1) for i in range(stage, n - 1, 2)]
    if not pairs:
        return jnp.zeros_like(x)
    return lax.ppermute(x, axis, pairs + [(j, i) for i, j in pairs])


def flip(x, axis, bits):
    return lax.ppermute(x, axis, [(i, i ^ bits) for i in range(lax.axis_size(axis))])


def shards(
    mesh_sizes,
    velocity,
    viscosity,
    cell_config,
    constraint_offsets,
    slot_cells,
    point_coords,
    strain_offsets,
    solid_velocity,
):
    axes = ("dx", "dy", "solid")
    comps, cx, cy, cz = velocity.shape[0], *velocity.shape[4:]
    nodes = velocity.shape[1] * velocity.shape[2] * velocity.shape[3]
    blocks = cx * cy
    nconf = constraint_offsets.shape[0]
    slots = slot_cells.shape[-1]
    n_dx, n_dy, n_solid = mesh_sizes
    face_rows = comps * nodes // 4
    lanes = pl.cdiv(slots + comps * nodes // 24 * 2 * blocks, 128) * 128
    dims = (comps, nodes, cx, cy, cz, nconf, slots, lanes)

    v = velocity.reshape(comps * nodes * blocks, cz)
    visc = viscosity.reshape(blocks, cz)
    config = cell_config.reshape(blocks, cz)
    offsets = constraint_offsets.reshape(nconf * nodes, nodes)
    targets = slot_cells.reshape(1, slots)
    xi = point_coords.reshape(3, 1, slots)
    strain = strain_offsets.reshape(9, 1, slots)
    motion = solid_velocity.reshape(3, 1, slots)

    vmem = pl.BlockSpec(memory_space=pltpu.VMEM)
    hbm = pl.BlockSpec(memory_space=pltpu.HBM)
    params = pltpu.CompilerParams(vmem_limit_bytes=VMEM_LIMIT)
    cells = blocks * cz
    face_y = jax.ShapeDtypeStruct((face_rows, cx * cz), F32)
    face_x = jax.ShapeDtypeStruct((face_rows, cy * cz), F32)
    def shape(*size, dtype=F32):
        return jax.ShapeDtypeStruct(size, dtype)

    def estimate(columns):
        return pl.CostEstimate(flops=2 * 6 * nconf * nodes * nodes * columns, bytes_accessed=1_000_000, transcendentals=0)

    fast = (n_dx, n_dy, n_solid, slots, lanes) == (4, 4, 2, 64, 128)
    talk, own, parted, matrix, hot, weights, config, offsets, visc = pl.pallas_call(
        functools.partial(begin, dims, axes, fast),
        out_shape=(
            shape(32, lanes),
            shape(24, lanes),
            shape(2 * comps * nodes, cells, dtype=BF16),
            shape(nconf * nodes, 3 * nodes, dtype=BF16),
            shape(cells, lanes, dtype=BF16),
            shape(4 * nodes, lanes),
            shape(*config.shape, dtype=config.dtype),
            shape(*offsets.shape),
            shape(*visc.shape),
        ),
        in_specs=[hbm] * 8,
        out_specs=(vmem,) * 9,
        scratch_shapes=[
            pltpu.VMEM(v.shape, F32),
            pltpu.VMEM(targets.shape, targets.dtype),
            pltpu.VMEM(xi.shape, F32),
            pltpu.VMEM(strain.shape, F32),
            pltpu.VMEM(motion.shape, F32),
            pltpu.SemaphoreType.DMA((8,)),
        ],
        compiler_params=params,
        name="begin",
    )(*(pltpu.with_memory_space_constraint(x, pltpu.HBM) for x in (v, config, offsets, targets, xi, strain, motion, visc)))

    con, xa, xb, ya, yb = pl.pallas_call(
        functools.partial(local, dims, axes),
        out_shape=(shape(2 * comps * nodes, cells, dtype=BF16), face_x, face_x, face_y, face_y),
        in_specs=[vmem] * 3,
        out_specs=(vmem,) * 5,
        scratch_shapes=[pltpu.VMEM((blocks * comps * nodes, cz), F32)],
        compiler_params=params,
        cost_estimate=estimate(comps * cells),
        name="local",
    )(parted, offsets, config)

    if fast:
        got_s = swap(talk, "solid", 0)
        got_xa = swap(xa, "dx", 0)
        got_xb = flip(xb, "dx", 3)
        mine = (iota((24, 128), 1) >= 64) == (lax.axis_index("solid") == 1)
        pair = jnp.where(mine, talk[:24], got_s[:24])
        got_3 = flip(jnp.concatenate([pair, yb, pair[:8]], axis=0), "dy", 3)
        got_2 = flip(jnp.concatenate([pair, yb[:8]], axis=0), "dy", 2)
        got_1 = flip(jnp.concatenate([pair, ya], axis=0), "dy", 1)
        parts = [got_2, got_1, pair]
        got_yb = got_3
        got_za, got_zb = got_s, got_s
    else:
        got_xa, got_xb = swap(xa, "dx", 0), swap(xb, "dx", 1)
        got_ya, got_yb = swap(ya, "dy", 0), swap(yb, "dy", 1)
        got_za, got_zb = swap(talk, "solid", 0), swap(talk, "solid", 1)
        got_parts = lax.all_to_all(talk[:24, :slots], ("dy", "solid"), split_axis=1, concat_axis=1, tiled=True)
        parts = [got_ya, jnp.pad(got_parts, ((0, 0), (0, lanes - slots)))]

    total = pl.pallas_call(
        functools.partial(middle, dims, axes, mesh_sizes, fast),
        out_shape=shape(comps * nodes, cells),
        in_specs=[vmem] * 9,
        out_specs=vmem,
        compiler_params=params,
        cost_estimate=estimate(comps * cells),
        name="middle",
    )(got_za, con, visc, offsets, matrix, config, got_xa, got_xb, got_zb)

    out, deform = pl.pallas_call(
        functools.partial(after, dims, axes, mesh_sizes, fast),
        out_shape=(
            jax.ShapeDtypeStruct(v.shape, F32),
            jax.ShapeDtypeStruct((9, 1, slots), F32),
        ),
        in_specs=[vmem] * (7 + len(parts)),
        out_specs=(hbm, hbm),
        scratch_shapes=[
            pltpu.VMEM(v.shape, F32),
            pltpu.VMEM(strain.shape, F32),
            pltpu.SemaphoreType.DMA((4 * comps + 1,)),
        ],
        compiler_params=params,
        name="after",
    )(total, got_yb, *parts, matrix, config, hot, weights, own)
    return out.reshape(velocity.shape), deform.reshape(strain_offsets.shape)


def solution(mesh):
    sizes = tuple(mesh.shape[a] for a in ("dx", "dy", "solid"))
    return jax.shard_map(
        functools.partial(shards, sizes),
        mesh=mesh,
        in_specs=(
            P(None, None, None, None, "dx", "dy", "solid"),
            P("dx", "dy", "solid"),
            P("dx", "dy", "solid"),
            P(),
            P("dx", ("dy", "solid"), None),
            P(None, "dx", ("dy", "solid"), None),
            P(None, None, "dx", ("dy", "solid"), None),
            P(None, "dx", ("dy", "solid"), None),
        ),
        out_specs=(
            P(None, None, None, None, "dx", "dy", "solid"),
            P(None, None, "dx", ("dy", "solid"), None),
        ),
        check_vma=False,
    )
```

```python
import functools

import jax
import jax.numpy as jnp
from jax import lax
from jax.experimental import pallas as pl
from jax.experimental.pallas import tpu as pltpu
from jax.sharding import PartitionSpec as P

TIME_STEP = 0.05
SPRING_RATE = 2.0
PENALTY = 4.0
NODE_POINTS = (0.0, 1.0 / 3.0, 2.0 / 3.0, 1.0)
F32, BF16 = jnp.float32, jnp.bfloat16
VMEM_LIMIT = 24 * 1024 * 1024


def iota(shape, dim):
    return lax.broadcasted_iota(jnp.int32, shape, dim)


def split(x):
    high = x.astype(BF16)
    low = (x - high.astype(F32)).astype(BF16)
    return high, low


def dot(a, b, dims=((1,), (0,))):
    return lax.dot_general(a, b, (dims, ((), ())), preferred_element_type=F32)


def lagrange(coord):
    values = []
    slopes = []
    for which in range(4):
        others = [NODE_POINTS[j] for j in range(4) if j != which]
        denom = 1.0
        for other in others:
            denom = denom * (NODE_POINTS[which] - other)
        scale = 1.0 / denom
        first = coord - others[0]
        second = coord - others[1]
        third = coord - others[2]
        values.append(first * second * third * scale)
        slopes.append((second * third + first * third + first * second) * scale)
    return values, slopes


def spread_rows(parts, dim, lanes):
    wide = [jnp.broadcast_to(p, (8, lanes)) for p in parts]
    if dim == 0:
        return jnp.concatenate([wide[a] for a in (0, 0, 1, 1, 2, 2, 3, 3)], axis=0)
    row = iota((8, lanes), 0)
    if dim == 1:
        even = jnp.where(row < 4, wide[0], wide[1])
        odd = jnp.where(row < 4, wide[2], wide[3])
        return jnp.concatenate([even, odd] * 4, axis=0)
    c = row & 3
    block = jnp.where(c == 0, wide[0], jnp.where(c == 1, wide[1], jnp.where(c == 2, wide[2], wide[3])))
    return jnp.concatenate([block] * 8, axis=0)


def shapes_of(xi, lanes):
    out = []
    for dim in range(3):
        values, slopes = lagrange(xi[dim])
        out.append((spread_rows(values, dim, lanes), spread_rows(slopes, dim, lanes)))
    return out


def one_hot(slots, cells):
    lanes = slots.shape[1]
    return jnp.where(iota((cells, lanes), 0) == slots, 1.0, 0.0).astype(BF16)


def configured(product, config, nconf):
    rows = product.shape[0] // nconf
    chosen = product[:rows]
    for which in range(1, nconf):
        chosen = jnp.where(config == which, product[which * rows : (which + 1) * rows], chosen)
    return chosen


def tripled(high, low):
    return jnp.concatenate([high, low, high], axis=0)


def constrain(matrix, columns, config_rows, store, nconf, comps, blocks, lanes):
    step = 2 if blocks % 2 == 0 else 1
    for k in range(comps):
        for first in range(0, blocks, step):
            values, parts = columns(k, range(first, first + step))
            product = dot(matrix, parts)
            for i in range(step):
                piece = product[:, i * lanes : (i + 1) * lanes]
                store(k, first + i, values[i] + configured(piece, config_rows[first + i], nconf))


def fetch(pairs, sems):
    copies = [pltpu.make_async_copy(src, dst, sems.at[i]) for i, (src, dst) in enumerate(pairs)]
    for copy in copies:
        copy.start()
    return copies


def plain_matrix(offsets):
    high, low = split(offsets)
    return jnp.concatenate([high, high, low], axis=1)


def turned_matrix(offsets, nconf, nodes):
    turned = jnp.concatenate([offsets[w * nodes : (w + 1) * nodes, :].T for w in range(nconf)], axis=0)
    high, low = split(turned)
    return jnp.concatenate([high, high, low], axis=1)


def begin(
    dims, axes, fast,
    v_hbm, config_hbm, offset_hbm, slot_hbm, xi_hbm, strain_hbm, motion_hbm, viscosity_hbm,
    talk_ref, own_ref, split_ref, matrix_ref, target_ref, weight_ref, config_ref, offset_ref, viscosity_ref,
    v_ref, slot_ref, xi_ref, strain_ref, motion_ref, sems,
):
    comps, nodes, cx, cy, cz, nconf, slots, lanes = dims
    blocks = cx * cy
    cells = blocks * cz
    copies = fetch(
        [(v_hbm, v_ref), (offset_hbm, offset_ref), (slot_hbm, slot_ref), (config_hbm, config_ref), (xi_hbm, xi_ref),
         (strain_hbm, strain_ref), (motion_hbm, motion_ref), (viscosity_hbm, viscosity_ref)],
        sems,
    )

    for copy in copies[2:5]:
        copy.wait()
    targets = jnp.concatenate([slot_ref[...]] * 2, axis=1)
    target_ref[...] = targets
    lane = iota((1, 128), 1)
    ends = jnp.full((1, 128), -1, jnp.int32)
    for y in range(blocks):
        ends = jnp.where(lane == 128 - 2 * blocks + y, y * cz, ends)
        ends = jnp.where(lane == 128 - blocks + y, (y + 1) * cz - 1, ends)
    hot = one_hot(jnp.concatenate([targets, ends], axis=1), cells)
    config = jnp.concatenate([config_ref[y : y + 1, :] for y in range(blocks)], axis=1)
    config = dot(jnp.broadcast_to(config.astype(F32), (16, cells)).astype(BF16), hot)[0:1, :]

    half = iota((1, lanes), 1) < slots
    xi = [jnp.concatenate([xi_ref[j]] * 2, axis=1) for j in range(3)]
    (px, dx), (py, dy), (pz, dz) = shapes_of(xi, lanes)
    basis = (jnp.where(half, px, dx) * (py * pz), px * jnp.where(half, dy * pz, py * dz))
    for copy in copies[:2] + copies[5:]:
        copy.wait()
    raw = []
    for k in range(comps):
        row = 2 * k * nodes
        for y in range(blocks):
            high, low = split(v_ref[pl.ds(k * nodes * blocks + y, nodes, stride=blocks), :])
            at = slice(y * cz, (y + 1) * cz)
            split_ref[row : row + nodes, at] = high
            split_ref[row + nodes : row + 2 * nodes, at] = low
        both = dot(split_ref[row : row + 2 * nodes, :], hot)
        raw.append(both[:nodes] + both[nodes:])
    matrix = turned_matrix(offset_ref[...], nconf, nodes)
    matrix_ref[...] = matrix
    product = dot(matrix, jnp.concatenate([tripled(*split(p)) for p in basis], axis=1))
    weights = []
    for j in range(2):
        weights.append(basis[j] + configured(product[:, j * lanes : (j + 1) * lanes], config[:, :lanes], nconf))
        weight_ref[j * nodes : (j + 1) * nodes, :] = weights[j]

    for k in range(comps):
        for j in range(2):
            sums = jnp.sum(raw[k][:, :lanes] * weights[j], axis=0, keepdims=True)
            other = pltpu.roll(sums, slots, axis=1)
            left, right = ((k, 3 + 3 * k), (4 + 3 * k, 5 + 3 * k))[j]
            own_ref[left : left + 1, :] = jnp.where(half, sums, other)
            own_ref[right : right + 1, :] = jnp.where(half, other, sums)
    for i in range(9):
        own_ref[12 + i : 13 + i, :] = jnp.concatenate([strain_ref[i]] * 2, axis=1)
    for i in range(3):
        own_ref[21 + i : 22 + i, :] = jnp.concatenate([motion_ref[i]] * 2, axis=1)

    count = comps * nodes // 24
    wide = 2 * blocks
    ends = jnp.concatenate([r[:, lanes:] for r in raw], axis=0)
    lane = iota((24, 128), 1)
    last = own_ref[:, lanes - 128 :]
    for g in range(count):
        start = 128 - (count - g) * wide
        group = pltpu.roll(ends[24 * g : 24 * (g + 1)], (start + wide) % 128, axis=1)
        last = jnp.where(lane >= start, group, last)
    last = jnp.concatenate([last, jnp.broadcast_to(config[:, lanes:], (8, 128))], axis=0)
    if fast:
        last = pltpu.roll(last, lax.axis_index(axes[2]) * slots, axis=1)
    else:
        talk_ref[0:24, :slots] = own_ref[:, :slots]
    talk_ref[:, talk_ref.shape[1] - 128 :] = last


def local(
    dims, axes,
    split_ref, offset_ref, config_ref,
    con_ref, xa_ref, xb_ref, ya_ref, yb_ref,
    field_ref,
):
    comps, nodes, cx, cy, cz, nconf, slots, lanes = dims
    blocks = cx * cy
    me_x, me_y = lax.axis_index(axes[0]), lax.axis_index(axes[1])
    even_x, even_y = me_x % 2 == 0, me_y % 2 == 0
    config_rows = [config_ref[y : y + 1, :] for y in range(blocks)]

    def columns(k, ys):
        at = slice(ys[0] * cz, (ys[-1] + 1) * cz)
        high = split_ref[2 * k * nodes : (2 * k + 1) * nodes, at]
        low = split_ref[(2 * k + 1) * nodes : (2 * k + 2) * nodes, at]
        value = high.astype(F32) + low.astype(F32)
        return [value[:, i * cz : (i + 1) * cz] for i in range(len(ys))], tripled(high, low)

    def store(k, y, value):
        field_ref[(y * comps + k) * nodes : (y * comps + k + 1) * nodes, :] = value
        part, rest = split(value)
        row = 2 * k * nodes
        con_ref[row : row + nodes, y * cz : (y + 1) * cz] = part
        con_ref[row + nodes : row + 2 * nodes, y * cz : (y + 1) * cz] = rest

    constrain(plain_matrix(offset_ref[...]), columns, config_rows, store, nconf, comps, blocks, cz)

    face = nodes // 4
    for k in range(comps):
        for y in range(cy):
            low_row = (y * comps + k) * nodes
            up_row = (((cx - 1) * cy + y) * comps + k + 1) * nodes
            lower = field_ref[low_row : low_row + face, :]
            upper = field_ref[up_row - face : up_row, :]
            cells = slice(y * cz, (y + 1) * cz)
            xa_ref[k * face : (k + 1) * face, cells] = jnp.where(even_x, upper, lower)
            xb_ref[k * face : (k + 1) * face, cells] = jnp.where(even_x, lower, upper)
        for a in range(4):
            into = k * face + a * 4
            for x in range(cx):
                first = (x * cy * comps + k) * nodes + a * face
                last = ((x * cy + cy - 1) * comps + k) * nodes + a * face
                lower = field_ref[first : first + 4, :]
                upper = field_ref[last + 12 : last + 16, :]
                ya_ref[into : into + 4, x * cz : (x + 1) * cz] = jnp.where(even_y, upper, lower)
                yb_ref[into : into + 4, x * cz : (x + 1) * cz] = jnp.where(even_y, lower, upper)


def solid(vel, grad, strain, motion):
    deform = [strain[3 * j + l] + (1.0 if j == l else 0.0) for j in range(3) for l in range(3)]
    moved = []
    for k in range(3):
        for l in range(3):
            change = sum(grad[3 * k + j] * deform[3 * j + l] for j in range(3))
            moved.append(deform[3 * k + l] + TIME_STEP * change)
    stress = [
        sum(moved[3 * k + l] * moved[3 * m + l] for l in range(3)) - (1.0 if k == m else 0.0)
        for k in range(3) for m in range(3)
    ]
    drag = [SPRING_RATE * (motion[k] - vel[k]) for k in range(3)]
    return moved, stress, drag


def node_tables():
    i, j = iota((64, 64), 0), iota((64, 64), 1)
    digits = [((i >> s) & 3, (j >> s) & 3) for s in (4, 2, 0)]
    same = [p == q for p, q in digits]
    lap = jnp.zeros((64, 64), F32)
    swaps = []
    for d in range(3):
        others = same[(d + 1) % 3] & same[(d + 2) % 3]
        p, q = digits[d]
        line = jnp.where(p == q, 2.0, jnp.where((p - q == 1) | (q - p == 1), -1.0, 0.0))
        lap = lap + jnp.where(others, line, 0.0)
        swaps.append(jnp.where(others & (((p == 0) & (q == 3)) | ((p == 3) & (q == 0))), 1.0, 0.0))
    return jnp.concatenate([lap, swaps[2], swaps[1]], axis=0).astype(BF16)


def sides(even, open_b, a, b):
    b = jnp.where(open_b, b, 0.0)
    return jnp.where(even, b, a), jnp.where(even, a, b)


def place(axis, n):
    index = lax.axis_index(axis)
    even = index % 2 == 0
    return even, jnp.where(even, index, n - 1 - index) > 0


def middle(
    dims, axes, sizes, fast,
    za_ref, con_ref, viscosity_ref, offset_ref, matrix_ref, config_ref, xa_ref, xb_ref, zb_ref, target_ref,
    total_ref, hot_ref,
):
    comps, nodes, cx, cy, cz, nconf, slots, lanes = dims
    blocks = cx * cy
    face = nodes // 4
    even_x, open_x = place(axes[0], sizes[0])
    even_z, open_z = place(axes[2], sizes[2])

    table = node_tables()
    table = jnp.concatenate([table, table], axis=1)
    row = iota((nodes, cz), 0)
    a, b, c = (row >> 4) & 3, (row >> 2) & 3, row & 3

    def ends(p):
        return jnp.where((p == 0) | (p == 3), PENALTY, 0.0)

    keep = 1.0 + ends(a) + ends(b) + ends(c)
    lane = iota((nodes, cz), 1)
    count = comps * nodes // 24
    wide = 2 * blocks
    plain = plain_matrix(offset_ref[...])
    hot_ref[...] = one_hot(jnp.concatenate([target_ref[...]] * 2, axis=1), blocks * cz)

    def ends_of(ref):
        last = ref[:, ref.shape[1] - 128 :]
        if fast:
            last = pltpu.roll(last, (lax.axis_index(axes[2]) + 1) % 2 * slots, axis=1)
        config = pltpu.roll(last[24:32], wide, axis=1)
        groups = [pltpu.roll(last[0:24], (count - g) * wide, axis=1) for g in range(count)]
        rows = jnp.concatenate(groups, axis=0)
        raw = rows[:nodes]
        spread_config = config[0:1]
        for k in range(1, comps):
            here = lane >= k * wide
            raw = jnp.where(here, pltpu.roll(rows[k * nodes : (k + 1) * nodes], k * wide, axis=1), raw)
            spread_config = jnp.where(here[0:1], pltpu.roll(config, k * wide, axis=1)[0:1], spread_config)
        raw = jnp.where(lane < comps * wide, raw, 0.0)
        return raw + configured(dot(plain, tripled(*split(raw))), spread_config, nconf)

    z_a = ends_of(za_ref)
    z_low, z_up = sides(even_z, open_z, z_a, z_a if fast else ends_of(zb_ref))
    z_low, z_up = pltpu.roll(z_low, nodes - 3, axis=0), pltpu.roll(z_up, 3, axis=0)
    config_rows = [config_ref[y : y + 1, :] for y in range(blocks)]
    matrix = matrix_ref[...]

    for k in range(comps):
        pair = con_ref[2 * k * nodes : 2 * (k + 1) * nodes, :]
        ops = dot(table, pair)
        rows = slice(k * face, (k + 1) * face)
        x_low, x_up = sides(even_x, open_x, xa_ref[rows, :], xb_ref[rows, :])
        values = []
        for y in range(blocks):
            x_at, y_at = y // cy, y % cy
            cells = slice(y * cz, (y + 1) * cz)
            value = pair[:nodes, cells].astype(F32) + pair[nodes:, cells].astype(F32)
            total = keep * value + viscosity_ref[y : y + 1, :] * ops[0:nodes, cells]
            moved_z = ops[nodes : 2 * nodes, cells]
            below = jnp.where(lane == 0, pltpu.roll(z_low, cz - k * wide - blocks - y, axis=1), pltpu.roll(moved_z, 1, axis=1))
            above = jnp.where(
                lane == cz - 1, pltpu.roll(z_up, cz - 1 - k * wide - y, axis=1), pltpu.roll(moved_z, cz - 1, axis=1)
            )
            near = jnp.where(c == 0, below, jnp.where(c == 3, above, 0.0))
            if y_at > 0:
                near = near + jnp.where(b == 0, ops[2 * nodes : 3 * nodes, (y - 1) * cz : y * cz], 0.0)
            if y_at < cy - 1:
                near = near + jnp.where(b == 3, ops[2 * nodes : 3 * nodes, (y + 1) * cz : (y + 2) * cz], 0.0)
            total = total - PENALTY * near
            plane = slice(y_at * cz, (y_at + 1) * cz)
            if x_at > 0:
                other = slice((y - cy) * cz, (y - cy + 1) * cz)
                below = pair[nodes - face : nodes, other].astype(F32) + pair[2 * nodes - face :, other].astype(F32)
            else:
                below = x_low[:, plane]
            if x_at < cx - 1:
                other = slice((y + cy) * cz, (y + cy + 1) * cz)
                above = pair[:face, other].astype(F32) + pair[nodes : nodes + face, other].astype(F32)
            else:
                above = x_up[:, plane]
            total = jnp.concatenate(
                [total[:face] - PENALTY * below, total[face : nodes - face], total[nodes - face :] - PENALTY * above],
                axis=0,
            )
            values.append(total)
        inner = [y for y in range(blocks) if 0 < y % cy < cy - 1]
        if inner:
            product = dot(matrix, tripled(*split(jnp.concatenate([values[y] for y in inner], axis=1))))
            for i, y in enumerate(inner):
                values[y] = values[y] + configured(product[:, i * cz : (i + 1) * cz], config_rows[y], nconf)
        for y in range(blocks):
            total_ref[k * nodes : (k + 1) * nodes, y * cz : (y + 1) * cz] = values[y]


def outer_blocks(cx, cy):
    return [y for y in range(cx * cy) if y % cy in (0, cy - 1)]


def widen(face, nodes):
    return jnp.concatenate([face[4 * (i // 4) : 4 * (i // 4) + 4] for i in range(nodes // 4)], axis=0)


def gather_parts(refs, axes):
    me_y, me_s = lax.axis_index(axes[1]), lax.axis_index(axes[2])
    me = me_y * 2 + me_s
    lane = iota((24, 128), 1) >> 3
    parts = jnp.zeros((24, 128), F32)
    for flip, ref in enumerate(refs):
        block = ref[0:24, :]
        for half in range(2):
            source = (me_y ^ flip) * 2 + half
            shift = (source - me) * 8 + (128 - 64 * half)
            parts = jnp.where(lane == source, pltpu.roll(block, shift & 127, axis=1), parts)
    return parts + pltpu.roll(parts, 64, axis=1)


def rim(
    dims, axes, sizes, fast,
    total_ref, yb_ref, ya_ref, matrix_ref, config_ref,
    rim_ref,
):
    comps, nodes, cx, cy, cz, nconf, slots, lanes = dims
    face = nodes // 4
    even_y, open_y = place(axes[1], sizes[1])
    first = 24 if fast else 0
    b = (iota((nodes, cz), 0) >> 2) & 3
    matrix = matrix_ref[...]
    for k in range(comps):
        rows = slice(first + k * face, first + (k + 1) * face)
        y_low, y_up = sides(even_y, open_y, ya_ref[rows, :], yb_ref[rows, :])
        outer = outer_blocks(cx, cy)
        values = []
        for y in outer:
            plane = slice(y // cy * cz, (y // cy + 1) * cz)
            value = total_ref[k * nodes : (k + 1) * nodes, y * cz : (y + 1) * cz]
            if y % cy == 0:
                value = value - jnp.where(b == 0, PENALTY * widen(y_low[:, plane], nodes), 0.0)
            if y % cy == cy - 1:
                value = value - jnp.where(b == 3, PENALTY * widen(y_up[:, plane], nodes), 0.0)
            values.append(value)
        product = dot(matrix, tripled(*split(jnp.concatenate(values, axis=1))))
        for i, y in enumerate(outer):
            at = slice(i * cz, (i + 1) * cz)
            rim_ref[k * nodes : (k + 1) * nodes, at] = values[i] + configured(product[:, at], config_ref[y : y + 1, :], nconf)


def after(
    dims, axes, fast,
    total_ref, *refs,
):
    comps, nodes, cx, cy, cz, nconf, slots, lanes = dims
    blocks = cx * cy
    if fast:
        got_3, got_2, got_1, pair_ref, *refs = refs
        part_refs = (pair_ref, got_1, got_2, got_3)
    else:
        *part_refs, refs = refs[0], refs[1:]
    rim_ref, hot_ref, weight_ref, own_ref, out_hbm, deform_hbm, out_ref, deform_ref, sems = refs

    parts = gather_parts(part_refs, axes) if fast else part_refs[0][...]
    own = [own_ref[i : i + 1, :] for i in range(24)]
    got = [parts[i : i + 1, :] for i in range(24)]
    _, stress, drag = solid(own[0:3], own[3:12], got[12:21], got[21:24])
    moved, _, _ = solid(got[0:3], got[3:12], own[12:21], own[21:24])
    for i in range(9):
        deform_ref[i] = moved[i][:, :slots]
    copies = [pltpu.make_async_copy(deform_ref, deform_hbm, sems.at[comps])]
    copies[0].start()
    hot = hot_ref[...]
    half = iota((1, lanes), 1) < slots
    highs, lows = [], []
    for k in range(comps):
        force = jnp.where(half, drag[k], -stress[3 * k]) * weight_ref[:nodes, :]
        force = force - jnp.where(half, stress[3 * k + 1], stress[3 * k + 2]) * weight_ref[nodes:, :]
        high, low = split(force)
        highs.append(high)
        lows.append(low)
    pieces = jnp.concatenate([jnp.concatenate(highs, axis=0), jnp.concatenate(lows, axis=0)], axis=1)
    spreads = dot(pieces, hot, ((1,), (1,)))

    outer = outer_blocks(cx, cy)
    for k in range(comps):
        rows = slice(k * nodes, (k + 1) * nodes)
        for y in range(blocks):
            cells = slice(y * cz, (y + 1) * cz)
            if y in outer:
                value = rim_ref[rows, outer.index(y) * cz : (outer.index(y) + 1) * cz]
            else:
                value = total_ref[rows, cells]
            out_ref[pl.ds(k * nodes * blocks + y, nodes, stride=blocks), :] = value - spreads[rows, cells]
        done = slice(k * nodes * blocks, (k + 1) * nodes * blocks)
        copies.append(pltpu.make_async_copy(out_ref.at[done, :], out_hbm.at[done, :], sems.at[k]))
        copies[-1].start()
    for copy in copies:
        copy.wait()


def swap(x, axis, stage):
    n = lax.axis_size(axis)
    pairs = [(i, i + 1) for i in range(stage, n - 1, 2)]
    if not pairs:
        return jnp.zeros_like(x)
    return lax.ppermute(x, axis, pairs + [(j, i) for i, j in pairs])


def flip(x, axis, bits):
    return lax.ppermute(x, axis, [(i, i ^ bits) for i in range(lax.axis_size(axis))])


def shards(
    mesh_sizes,
    velocity,
    viscosity,
    cell_config,
    constraint_offsets,
    slot_cells,
    point_coords,
    strain_offsets,
    solid_velocity,
):
    axes = ("dx", "dy", "solid")
    comps, cx, cy, cz = velocity.shape[0], *velocity.shape[4:]
    nodes = velocity.shape[1] * velocity.shape[2] * velocity.shape[3]
    blocks = cx * cy
    nconf = constraint_offsets.shape[0]
    slots = slot_cells.shape[-1]
    n_dx, n_dy, n_solid = mesh_sizes
    face_rows = comps * nodes // 4
    lanes = 2 * slots
    talk_lanes = lanes if comps * nodes // 24 * 2 * blocks <= slots == 64 else slots + 128
    dims = (comps, nodes, cx, cy, cz, nconf, slots, lanes)

    v = velocity.reshape(comps * nodes * blocks, cz)
    visc = viscosity.reshape(blocks, cz)
    config = cell_config.reshape(blocks, cz)
    offsets = constraint_offsets.reshape(nconf * nodes, nodes)
    targets = slot_cells.reshape(1, slots)
    xi = point_coords.reshape(3, 1, slots)
    strain = strain_offsets.reshape(9, 1, slots)
    motion = solid_velocity.reshape(3, 1, slots)

    vmem = pl.BlockSpec(memory_space=pltpu.VMEM)
    hbm = pl.BlockSpec(memory_space=pltpu.HBM)
    params = pltpu.CompilerParams(vmem_limit_bytes=VMEM_LIMIT)
    cells = blocks * cz
    face_y = jax.ShapeDtypeStruct((face_rows, cx * cz), F32)
    face_x = jax.ShapeDtypeStruct((face_rows, cy * cz), F32)
    def shape(*size, dtype=F32):
        return jax.ShapeDtypeStruct(size, dtype)

    def estimate(columns):
        return pl.CostEstimate(flops=2 * 6 * nconf * nodes * nodes * columns, bytes_accessed=1_000_000, transcendentals=0)

    fast = (n_dx, n_dy, n_solid, slots, talk_lanes) == (4, 4, 2, 64, 128)
    talk, own, parted, matrix, targets, weights, config, offsets, visc = pl.pallas_call(
        functools.partial(begin, dims, axes, fast),
        out_shape=(
            shape(32, talk_lanes),
            shape(24, lanes),
            shape(2 * comps * nodes, cells, dtype=BF16),
            shape(nconf * nodes, 3 * nodes, dtype=BF16),
            shape(1, lanes, dtype=targets.dtype),
            shape(2 * nodes, lanes),
            shape(*config.shape, dtype=config.dtype),
            shape(*offsets.shape),
            shape(*visc.shape),
        ),
        in_specs=[hbm] * 8,
        out_specs=(vmem,) * 9,
        scratch_shapes=[
            pltpu.VMEM(v.shape, F32),
            pltpu.VMEM(targets.shape, targets.dtype),
            pltpu.VMEM(xi.shape, F32),
            pltpu.VMEM(strain.shape, F32),
            pltpu.VMEM(motion.shape, F32),
            pltpu.SemaphoreType.DMA((8,)),
        ],
        compiler_params=params,
        name="begin",
    )(*(pltpu.with_memory_space_constraint(x, pltpu.HBM) for x in (v, config, offsets, targets, xi, strain, motion, visc)))

    con, xa, xb, ya, yb = pl.pallas_call(
        functools.partial(local, dims, axes),
        out_shape=(shape(2 * comps * nodes, cells, dtype=BF16), face_x, face_x, face_y, face_y),
        in_specs=[vmem] * 3,
        out_specs=(vmem,) * 5,
        scratch_shapes=[pltpu.VMEM((blocks * comps * nodes, cz), F32)],
        compiler_params=params,
        cost_estimate=estimate(comps * cells),
        name="local",
    )(parted, offsets, config)

    if fast:
        got_s = swap(talk, "solid", 0)
        got_xa = swap(xa, "dx", 0)
        got_xb = flip(xb, "dx", 3)
        mine = (iota((24, 128), 1) >= 64) == (lax.axis_index("solid") == 1)
        pair = jnp.where(mine, talk[:24], got_s[:24])
        got_3 = flip(jnp.concatenate([pair, yb, pair[:8]], axis=0), "dy", 3)
        got_2 = flip(jnp.concatenate([pair, yb[:8]], axis=0), "dy", 2)
        got_1 = flip(jnp.concatenate([pair, ya], axis=0), "dy", 1)
        parts = [got_3, got_2, got_1, pair]
        got_ya, got_yb = got_1, got_3
        got_za, got_zb = got_s, got_s
    else:
        got_xa, got_xb = swap(xa, "dx", 0), swap(xb, "dx", 1)
        got_ya, got_yb = swap(ya, "dy", 0), swap(yb, "dy", 1)
        got_za, got_zb = swap(talk, "solid", 0), swap(talk, "solid", 1)
        got_parts = lax.all_to_all(talk[:24, :slots], ("dy", "solid"), split_axis=1, concat_axis=1, tiled=True)
        parts = [jnp.concatenate([got_parts] * 2, axis=1)]

    total, hot = pl.pallas_call(
        functools.partial(middle, dims, axes, mesh_sizes, fast),
        out_shape=(shape(comps * nodes, cells), shape(cells, 2 * lanes, dtype=BF16)),
        in_specs=[vmem] * 10,
        out_specs=(vmem,) * 2,
        compiler_params=params,
        cost_estimate=estimate(comps * cells),
        name="middle",
    )(got_za, con, visc, offsets, matrix, config, got_xa, got_xb, got_zb, targets)

    rims = pl.pallas_call(
        functools.partial(rim, dims, axes, mesh_sizes, fast),
        out_shape=shape(comps * nodes, len(outer_blocks(cx, cy)) * cz),
        in_specs=[vmem] * 5,
        out_specs=vmem,
        compiler_params=params,
        cost_estimate=estimate(comps * cells),
        name="rim",
    )(total, got_yb, got_ya, matrix, config)

    out, deform = pl.pallas_call(
        functools.partial(after, dims, axes, fast),
        out_shape=(shape(*v.shape), shape(9, 1, slots)),
        in_specs=[vmem] * (5 + len(parts)),
        out_specs=(hbm, hbm),
        scratch_shapes=[
            pltpu.VMEM(v.shape, F32),
            pltpu.VMEM(strain.shape, F32),
            pltpu.SemaphoreType.DMA((comps + 1,)),
        ],
        compiler_params=params,
        name="after",
    )(total, *parts, rims, hot, weights, own)
    return out.reshape(velocity.shape), deform.reshape(strain_offsets.shape)


def solution(mesh):
    sizes = tuple(mesh.shape[a] for a in ("dx", "dy", "solid"))
    return jax.shard_map(
        functools.partial(shards, sizes),
        mesh=mesh,
        in_specs=(
            P(None, None, None, None, "dx", "dy", "solid"),
            P("dx", "dy", "solid"),
            P("dx", "dy", "solid"),
            P(),
            P("dx", ("dy", "solid"), None),
            P(None, "dx", ("dy", "solid"), None),
            P(None, None, "dx", ("dy", "solid"), None),
            P(None, "dx", ("dy", "solid"), None),
        ),
        out_specs=(
            P(None, None, None, None, "dx", "dy", "solid"),
            P(None, None, "dx", ("dy", "solid"), None),
        ),
        check_vma=False,
    )
```

```python
import functools

import jax
import jax.numpy as jnp
from jax import lax
from jax.experimental import pallas as pl
from jax.experimental.pallas import tpu as pltpu
from jax.sharding import PartitionSpec as P

TIME_STEP = 0.05
SPRING_RATE = 2.0
PENALTY = 4.0
NODE_POINTS = (0.0, 1.0 / 3.0, 2.0 / 3.0, 1.0)
F32, BF16 = jnp.float32, jnp.bfloat16
VMEM_LIMIT = 24 * 1024 * 1024


def iota(shape, dim):
    return lax.broadcasted_iota(jnp.int32, shape, dim)


def split(x):
    high = x.astype(BF16)
    low = (x - high.astype(F32)).astype(BF16)
    return high, low


def dot(a, b, dims=((1,), (0,))):
    return lax.dot_general(a, b, (dims, ((), ())), preferred_element_type=F32)


def lagrange(coord):
    values = []
    slopes = []
    for which in range(4):
        others = [NODE_POINTS[j] for j in range(4) if j != which]
        denom = 1.0
        for other in others:
            denom = denom * (NODE_POINTS[which] - other)
        scale = 1.0 / denom
        first = coord - others[0]
        second = coord - others[1]
        third = coord - others[2]
        values.append(first * second * third * scale)
        slopes.append((second * third + first * third + first * second) * scale)
    return values, slopes


def spread_rows(parts, dim, lanes):
    wide = [jnp.broadcast_to(p, (8, lanes)) for p in parts]
    if dim == 0:
        return jnp.concatenate([wide[a] for a in (0, 0, 1, 1, 2, 2, 3, 3)], axis=0)
    row = iota((8, lanes), 0)
    if dim == 1:
        even = jnp.where(row < 4, wide[0], wide[1])
        odd = jnp.where(row < 4, wide[2], wide[3])
        return jnp.concatenate([even, odd] * 4, axis=0)
    c = row & 3
    block = jnp.where(c == 0, wide[0], jnp.where(c == 1, wide[1], jnp.where(c == 2, wide[2], wide[3])))
    return jnp.concatenate([block] * 8, axis=0)


def shapes_of(xi, lanes):
    out = []
    for dim in range(3):
        values, slopes = lagrange(xi[dim])
        out.append((spread_rows(values, dim, lanes), spread_rows(slopes, dim, lanes)))
    return out


def one_hot(slots, cells):
    lanes = slots.shape[1]
    return jnp.where(iota((cells, lanes), 0) == slots, 1.0, 0.0).astype(BF16)


def configured(product, config, nconf):
    rows = product.shape[0] // nconf
    chosen = product[:rows]
    for which in range(1, nconf):
        chosen = jnp.where(config == which, product[which * rows : (which + 1) * rows], chosen)
    return chosen


def tripled(high, low):
    return jnp.concatenate([high, low, high], axis=0)


def turned_parts(high, low):
    return jnp.concatenate([high, high, low], axis=0)


def constrain(matrix, columns, config_rows, store, nconf, comps, blocks, lanes):
    step = 2 if blocks % 2 == 0 else 1
    for k in range(comps):
        for first in range(0, blocks, step):
            values, parts = columns(k, range(first, first + step))
            product = dot(matrix, parts)
            for i in range(step):
                piece = product[:, i * lanes : (i + 1) * lanes]
                store(k, first + i, values[i] + configured(piece, config_rows[first + i], nconf))


def fetch(pairs, sems):
    copies = [pltpu.make_async_copy(src, dst, sems.at[i]) for i, (src, dst) in enumerate(pairs)]
    for copy in copies:
        copy.start()
    return copies


def plain_matrix(offsets):
    high, low = split(offsets)
    return jnp.concatenate([high, high, low], axis=1)


def turned_matrix(offsets, nconf, nodes):
    blocks = [offsets[w * nodes : (w + 1) * nodes, :] for w in range(nconf)]
    highs, lows = [], []
    for block in blocks:
        high = block.astype(BF16).astype(F32)
        both = jnp.concatenate([high, block - high], axis=0).T.astype(BF16)
        highs.append(both)
        lows.append(both[:, :nodes])
    return jnp.concatenate([jnp.concatenate(highs, axis=0), jnp.concatenate(lows, axis=0)], axis=1)


def begin(
    dims, axes, fast,
    v_hbm, config_hbm, offset_hbm, slot_hbm, xi_hbm, strain_hbm, motion_hbm, viscosity_hbm,
    talk_ref, own_ref, split_ref, matrix_ref, target_ref, weight_ref, config_ref, offset_ref, viscosity_ref,
    v_ref, slot_ref, xi_ref, strain_ref, motion_ref, sems,
):
    comps, nodes, cx, cy, cz, nconf, slots, lanes = dims
    blocks = cx * cy
    cells = blocks * cz
    copies = fetch(
        [(v_hbm, v_ref), (offset_hbm, offset_ref), (slot_hbm, slot_ref), (config_hbm, config_ref), (xi_hbm, xi_ref),
         (strain_hbm, strain_ref), (motion_hbm, motion_ref), (viscosity_hbm, viscosity_ref)],
        sems,
    )

    for copy in copies:
        copy.wait()
    targets = jnp.concatenate([slot_ref[...]] * 2, axis=1)
    target_ref[...] = targets
    wide = 2 * blocks
    columns = pl.cdiv(slots + wide, 128) * 128
    lane = iota((1, columns), 1)
    both = jnp.concatenate([slot_ref[...], jnp.full((1, columns - slots), -1, jnp.int32)], axis=1)
    for y in range(blocks):
        both = jnp.where(lane == columns - wide + y, y * cz, both)
        both = jnp.where(lane == columns - blocks + y, (y + 1) * cz - 1, both)
    hot = one_hot(both, cells)
    config = jnp.concatenate([config_ref[y : y + 1, :] for y in range(blocks)], axis=1)
    config = dot(jnp.broadcast_to(config.astype(F32), (16, cells)).astype(BF16), hot)[0:1, :]

    half = iota((1, lanes), 1) < slots

    def twice(x):
        if 2 * slots == columns:
            return jnp.where(iota(x.shape, 1) < slots, x, pltpu.roll(x, slots, axis=1))
        return jnp.concatenate([x[:, :slots]] * 2, axis=1)

    config_twice = twice(config)
    xi = [jnp.concatenate([xi_ref[j]] * 2, axis=1) for j in range(3)]
    (px, dx), (py, dy), (pz, dz) = shapes_of(xi, lanes)
    basis = (jnp.where(half, px, dx) * (py * pz), px * jnp.where(half, dy * pz, py * dz))
    matrix = turned_matrix(offset_ref[...], nconf, nodes)
    matrix_ref[...] = matrix
    raw = []
    for k in range(comps):
        row = 2 * k * nodes
        for y in range(blocks):
            high, low = split(v_ref[pl.ds(k * nodes * blocks + y, nodes, stride=blocks), :])
            at = slice(y * cz, (y + 1) * cz)
            split_ref[row : row + nodes, at] = high
            split_ref[row + nodes : row + 2 * nodes, at] = low
        both = dot(split_ref[row : row + 2 * nodes, :], hot)
        raw.append(both[:nodes] + both[nodes:])
    product = dot(matrix, jnp.concatenate([turned_parts(*split(p)) for p in basis], axis=1))
    weights = []
    for j in range(2):
        weights.append(basis[j] + configured(product[:, j * lanes : (j + 1) * lanes], config_twice, nconf))
        weight_ref[j * nodes : (j + 1) * nodes, :] = weights[j]

    for k in range(comps):
        value = twice(raw[k])
        for j in range(2):
            sums = jnp.sum(value * weights[j], axis=0, keepdims=True)
            other = pltpu.roll(sums, slots, axis=1)
            left, right = ((k, 3 + 3 * k), (4 + 3 * k, 5 + 3 * k))[j]
            own_ref[left : left + 1, :] = jnp.where(half, sums, other)
            own_ref[right : right + 1, :] = jnp.where(half, other, sums)
    for i in range(9):
        own_ref[12 + i : 13 + i, :] = jnp.concatenate([strain_ref[i]] * 2, axis=1)
    for i in range(3):
        own_ref[21 + i : 22 + i, :] = jnp.concatenate([motion_ref[i]] * 2, axis=1)

    count = comps * nodes // 24
    ends = jnp.concatenate([r[:, columns - 128 :] for r in raw], axis=0)
    lane = iota((24, 128), 1)
    last = own_ref[:, lanes - 128 :]
    for g in range(count):
        start = 128 - (count - g) * wide
        group = pltpu.roll(ends[24 * g : 24 * (g + 1)], (start + wide) % 128, axis=1)
        last = jnp.where(lane >= start, group, last)
    last = jnp.concatenate([last, jnp.broadcast_to(config[:, columns - 128 :], (8, 128))], axis=0)
    if fast:
        last = pltpu.roll(last, lax.axis_index(axes[2]) * slots, axis=1)
    else:
        talk_ref[0:24, :slots] = own_ref[:, :slots]
    talk_ref[:, talk_ref.shape[1] - 128 :] = last


def local(
    dims, axes,
    split_ref, offset_ref, config_ref,
    con_ref, xa_ref, xb_ref, ya_ref, yb_ref,
    field_ref,
):
    comps, nodes, cx, cy, cz, nconf, slots, lanes = dims
    blocks = cx * cy
    me_x, me_y = lax.axis_index(axes[0]), lax.axis_index(axes[1])
    even_x, even_y = me_x % 2 == 0, me_y % 2 == 0
    config_rows = [config_ref[y : y + 1, :] for y in range(blocks)]

    def columns(k, ys):
        at = slice(ys[0] * cz, (ys[-1] + 1) * cz)
        high = split_ref[2 * k * nodes : (2 * k + 1) * nodes, at]
        low = split_ref[(2 * k + 1) * nodes : (2 * k + 2) * nodes, at]
        value = high.astype(F32) + low.astype(F32)
        return [value[:, i * cz : (i + 1) * cz] for i in range(len(ys))], tripled(high, low)

    def store(k, y, value):
        field_ref[(y * comps + k) * nodes : (y * comps + k + 1) * nodes, :] = value
        part, rest = split(value)
        row = 2 * k * nodes
        con_ref[row : row + nodes, y * cz : (y + 1) * cz] = part
        con_ref[row + nodes : row + 2 * nodes, y * cz : (y + 1) * cz] = rest

    constrain(plain_matrix(offset_ref[...]), columns, config_rows, store, nconf, comps, blocks, cz)

    face = nodes // 4
    for k in range(comps):
        for y in range(cy):
            low_row = (y * comps + k) * nodes
            up_row = (((cx - 1) * cy + y) * comps + k + 1) * nodes
            lower = field_ref[low_row : low_row + face, :]
            upper = field_ref[up_row - face : up_row, :]
            cells = slice(y * cz, (y + 1) * cz)
            xa_ref[k * face : (k + 1) * face, cells] = jnp.where(even_x, upper, lower)
            xb_ref[k * face : (k + 1) * face, cells] = jnp.where(even_x, lower, upper)
        for a in range(4):
            into = k * face + a * 4
            for x in range(cx):
                first = (x * cy * comps + k) * nodes + a * face
                last = ((x * cy + cy - 1) * comps + k) * nodes + a * face
                lower = field_ref[first : first + 4, :]
                upper = field_ref[last + 12 : last + 16, :]
                ya_ref[into : into + 4, x * cz : (x + 1) * cz] = jnp.where(even_y, upper, lower)
                yb_ref[into : into + 4, x * cz : (x + 1) * cz] = jnp.where(even_y, lower, upper)


def solid(vel, grad, strain, motion):
    deform = [strain[3 * j + l] + (1.0 if j == l else 0.0) for j in range(3) for l in range(3)]
    moved = []
    for k in range(3):
        for l in range(3):
            change = sum(grad[3 * k + j] * deform[3 * j + l] for j in range(3))
            moved.append(deform[3 * k + l] + TIME_STEP * change)
    stress = [
        sum(moved[3 * k + l] * moved[3 * m + l] for l in range(3)) - (1.0 if k == m else 0.0)
        for k in range(3) for m in range(3)
    ]
    drag = [SPRING_RATE * (motion[k] - vel[k]) for k in range(3)]
    return moved, stress, drag


def node_tables():
    i, j = iota((64, 64), 0), iota((64, 64), 1)
    digits = [((i >> s) & 3, (j >> s) & 3) for s in (4, 2, 0)]
    same = [p == q for p, q in digits]
    lap = jnp.zeros((64, 64), F32)
    swaps = []
    for d in range(3):
        others = same[(d + 1) % 3] & same[(d + 2) % 3]
        p, q = digits[d]
        line = jnp.where(p == q, 2.0, jnp.where((p - q == 1) | (q - p == 1), -1.0, 0.0))
        lap = lap + jnp.where(others, line, 0.0)
        swaps.append(jnp.where(others & (((p == 0) & (q == 3)) | ((p == 3) & (q == 0))), 1.0, 0.0))
    return jnp.concatenate([lap, swaps[2], swaps[1]], axis=0).astype(BF16)


def sides(even, open_b, a, b):
    b = jnp.where(open_b, b, 0.0)
    return jnp.where(even, b, a), jnp.where(even, a, b)


def place(axis, n):
    index = lax.axis_index(axis)
    even = index % 2 == 0
    return even, jnp.where(even, index, n - 1 - index) > 0


def middle(
    dims, axes, sizes, fast,
    za_ref, con_ref, viscosity_ref, offset_ref, matrix_ref, config_ref, xa_ref, xb_ref, zb_ref, target_ref,
    total_ref, hot_ref,
):
    comps, nodes, cx, cy, cz, nconf, slots, lanes = dims
    blocks = cx * cy
    face = nodes // 4
    even_x, open_x = place(axes[0], sizes[0])
    even_z, open_z = place(axes[2], sizes[2])

    table = node_tables()
    table = jnp.concatenate([table, table], axis=1)
    row = iota((nodes, cz), 0)
    a, b, c = (row >> 4) & 3, (row >> 2) & 3, row & 3

    def ends(p):
        return jnp.where((p == 0) | (p == 3), PENALTY, 0.0)

    keep = 1.0 + ends(a) + ends(b) + ends(c)
    lane = iota((nodes, cz), 1)
    count = comps * nodes // 24
    wide = 2 * blocks
    plain = plain_matrix(offset_ref[...])
    hot_ref[...] = one_hot(jnp.concatenate([target_ref[...]] * 2, axis=1), blocks * cz)

    def ends_of(ref):
        last = ref[:, ref.shape[1] - 128 :]
        if fast:
            last = pltpu.roll(last, (lax.axis_index(axes[2]) + 1) % 2 * slots, axis=1)
        config = pltpu.roll(last[24:32], wide, axis=1)
        groups = [pltpu.roll(last[0:24], (count - g) * wide, axis=1) for g in range(count)]
        rows = jnp.concatenate(groups, axis=0)
        raw = rows[:nodes]
        spread_config = config[0:1]
        for k in range(1, comps):
            here = lane >= k * wide
            raw = jnp.where(here, pltpu.roll(rows[k * nodes : (k + 1) * nodes], k * wide, axis=1), raw)
            spread_config = jnp.where(here[0:1], pltpu.roll(config, k * wide, axis=1)[0:1], spread_config)
        raw = jnp.where(lane < comps * wide, raw, 0.0)
        return raw + configured(dot(plain, tripled(*split(raw))), spread_config, nconf)

    z_a = ends_of(za_ref)
    z_low, z_up = sides(even_z, open_z, z_a, z_a if fast else ends_of(zb_ref))
    z_low, z_up = pltpu.roll(z_low, nodes - 3, axis=0), pltpu.roll(z_up, 3, axis=0)
    config_rows = [config_ref[y : y + 1, :] for y in range(blocks)]
    matrix = matrix_ref[...]

    for k in range(comps):
        pair = con_ref[2 * k * nodes : 2 * (k + 1) * nodes, :]
        ops = dot(table, pair)
        rows = slice(k * face, (k + 1) * face)
        x_low, x_up = sides(even_x, open_x, xa_ref[rows, :], xb_ref[rows, :])
        values = []
        for y in range(blocks):
            x_at, y_at = y // cy, y % cy
            cells = slice(y * cz, (y + 1) * cz)
            value = pair[:nodes, cells].astype(F32) + pair[nodes:, cells].astype(F32)
            total = keep * value + viscosity_ref[y : y + 1, :] * ops[0:nodes, cells]
            moved_z = ops[nodes : 2 * nodes, cells]
            below = jnp.where(lane == 0, pltpu.roll(z_low, cz - k * wide - blocks - y, axis=1), pltpu.roll(moved_z, 1, axis=1))
            above = jnp.where(
                lane == cz - 1, pltpu.roll(z_up, cz - 1 - k * wide - y, axis=1), pltpu.roll(moved_z, cz - 1, axis=1)
            )
            near = jnp.where(c == 0, below, jnp.where(c == 3, above, 0.0))
            if y_at > 0:
                near = near + jnp.where(b == 0, ops[2 * nodes : 3 * nodes, (y - 1) * cz : y * cz], 0.0)
            if y_at < cy - 1:
                near = near + jnp.where(b == 3, ops[2 * nodes : 3 * nodes, (y + 1) * cz : (y + 2) * cz], 0.0)
            total = total - PENALTY * near
            plane = slice(y_at * cz, (y_at + 1) * cz)
            if x_at > 0:
                other = slice((y - cy) * cz, (y - cy + 1) * cz)
                below = pair[nodes - face : nodes, other].astype(F32) + pair[2 * nodes - face :, other].astype(F32)
            else:
                below = x_low[:, plane]
            if x_at < cx - 1:
                other = slice((y + cy) * cz, (y + cy + 1) * cz)
                above = pair[:face, other].astype(F32) + pair[nodes : nodes + face, other].astype(F32)
            else:
                above = x_up[:, plane]
            total = jnp.concatenate(
                [total[:face] - PENALTY * below, total[face : nodes - face], total[nodes - face :] - PENALTY * above],
                axis=0,
            )
            values.append(total)
        inner = [y for y in range(blocks) if 0 < y % cy < cy - 1]
        if inner:
            product = dot(matrix, turned_parts(*split(jnp.concatenate([values[y] for y in inner], axis=1))))
            for i, y in enumerate(inner):
                values[y] = values[y] + configured(product[:, i * cz : (i + 1) * cz], config_rows[y], nconf)
        for y in range(blocks):
            total_ref[k * nodes : (k + 1) * nodes, y * cz : (y + 1) * cz] = values[y]


def outer_blocks(cx, cy):
    return [y for y in range(cx * cy) if y % cy in (0, cy - 1)]


def widen(face, nodes):
    return jnp.concatenate([face[4 * (i // 4) : 4 * (i // 4) + 4] for i in range(nodes // 4)], axis=0)


def gather_parts(refs, axes):
    me_y, me_s = lax.axis_index(axes[1]), lax.axis_index(axes[2])
    me = me_y * 2 + me_s
    lane = iota((24, 128), 1) >> 3
    parts = jnp.zeros((24, 128), F32)
    for flip, ref in enumerate(refs):
        block = ref[0:24, :]
        for half in range(2):
            source = (me_y ^ flip) * 2 + half
            shift = (source - me) * 8 + (128 - 64 * half)
            parts = jnp.where(lane == source, pltpu.roll(block, shift & 127, axis=1), parts)
    return parts + pltpu.roll(parts, 64, axis=1)


def rim(
    dims, axes, sizes, fast,
    total_ref, yb_ref, ya_ref, matrix_ref, config_ref,
    rim_ref,
):
    comps, nodes, cx, cy, cz, nconf, slots, lanes = dims
    face = nodes // 4
    even_y, open_y = place(axes[1], sizes[1])
    first = 24 if fast else 0
    b = (iota((nodes, cz), 0) >> 2) & 3
    matrix = matrix_ref[...]
    for k in range(comps):
        rows = slice(first + k * face, first + (k + 1) * face)
        y_low, y_up = sides(even_y, open_y, ya_ref[rows, :], yb_ref[rows, :])
        outer = outer_blocks(cx, cy)
        values = []
        for y in outer:
            plane = slice(y // cy * cz, (y // cy + 1) * cz)
            value = total_ref[k * nodes : (k + 1) * nodes, y * cz : (y + 1) * cz]
            if y % cy == 0:
                value = value - jnp.where(b == 0, PENALTY * widen(y_low[:, plane], nodes), 0.0)
            if y % cy == cy - 1:
                value = value - jnp.where(b == 3, PENALTY * widen(y_up[:, plane], nodes), 0.0)
            values.append(value)
        product = dot(matrix, turned_parts(*split(jnp.concatenate(values, axis=1))))
        for i, y in enumerate(outer):
            at = slice(i * cz, (i + 1) * cz)
            rim_ref[k * nodes : (k + 1) * nodes, at] = values[i] + configured(product[:, at], config_ref[y : y + 1, :], nconf)


def after(
    dims, axes, fast,
    total_ref, *refs,
):
    comps, nodes, cx, cy, cz, nconf, slots, lanes = dims
    blocks = cx * cy
    if fast:
        got_3, got_2, got_1, pair_ref, *refs = refs
        part_refs = (pair_ref, got_1, got_2, got_3)
    else:
        *part_refs, refs = refs[0], refs[1:]
    rim_ref, hot_ref, weight_ref, own_ref, out_hbm, deform_hbm, out_ref, deform_ref, sems = refs

    parts = gather_parts(part_refs, axes) if fast else part_refs[0][...]
    own = [own_ref[i : i + 1, :] for i in range(24)]
    got = [parts[i : i + 1, :] for i in range(24)]
    _, stress, drag = solid(own[0:3], own[3:12], got[12:21], got[21:24])
    moved, _, _ = solid(got[0:3], got[3:12], own[12:21], own[21:24])
    for i in range(9):
        deform_ref[i] = moved[i][:, :slots]
    copies = [pltpu.make_async_copy(deform_ref, deform_hbm, sems.at[comps])]
    copies[0].start()
    hot = hot_ref[...]
    half = iota((1, lanes), 1) < slots
    highs, lows = [], []
    for k in range(comps):
        force = jnp.where(half, drag[k], -stress[3 * k]) * weight_ref[:nodes, :]
        force = force - jnp.where(half, stress[3 * k + 1], stress[3 * k + 2]) * weight_ref[nodes:, :]
        high, low = split(force)
        highs.append(high)
        lows.append(low)
    pieces = jnp.concatenate([jnp.concatenate(highs, axis=0), jnp.concatenate(lows, axis=0)], axis=1)
    spreads = dot(pieces, hot, ((1,), (1,)))

    outer = outer_blocks(cx, cy)
    for k in range(comps):
        rows = slice(k * nodes, (k + 1) * nodes)
        for y in range(blocks):
            cells = slice(y * cz, (y + 1) * cz)
            if y in outer:
                value = rim_ref[rows, outer.index(y) * cz : (outer.index(y) + 1) * cz]
            else:
                value = total_ref[rows, cells]
            out_ref[pl.ds(k * nodes * blocks + y, nodes, stride=blocks), :] = value - spreads[rows, cells]
        done = slice(k * nodes * blocks, (k + 1) * nodes * blocks)
        copies.append(pltpu.make_async_copy(out_ref.at[done, :], out_hbm.at[done, :], sems.at[k]))
        copies[-1].start()
    for copy in copies:
        copy.wait()


def swap(x, axis, stage):
    n = lax.axis_size(axis)
    pairs = [(i, i + 1) for i in range(stage, n - 1, 2)]
    if not pairs:
        return jnp.zeros_like(x)
    return lax.ppermute(x, axis, pairs + [(j, i) for i, j in pairs])


def flip(x, axis, bits):
    return lax.ppermute(x, axis, [(i, i ^ bits) for i in range(lax.axis_size(axis))])


def shards(
    mesh_sizes,
    velocity,
    viscosity,
    cell_config,
    constraint_offsets,
    slot_cells,
    point_coords,
    strain_offsets,
    solid_velocity,
):
    axes = ("dx", "dy", "solid")
    comps, cx, cy, cz = velocity.shape[0], *velocity.shape[4:]
    nodes = velocity.shape[1] * velocity.shape[2] * velocity.shape[3]
    blocks = cx * cy
    nconf = constraint_offsets.shape[0]
    slots = slot_cells.shape[-1]
    n_dx, n_dy, n_solid = mesh_sizes
    face_rows = comps * nodes // 4
    lanes = 2 * slots
    talk_lanes = lanes if comps * nodes // 24 * 2 * blocks <= slots == 64 else slots + 128
    dims = (comps, nodes, cx, cy, cz, nconf, slots, lanes)

    v = velocity.reshape(comps * nodes * blocks, cz)
    visc = viscosity.reshape(blocks, cz)
    config = cell_config.reshape(blocks, cz)
    offsets = constraint_offsets.reshape(nconf * nodes, nodes)
    targets = slot_cells.reshape(1, slots)
    xi = point_coords.reshape(3, 1, slots)
    strain = strain_offsets.reshape(9, 1, slots)
    motion = solid_velocity.reshape(3, 1, slots)

    vmem = pl.BlockSpec(memory_space=pltpu.VMEM)
    hbm = pl.BlockSpec(memory_space=pltpu.HBM)
    params = pltpu.CompilerParams(vmem_limit_bytes=VMEM_LIMIT)
    cells = blocks * cz
    face_y = jax.ShapeDtypeStruct((face_rows, cx * cz), F32)
    face_x = jax.ShapeDtypeStruct((face_rows, cy * cz), F32)
    def shape(*size, dtype=F32):
        return jax.ShapeDtypeStruct(size, dtype)

    def estimate(columns):
        return pl.CostEstimate(flops=2 * 6 * nconf * nodes * nodes * columns, bytes_accessed=1_000_000, transcendentals=0)

    fast = (n_dx, n_dy, n_solid, slots, talk_lanes) == (4, 4, 2, 64, 128)
    talk, own, parted, matrix, targets, weights, config, offsets, visc = pl.pallas_call(
        functools.partial(begin, dims, axes, fast),
        out_shape=(
            shape(32, talk_lanes),
            shape(24, lanes),
            shape(2 * comps * nodes, cells, dtype=BF16),
            shape(nconf * nodes, 3 * nodes, dtype=BF16),
            shape(1, lanes, dtype=targets.dtype),
            shape(2 * nodes, lanes),
            shape(*config.shape, dtype=config.dtype),
            shape(*offsets.shape),
            shape(*visc.shape),
        ),
        in_specs=[hbm] * 8,
        out_specs=(vmem,) * 9,
        scratch_shapes=[
            pltpu.VMEM(v.shape, F32),
            pltpu.VMEM(targets.shape, targets.dtype),
            pltpu.VMEM(xi.shape, F32),
            pltpu.VMEM(strain.shape, F32),
            pltpu.VMEM(motion.shape, F32),
            pltpu.SemaphoreType.DMA((8,)),
        ],
        compiler_params=params,
        name="begin",
    )(*(pltpu.with_memory_space_constraint(x, pltpu.HBM) for x in (v, config, offsets, targets, xi, strain, motion, visc)))

    con, xa, xb, ya, yb = pl.pallas_call(
        functools.partial(local, dims, axes),
        out_shape=(shape(2 * comps * nodes, cells, dtype=BF16), face_x, face_x, face_y, face_y),
        in_specs=[vmem] * 3,
        out_specs=(vmem,) * 5,
        scratch_shapes=[pltpu.VMEM((blocks * comps * nodes, cz), F32)],
        compiler_params=params,
        cost_estimate=estimate(comps * cells),
        name="local",
    )(parted, offsets, config)

    if fast:
        got_s = swap(talk, "solid", 0)
        got_xa = swap(xa, "dx", 0)
        got_xb = flip(xb, "dx", 3)
        mine = (iota((24, 128), 1) >= 64) == (lax.axis_index("solid") == 1)
        pair = jnp.where(mine, talk[:24], got_s[:24])
        got_3 = flip(jnp.concatenate([pair, yb], axis=0), "dy", 3)
        got_2 = flip(jnp.concatenate([pair, yb[:8]], axis=0), "dy", 2)
        got_1 = flip(jnp.concatenate([pair, ya], axis=0), "dy", 1)
        parts = [got_3, got_2, got_1, pair]
        got_ya, got_yb = got_1, got_3
        got_za, got_zb = got_s, got_s
    else:
        got_xa, got_xb = swap(xa, "dx", 0), swap(xb, "dx", 1)
        got_ya, got_yb = swap(ya, "dy", 0), swap(yb, "dy", 1)
        got_za, got_zb = swap(talk, "solid", 0), swap(talk, "solid", 1)
        got_parts = lax.all_to_all(talk[:24, :slots], ("dy", "solid"), split_axis=1, concat_axis=1, tiled=True)
        parts = [jnp.concatenate([got_parts] * 2, axis=1)]

    total, hot = pl.pallas_call(
        functools.partial(middle, dims, axes, mesh_sizes, fast),
        out_shape=(shape(comps * nodes, cells), shape(cells, 2 * lanes, dtype=BF16)),
        in_specs=[vmem] * 10,
        out_specs=(vmem,) * 2,
        compiler_params=params,
        cost_estimate=estimate(comps * cells),
        name="middle",
    )(got_za, con, visc, offsets, matrix, config, got_xa, got_xb, got_zb, targets)

    rims = pl.pallas_call(
        functools.partial(rim, dims, axes, mesh_sizes, fast),
        out_shape=shape(comps * nodes, len(outer_blocks(cx, cy)) * cz),
        in_specs=[vmem] * 5,
        out_specs=vmem,
        compiler_params=params,
        cost_estimate=estimate(comps * cells),
        name="rim",
    )(total, got_yb, got_ya, matrix, config)

    out, deform = pl.pallas_call(
        functools.partial(after, dims, axes, fast),
        out_shape=(shape(*v.shape), shape(9, 1, slots)),
        in_specs=[vmem] * (5 + len(parts)),
        out_specs=(hbm, hbm),
        scratch_shapes=[
            pltpu.VMEM(v.shape, F32),
            pltpu.VMEM(strain.shape, F32),
            pltpu.SemaphoreType.DMA((comps + 1,)),
        ],
        compiler_params=params,
        name="after",
    )(total, *parts, rims, hot, weights, own)
    return out.reshape(velocity.shape), deform.reshape(strain_offsets.shape)


def solution(mesh):
    sizes = tuple(mesh.shape[a] for a in ("dx", "dy", "solid"))
    return jax.shard_map(
        functools.partial(shards, sizes),
        mesh=mesh,
        in_specs=(
            P(None, None, None, None, "dx", "dy", "solid"),
            P("dx", "dy", "solid"),
            P("dx", "dy", "solid"),
            P(),
            P("dx", ("dy", "solid"), None),
            P(None, "dx", ("dy", "solid"), None),
            P(None, None, "dx", ("dy", "solid"), None),
            P(None, "dx", ("dy", "solid"), None),
        ),
        out_specs=(
            P(None, None, None, None, "dx", "dy", "solid"),
            P(None, None, "dx", ("dy", "solid"), None),
        ),
        check_vma=False,
    )
```

```python
import functools

import jax
import jax.numpy as jnp
from jax import lax
from jax.experimental import pallas as pl
from jax.experimental.pallas import tpu as pltpu
from jax.sharding import PartitionSpec as P

TIME_STEP = 0.05
SPRING_RATE = 2.0
PENALTY = 4.0
NODE_POINTS = (0.0, 1.0 / 3.0, 2.0 / 3.0, 1.0)
F32, BF16 = jnp.float32, jnp.bfloat16
VMEM_LIMIT = 24 * 1024 * 1024


def iota(shape, dim):
    return lax.broadcasted_iota(jnp.int32, shape, dim)


def split(x):
    high = x.astype(BF16)
    low = (x - high.astype(F32)).astype(BF16)
    return high, low


def dot(a, b, dims=((1,), (0,))):
    return lax.dot_general(a, b, (dims, ((), ())), preferred_element_type=F32)


def lagrange(coord):
    values = []
    slopes = []
    for which in range(4):
        others = [NODE_POINTS[j] for j in range(4) if j != which]
        denom = 1.0
        for other in others:
            denom = denom * (NODE_POINTS[which] - other)
        scale = 1.0 / denom
        first = coord - others[0]
        second = coord - others[1]
        third = coord - others[2]
        values.append(first * second * third * scale)
        slopes.append((second * third + first * third + first * second) * scale)
    return values, slopes


def spread_rows(parts, dim, lanes):
    wide = [jnp.broadcast_to(p, (8, lanes)) for p in parts]
    if dim == 0:
        return jnp.concatenate([wide[a] for a in (0, 0, 1, 1, 2, 2, 3, 3)], axis=0)
    row = iota((8, lanes), 0)
    if dim == 1:
        even = jnp.where(row < 4, wide[0], wide[1])
        odd = jnp.where(row < 4, wide[2], wide[3])
        return jnp.concatenate([even, odd] * 4, axis=0)
    c = row & 3
    block = jnp.where(c == 0, wide[0], jnp.where(c == 1, wide[1], jnp.where(c == 2, wide[2], wide[3])))
    return jnp.concatenate([block] * 8, axis=0)


def shapes_of(xi, lanes):
    out = []
    for dim in range(3):
        values, slopes = lagrange(xi[dim])
        out.append((spread_rows(values, dim, lanes), spread_rows(slopes, dim, lanes)))
    return out


def one_hot(slots, cells):
    lanes = slots.shape[1]
    return jnp.where(iota((cells, lanes), 0) == slots, 1.0, 0.0).astype(BF16)


def configured(product, config, nconf):
    rows = product.shape[0] // nconf
    chosen = product[:rows]
    for which in range(1, nconf):
        chosen = jnp.where(config == which, product[which * rows : (which + 1) * rows], chosen)
    return chosen


def tripled(high, low):
    return jnp.concatenate([high, low, high], axis=0)


def turned_parts(high, low):
    return jnp.concatenate([high, high, low], axis=0)


def constrain(matrix, columns, config_rows, store, nconf, comps, blocks, lanes):
    step = 2 if blocks % 2 == 0 else 1
    for k in range(comps):
        for first in range(0, blocks, step):
            values, parts = columns(k, range(first, first + step))
            product = dot(matrix, parts)
            for i in range(step):
                piece = product[:, i * lanes : (i + 1) * lanes]
                store(k, first + i, values[i] + configured(piece, config_rows[first + i], nconf))


def fetch(pairs, sems):
    copies = [pltpu.make_async_copy(src, dst, sems.at[i]) for i, (src, dst) in enumerate(pairs)]
    for copy in copies:
        copy.start()
    return copies


def plain_matrix(offsets):
    high, low = split(offsets)
    return jnp.concatenate([high, high, low], axis=1)


def turned_matrix(offsets, nconf, nodes):
    blocks = [offsets[w * nodes : (w + 1) * nodes, :] for w in range(nconf)]
    highs, lows = [], []
    for block in blocks:
        high = block.astype(BF16).astype(F32)
        both = jnp.concatenate([high, block - high], axis=0).T.astype(BF16)
        highs.append(both)
        lows.append(both[:, :nodes])
    return jnp.concatenate([jnp.concatenate(highs, axis=0), jnp.concatenate(lows, axis=0)], axis=1)


def begin(
    dims, axes, fast,
    v_hbm, config_hbm, offset_hbm, slot_hbm, xi_hbm, strain_hbm, motion_hbm, viscosity_hbm,
    talk_ref, self_ref, own_ref, split_ref, matrix_ref, target_ref, weight_ref, config_ref, offset_ref, viscosity_ref,
    v_ref, slot_ref, xi_ref, strain_ref, motion_ref, sems,
):
    comps, nodes, cx, cy, cz, nconf, slots, lanes = dims
    blocks = cx * cy
    cells = blocks * cz
    copies = fetch(
        [(v_hbm, v_ref), (offset_hbm, offset_ref), (slot_hbm, slot_ref), (config_hbm, config_ref), (xi_hbm, xi_ref),
         (strain_hbm, strain_ref), (motion_hbm, motion_ref), (viscosity_hbm, viscosity_ref)],
        sems,
    )

    for copy in copies:
        copy.wait()
    targets = jnp.concatenate([slot_ref[...]] * 2, axis=1)
    target_ref[...] = targets
    wide = 2 * blocks
    columns = pl.cdiv(slots + wide, 128) * 128
    lane = iota((1, columns), 1)
    both = jnp.concatenate([slot_ref[...], jnp.full((1, columns - slots), -1, jnp.int32)], axis=1)
    for y in range(blocks):
        both = jnp.where(lane == columns - wide + y, y * cz, both)
        both = jnp.where(lane == columns - blocks + y, (y + 1) * cz - 1, both)
    hot = one_hot(both, cells)
    config = jnp.concatenate([config_ref[y : y + 1, :] for y in range(blocks)], axis=1)
    config = dot(jnp.broadcast_to(config.astype(F32), (16, cells)).astype(BF16), hot)[0:1, :]

    half = iota((1, lanes), 1) < slots

    def twice(x):
        if 2 * slots == columns:
            return jnp.where(iota(x.shape, 1) < slots, x, pltpu.roll(x, slots, axis=1))
        return jnp.concatenate([x[:, :slots]] * 2, axis=1)

    config_twice = twice(config)
    xi = [jnp.concatenate([xi_ref[j]] * 2, axis=1) for j in range(3)]
    (px, dx), (py, dy), (pz, dz) = shapes_of(xi, lanes)
    basis = (jnp.where(half, px, dx) * (py * pz), px * jnp.where(half, dy * pz, py * dz))
    matrix = turned_matrix(offset_ref[...], nconf, nodes)
    matrix_ref[...] = matrix
    raw = []
    for k in range(comps):
        row = 2 * k * nodes
        for y in range(blocks):
            high, low = split(v_ref[pl.ds(k * nodes * blocks + y, nodes, stride=blocks), :])
            at = slice(y * cz, (y + 1) * cz)
            split_ref[row : row + nodes, at] = high
            split_ref[row + nodes : row + 2 * nodes, at] = low
        both = dot(split_ref[row : row + 2 * nodes, :], hot)
        raw.append(both[:nodes] + both[nodes:])
    product = dot(matrix, jnp.concatenate([turned_parts(*split(p)) for p in basis], axis=1))
    weights = []
    for j in range(2):
        weights.append(basis[j] + configured(product[:, j * lanes : (j + 1) * lanes], config_twice, nconf))
        weight_ref[j * nodes : (j + 1) * nodes, :] = weights[j]

    for k in range(comps):
        value = twice(raw[k])
        for j in range(2):
            sums = jnp.sum(value * weights[j], axis=0, keepdims=True)
            other = pltpu.roll(sums, slots, axis=1)
            left, right = ((k, 3 + 3 * k), (4 + 3 * k, 5 + 3 * k))[j]
            own_ref[left : left + 1, :] = jnp.where(half, sums, other)
            own_ref[right : right + 1, :] = jnp.where(half, other, sums)
    for i in range(9):
        own_ref[16 + i : 17 + i, :] = jnp.concatenate([strain_ref[i]] * 2, axis=1)
    for i in range(3):
        own_ref[25 + i : 26 + i, :] = jnp.concatenate([motion_ref[i]] * 2, axis=1)
    for i in (12, 28):
        own_ref[i : i + 4, :] = jnp.zeros((4, lanes), F32)

    count = comps * nodes // 16
    ends = jnp.concatenate([r[:, columns - 128 :] for r in raw], axis=0)
    lane = iota((16, 128), 1)
    at_end = 128 - wide
    packed = jnp.broadcast_to(pltpu.roll(config[:, columns - 128 :], (count * wide - at_end) % 128, axis=1), (16, 128))
    for g in range(count):
        group = pltpu.roll(ends[16 * g : 16 * (g + 1)], (g * wide - at_end) % 128, axis=1)
        packed = jnp.where((lane >= g * wide) & (lane < (g + 1) * wide), group, packed)
    talk_ref[talk_ref.shape[0] - 16 :, :] = packed
    if fast:
        parts = jnp.where(lane < slots, own_ref[0:16, :], own_ref[16:32, :])
        self_ref[...] = parts
        talk_ref[0:16, :] = jnp.where(lane & 8 == 0, pltpu.roll(parts, 120, axis=1), pltpu.roll(parts, 8, axis=1))
    else:
        self_ref[...] = jnp.zeros_like(self_ref)


def local(
    dims, axes,
    split_ref, offset_ref, config_ref,
    con_ref, xa_ref, xb_ref, ya_ref, yb_ref,
    field_ref,
):
    comps, nodes, cx, cy, cz, nconf, slots, lanes = dims
    blocks = cx * cy
    me_x, me_y = lax.axis_index(axes[0]), lax.axis_index(axes[1])
    even_x, even_y = me_x % 2 == 0, me_y % 2 == 0
    config_rows = [config_ref[y : y + 1, :] for y in range(blocks)]

    def columns(k, ys):
        at = slice(ys[0] * cz, (ys[-1] + 1) * cz)
        high = split_ref[2 * k * nodes : (2 * k + 1) * nodes, at]
        low = split_ref[(2 * k + 1) * nodes : (2 * k + 2) * nodes, at]
        value = high.astype(F32) + low.astype(F32)
        return [value[:, i * cz : (i + 1) * cz] for i in range(len(ys))], tripled(high, low)

    def store(k, y, value):
        field_ref[(y * comps + k) * nodes : (y * comps + k + 1) * nodes, :] = value
        part, rest = split(value)
        row = 2 * k * nodes
        con_ref[row : row + nodes, y * cz : (y + 1) * cz] = part
        con_ref[row + nodes : row + 2 * nodes, y * cz : (y + 1) * cz] = rest

    constrain(plain_matrix(offset_ref[...]), columns, config_rows, store, nconf, comps, blocks, cz)

    face = nodes // 4
    for k in range(comps):
        for y in range(cy):
            low_row = (y * comps + k) * nodes
            up_row = (((cx - 1) * cy + y) * comps + k + 1) * nodes
            lower = field_ref[low_row : low_row + face, :]
            upper = field_ref[up_row - face : up_row, :]
            cells = slice(y * cz, (y + 1) * cz)
            xa_ref[k * face : (k + 1) * face, cells] = jnp.where(even_x, upper, lower)
            xb_ref[k * face : (k + 1) * face, cells] = jnp.where(even_x, lower, upper)
        for a in range(4):
            into = k * face + a * 4
            for x in range(cx):
                first = (x * cy * comps + k) * nodes + a * face
                last = ((x * cy + cy - 1) * comps + k) * nodes + a * face
                lower = field_ref[first : first + 4, :]
                upper = field_ref[last + 12 : last + 16, :]
                ya_ref[into : into + 4, x * cz : (x + 1) * cz] = jnp.where(even_y, upper, lower)
                yb_ref[into : into + 4, x * cz : (x + 1) * cz] = jnp.where(even_y, lower, upper)


def solid(vel, grad, strain, motion):
    deform = [strain[3 * j + l] + (1.0 if j == l else 0.0) for j in range(3) for l in range(3)]
    moved = []
    for k in range(3):
        for l in range(3):
            change = sum(grad[3 * k + j] * deform[3 * j + l] for j in range(3))
            moved.append(deform[3 * k + l] + TIME_STEP * change)
    stress = [
        sum(moved[3 * k + l] * moved[3 * m + l] for l in range(3)) - (1.0 if k == m else 0.0)
        for k in range(3) for m in range(3)
    ]
    drag = [SPRING_RATE * (motion[k] - vel[k]) for k in range(3)]
    return moved, stress, drag


def node_tables():
    i, j = iota((64, 64), 0), iota((64, 64), 1)
    digits = [((i >> s) & 3, (j >> s) & 3) for s in (4, 2, 0)]
    same = [p == q for p, q in digits]
    lap = jnp.zeros((64, 64), F32)
    swaps = []
    for d in range(3):
        others = same[(d + 1) % 3] & same[(d + 2) % 3]
        p, q = digits[d]
        line = jnp.where(p == q, 2.0, jnp.where((p - q == 1) | (q - p == 1), -1.0, 0.0))
        lap = lap + jnp.where(others, line, 0.0)
        swaps.append(jnp.where(others & (((p == 0) & (q == 3)) | ((p == 3) & (q == 0))), 1.0, 0.0))
    return jnp.concatenate([lap, swaps[2], swaps[1]], axis=0).astype(BF16)


def sides(even, open_b, a, b):
    b = jnp.where(open_b, b, 0.0)
    return jnp.where(even, b, a), jnp.where(even, a, b)


def place(axis, n):
    index = lax.axis_index(axis)
    even = index % 2 == 0
    return even, jnp.where(even, index, n - 1 - index) > 0


def middle(
    dims, axes, sizes, fast,
    za_ref, con_ref, viscosity_ref, offset_ref, matrix_ref, config_ref, xa_ref, xb_ref, zb_ref, target_ref,
    total_ref, hot_ref,
):
    comps, nodes, cx, cy, cz, nconf, slots, lanes = dims
    blocks = cx * cy
    face = nodes // 4
    even_x, open_x = place(axes[0], sizes[0])
    even_z, open_z = place(axes[2], sizes[2])

    table = node_tables()
    table = jnp.concatenate([table, table], axis=1)
    row = iota((nodes, cz), 0)
    a, b, c = (row >> 4) & 3, (row >> 2) & 3, row & 3

    def ends(p):
        return jnp.where((p == 0) | (p == 3), PENALTY, 0.0)

    keep = 1.0 + ends(a) + ends(b) + ends(c)
    lane = iota((nodes, cz), 1)
    count = comps * nodes // 16
    wide = 2 * blocks
    plain = plain_matrix(offset_ref[...])
    hot_ref[...] = one_hot(jnp.concatenate([target_ref[...]] * 2, axis=1), blocks * cz)

    def ends_of(ref):
        packed = ref[ref.shape[0] - 16 :, :]
        config = pltpu.roll(packed, (128 - count * wide) % 128, axis=1)
        groups = [pltpu.roll(packed, (128 - g * wide) % 128, axis=1) for g in range(count)]
        rows = jnp.concatenate(groups, axis=0)
        raw = rows[:nodes]
        spread_config = config[0:1]
        for k in range(1, comps):
            here = lane >= k * wide
            raw = jnp.where(here, pltpu.roll(rows[k * nodes : (k + 1) * nodes], k * wide, axis=1), raw)
            spread_config = jnp.where(here[0:1], pltpu.roll(config, k * wide, axis=1)[0:1], spread_config)
        raw = jnp.where(lane < comps * wide, raw, 0.0)
        return raw + configured(dot(plain, tripled(*split(raw))), spread_config, nconf)

    z_a = ends_of(za_ref)
    z_low, z_up = sides(even_z, open_z, z_a, z_a if fast else ends_of(zb_ref))
    z_low, z_up = pltpu.roll(z_low, nodes - 3, axis=0), pltpu.roll(z_up, 3, axis=0)
    config_rows = [config_ref[y : y + 1, :] for y in range(blocks)]
    matrix = matrix_ref[...]

    for k in range(comps):
        pair = con_ref[2 * k * nodes : 2 * (k + 1) * nodes, :]
        ops = dot(table, pair)
        rows = slice(k * face, (k + 1) * face)
        x_low, x_up = sides(even_x, open_x, xa_ref[rows, :], xb_ref[rows, :])
        values = []
        for y in range(blocks):
            x_at, y_at = y // cy, y % cy
            cells = slice(y * cz, (y + 1) * cz)
            value = pair[:nodes, cells].astype(F32) + pair[nodes:, cells].astype(F32)
            total = keep * value + viscosity_ref[y : y + 1, :] * ops[0:nodes, cells]
            moved_z = ops[nodes : 2 * nodes, cells]
            below = jnp.where(lane == 0, pltpu.roll(z_low, cz - k * wide - blocks - y, axis=1), pltpu.roll(moved_z, 1, axis=1))
            above = jnp.where(
                lane == cz - 1, pltpu.roll(z_up, cz - 1 - k * wide - y, axis=1), pltpu.roll(moved_z, cz - 1, axis=1)
            )
            near = jnp.where(c == 0, below, jnp.where(c == 3, above, 0.0))
            if y_at > 0:
                near = near + jnp.where(b == 0, ops[2 * nodes : 3 * nodes, (y - 1) * cz : y * cz], 0.0)
            if y_at < cy - 1:
                near = near + jnp.where(b == 3, ops[2 * nodes : 3 * nodes, (y + 1) * cz : (y + 2) * cz], 0.0)
            total = total - PENALTY * near
            plane = slice(y_at * cz, (y_at + 1) * cz)
            if x_at > 0:
                other = slice((y - cy) * cz, (y - cy + 1) * cz)
                below = pair[nodes - face : nodes, other].astype(F32) + pair[2 * nodes - face :, other].astype(F32)
            else:
                below = x_low[:, plane]
            if x_at < cx - 1:
                other = slice((y + cy) * cz, (y + cy + 1) * cz)
                above = pair[:face, other].astype(F32) + pair[nodes : nodes + face, other].astype(F32)
            else:
                above = x_up[:, plane]
            total = jnp.concatenate(
                [total[:face] - PENALTY * below, total[face : nodes - face], total[nodes - face :] - PENALTY * above],
                axis=0,
            )
            values.append(total)
        inner = [y for y in range(blocks) if 0 < y % cy < cy - 1]
        if inner:
            product = dot(matrix, turned_parts(*split(jnp.concatenate([values[y] for y in inner], axis=1))))
            for i, y in enumerate(inner):
                values[y] = values[y] + configured(product[:, i * cz : (i + 1) * cz], config_rows[y], nconf)
        for y in range(blocks):
            total_ref[k * nodes : (k + 1) * nodes, y * cz : (y + 1) * cz] = values[y]


def outer_blocks(cx, cy):
    return [y for y in range(cx * cy) if y % cy in (0, cy - 1)]


def widen(face, nodes):
    return jnp.concatenate([face[4 * (i // 4) : 4 * (i // 4) + 4] for i in range(nodes // 4)], axis=0)


def gather_parts(refs, axes):
    me_y, me_s = lax.axis_index(axes[1]), lax.axis_index(axes[2])
    lane = iota((16, 128), 1)
    parts = jnp.zeros((16, 128), F32)
    for bits, ref in enumerate(refs):
        block = ref[0:16, :]
        for side in range(2):
            place = me_y * 2 + (me_s ^ side)
            source = (me_y ^ bits) * 2 + (me_s ^ side)
            moved = pltpu.roll(block, ((source - place) * 8) & 127, axis=1)
            parts = jnp.where((lane & 63) >> 3 == source, moved, parts)
    other = pltpu.roll(parts, 64, axis=1)
    return jnp.concatenate([jnp.where(lane < 64, parts, other), jnp.where(lane < 64, other, parts)], axis=0)


def rim(
    dims, axes, sizes, fast,
    total_ref, yb_ref, ya_ref, matrix_ref, config_ref,
    rim_ref,
):
    comps, nodes, cx, cy, cz, nconf, slots, lanes = dims
    face = nodes // 4
    even_y, open_y = place(axes[1], sizes[1])
    first = 16 if fast else 0
    b = (iota((nodes, cz), 0) >> 2) & 3
    matrix = matrix_ref[...]
    for k in range(comps):
        rows = slice(first + k * face, first + (k + 1) * face)
        y_low, y_up = sides(even_y, open_y, ya_ref[rows, :], yb_ref[rows, :])
        outer = outer_blocks(cx, cy)
        values = []
        for y in outer:
            plane = slice(y // cy * cz, (y // cy + 1) * cz)
            value = total_ref[k * nodes : (k + 1) * nodes, y * cz : (y + 1) * cz]
            if y % cy == 0:
                value = value - jnp.where(b == 0, PENALTY * widen(y_low[:, plane], nodes), 0.0)
            if y % cy == cy - 1:
                value = value - jnp.where(b == 3, PENALTY * widen(y_up[:, plane], nodes), 0.0)
            values.append(value)
        product = dot(matrix, turned_parts(*split(jnp.concatenate(values, axis=1))))
        for i, y in enumerate(outer):
            at = slice(i * cz, (i + 1) * cz)
            rim_ref[k * nodes : (k + 1) * nodes, at] = values[i] + configured(product[:, at], config_ref[y : y + 1, :], nconf)


def after(
    dims, axes, fast,
    total_ref, *refs,
):
    comps, nodes, cx, cy, cz, nconf, slots, lanes = dims
    blocks = cx * cy
    if fast:
        got_3, got_2, got_1, pair_ref, *refs = refs
        part_refs = (pair_ref, got_1, got_2, got_3)
    else:
        *part_refs, refs = refs[0], refs[1:]
    rim_ref, hot_ref, weight_ref, own_ref, out_hbm, deform_hbm, out_ref, deform_ref, sems = refs

    parts = gather_parts(part_refs, axes) if fast else part_refs[0][...]
    own = [own_ref[i : i + 1, :] for i in range(32)]
    got = [parts[i : i + 1, :] for i in range(32)]
    _, stress, drag = solid(own[0:3], own[3:12], got[16:25], got[25:28])
    moved, _, _ = solid(got[0:3], got[3:12], own[16:25], own[25:28])
    for i in range(9):
        deform_ref[i] = moved[i][:, :slots]
    copies = [pltpu.make_async_copy(deform_ref, deform_hbm, sems.at[comps])]
    copies[0].start()
    hot = hot_ref[...]
    half = iota((1, lanes), 1) < slots
    highs, lows = [], []
    for k in range(comps):
        force = jnp.where(half, drag[k], -stress[3 * k]) * weight_ref[:nodes, :]
        force = force - jnp.where(half, stress[3 * k + 1], stress[3 * k + 2]) * weight_ref[nodes:, :]
        high, low = split(force)
        highs.append(high)
        lows.append(low)
    pieces = jnp.concatenate([jnp.concatenate(highs, axis=0), jnp.concatenate(lows, axis=0)], axis=1)
    spreads = dot(pieces, hot, ((1,), (1,)))

    outer = outer_blocks(cx, cy)
    for k in range(comps):
        rows = slice(k * nodes, (k + 1) * nodes)
        for y in range(blocks):
            cells = slice(y * cz, (y + 1) * cz)
            if y in outer:
                value = rim_ref[rows, outer.index(y) * cz : (outer.index(y) + 1) * cz]
            else:
                value = total_ref[rows, cells]
            out_ref[pl.ds(k * nodes * blocks + y, nodes, stride=blocks), :] = value - spreads[rows, cells]
        done = slice(k * nodes * blocks, (k + 1) * nodes * blocks)
        copies.append(pltpu.make_async_copy(out_ref.at[done, :], out_hbm.at[done, :], sems.at[k]))
        copies[-1].start()
    for copy in copies:
        copy.wait()


def swap(x, axis, stage):
    n = lax.axis_size(axis)
    pairs = [(i, i + 1) for i in range(stage, n - 1, 2)]
    if not pairs:
        return jnp.zeros_like(x)
    return lax.ppermute(x, axis, pairs + [(j, i) for i, j in pairs])


def flip(x, axis, bits):
    return lax.ppermute(x, axis, [(i, i ^ bits) for i in range(lax.axis_size(axis))])


def shards(
    mesh_sizes,
    velocity,
    viscosity,
    cell_config,
    constraint_offsets,
    slot_cells,
    point_coords,
    strain_offsets,
    solid_velocity,
):
    axes = ("dx", "dy", "solid")
    comps, cx, cy, cz = velocity.shape[0], *velocity.shape[4:]
    nodes = velocity.shape[1] * velocity.shape[2] * velocity.shape[3]
    blocks = cx * cy
    nconf = constraint_offsets.shape[0]
    slots = slot_cells.shape[-1]
    n_dx, n_dy, n_solid = mesh_sizes
    face_rows = comps * nodes // 4
    lanes = 2 * slots
    dims = (comps, nodes, cx, cy, cz, nconf, slots, lanes)

    v = velocity.reshape(comps * nodes * blocks, cz)
    visc = viscosity.reshape(blocks, cz)
    config = cell_config.reshape(blocks, cz)
    offsets = constraint_offsets.reshape(nconf * nodes, nodes)
    targets = slot_cells.reshape(1, slots)
    xi = point_coords.reshape(3, 1, slots)
    strain = strain_offsets.reshape(9, 1, slots)
    motion = solid_velocity.reshape(3, 1, slots)

    vmem = pl.BlockSpec(memory_space=pltpu.VMEM)
    hbm = pl.BlockSpec(memory_space=pltpu.HBM)
    params = pltpu.CompilerParams(vmem_limit_bytes=VMEM_LIMIT)
    cells = blocks * cz
    face_y = jax.ShapeDtypeStruct((face_rows, cx * cz), F32)
    face_x = jax.ShapeDtypeStruct((face_rows, cy * cz), F32)
    def shape(*size, dtype=F32):
        return jax.ShapeDtypeStruct(size, dtype)

    def estimate(columns):
        return pl.CostEstimate(flops=2 * 6 * nconf * nodes * nodes * columns, bytes_accessed=1_000_000, transcendentals=0)

    fast = (n_dx, n_dy, n_solid, slots) == (4, 4, 2, 64)
    talk, mine, own, parted, matrix, targets, weights, config, offsets, visc = pl.pallas_call(
        functools.partial(begin, dims, axes, fast),
        out_shape=(
            shape(32 if fast else 16, 128),
            shape(16, 128),
            shape(32, lanes),
            shape(2 * comps * nodes, cells, dtype=BF16),
            shape(nconf * nodes, 3 * nodes, dtype=BF16),
            shape(1, lanes, dtype=targets.dtype),
            shape(2 * nodes, lanes),
            shape(*config.shape, dtype=config.dtype),
            shape(*offsets.shape),
            shape(*visc.shape),
        ),
        in_specs=[hbm] * 8,
        out_specs=(vmem,) * 10,
        scratch_shapes=[
            pltpu.VMEM(v.shape, F32),
            pltpu.VMEM(targets.shape, targets.dtype),
            pltpu.VMEM(xi.shape, F32),
            pltpu.VMEM(strain.shape, F32),
            pltpu.VMEM(motion.shape, F32),
            pltpu.SemaphoreType.DMA((8,)),
        ],
        compiler_params=params,
        name="begin",
    )(*(pltpu.with_memory_space_constraint(x, pltpu.HBM) for x in (v, config, offsets, targets, xi, strain, motion, visc)))

    con, xa, xb, ya, yb = pl.pallas_call(
        functools.partial(local, dims, axes),
        out_shape=(shape(2 * comps * nodes, cells, dtype=BF16), face_x, face_x, face_y, face_y),
        in_specs=[vmem] * 3,
        out_specs=(vmem,) * 5,
        scratch_shapes=[pltpu.VMEM((blocks * comps * nodes, cz), F32)],
        compiler_params=params,
        cost_estimate=estimate(comps * cells),
        name="local",
    )(parted, offsets, config)

    if fast:
        got_s = swap(talk, "solid", 0)
        got_xa = swap(xa, "dx", 0)
        got_xb = flip(xb, "dx", 3)
        own_side = (iota((16, 128), 1) >> 3) & 1 == lax.axis_index("solid")
        pair = jnp.where(own_side, mine, got_s[:16])
        got_3 = flip(jnp.concatenate([pair, yb], axis=0), "dy", 3)
        got_2 = flip(jnp.concatenate([pair, yb[:8]], axis=0), "dy", 2)
        got_1 = flip(jnp.concatenate([pair, ya], axis=0), "dy", 1)
        parts = [got_3, got_2, got_1, pair]
        got_ya, got_yb = got_1, got_3
        got_za, got_zb = got_s, got_s
    else:
        got_xa, got_xb = swap(xa, "dx", 0), swap(xb, "dx", 1)
        got_ya, got_yb = swap(ya, "dy", 0), swap(yb, "dy", 1)
        got_za, got_zb = swap(talk, "solid", 0), swap(talk, "solid", 1)
        sent = jnp.concatenate([own[:12, :slots], own[16:28, :slots]], axis=0)
        got_parts = lax.all_to_all(sent, ("dy", "solid"), split_axis=1, concat_axis=1, tiled=True)
        got_parts = jnp.pad(got_parts.reshape(2, 12, slots), ((0, 0), (0, 4), (0, 0))).reshape(32, slots)
        parts = [jnp.concatenate([got_parts] * 2, axis=1)]

    total, hot = pl.pallas_call(
        functools.partial(middle, dims, axes, mesh_sizes, fast),
        out_shape=(shape(comps * nodes, cells), shape(cells, 2 * lanes, dtype=BF16)),
        in_specs=[vmem] * 10,
        out_specs=(vmem,) * 2,
        compiler_params=params,
        cost_estimate=estimate(comps * cells),
        name="middle",
    )(got_za, con, visc, offsets, matrix, config, got_xa, got_xb, got_zb, targets)

    rims = pl.pallas_call(
        functools.partial(rim, dims, axes, mesh_sizes, fast),
        out_shape=shape(comps * nodes, len(outer_blocks(cx, cy)) * cz),
        in_specs=[vmem] * 5,
        out_specs=vmem,
        compiler_params=params,
        cost_estimate=estimate(comps * cells),
        name="rim",
    )(total, got_yb, got_ya, matrix, config)

    out, deform = pl.pallas_call(
        functools.partial(after, dims, axes, fast),
        out_shape=(shape(*v.shape), shape(9, 1, slots)),
        in_specs=[vmem] * (5 + len(parts)),
        out_specs=(hbm, hbm),
        scratch_shapes=[
            pltpu.VMEM(v.shape, F32),
            pltpu.VMEM(strain.shape, F32),
            pltpu.SemaphoreType.DMA((comps + 1,)),
        ],
        compiler_params=params,
        name="after",
    )(total, *parts, rims, hot, weights, own)
    return out.reshape(velocity.shape), deform.reshape(strain_offsets.shape)


def solution(mesh):
    sizes = tuple(mesh.shape[a] for a in ("dx", "dy", "solid"))
    return jax.shard_map(
        functools.partial(shards, sizes),
        mesh=mesh,
        in_specs=(
            P(None, None, None, None, "dx", "dy", "solid"),
            P("dx", "dy", "solid"),
            P("dx", "dy", "solid"),
            P(),
            P("dx", ("dy", "solid"), None),
            P(None, "dx", ("dy", "solid"), None),
            P(None, None, "dx", ("dy", "solid"), None),
            P(None, "dx", ("dy", "solid"), None),
        ),
        out_specs=(
            P(None, None, None, None, "dx", "dy", "solid"),
            P(None, None, "dx", ("dy", "solid"), None),
        ),
        check_vma=False,
    )
```

```python
import functools

import jax
import jax.numpy as jnp
from jax import lax
from jax.experimental import pallas as pl
from jax.experimental.pallas import tpu as pltpu
from jax.sharding import PartitionSpec as P

TIME_STEP = 0.05
SPRING_RATE = 2.0
PENALTY = 4.0
NODE_POINTS = (0.0, 1.0 / 3.0, 2.0 / 3.0, 1.0)
F32, BF16 = jnp.float32, jnp.bfloat16
VMEM_LIMIT = 24 * 1024 * 1024


def iota(shape, dim):
    return lax.broadcasted_iota(jnp.int32, shape, dim)


def split(x):
    high = x.astype(BF16)
    low = (x - high.astype(F32)).astype(BF16)
    return high, low


def dot(a, b, dims=((1,), (0,))):
    return lax.dot_general(a, b, (dims, ((), ())), preferred_element_type=F32)


def lagrange(coord):
    values = []
    slopes = []
    for which in range(4):
        others = [NODE_POINTS[j] for j in range(4) if j != which]
        denom = 1.0
        for other in others:
            denom = denom * (NODE_POINTS[which] - other)
        scale = 1.0 / denom
        first = coord - others[0]
        second = coord - others[1]
        third = coord - others[2]
        values.append(first * second * third * scale)
        slopes.append((second * third + first * third + first * second) * scale)
    return values, slopes


def spread_rows(parts, dim, lanes):
    wide = [jnp.broadcast_to(p, (8, lanes)) for p in parts]
    if dim == 0:
        return jnp.concatenate([wide[a] for a in (0, 0, 1, 1, 2, 2, 3, 3)], axis=0)
    row = iota((8, lanes), 0)
    if dim == 1:
        even = jnp.where(row < 4, wide[0], wide[1])
        odd = jnp.where(row < 4, wide[2], wide[3])
        return jnp.concatenate([even, odd] * 4, axis=0)
    c = row & 3
    block = jnp.where(c == 0, wide[0], jnp.where(c == 1, wide[1], jnp.where(c == 2, wide[2], wide[3])))
    return jnp.concatenate([block] * 8, axis=0)


def shapes_of(xi, lanes):
    out = []
    for dim in range(3):
        values, slopes = lagrange(xi[dim])
        out.append((spread_rows(values, dim, lanes), spread_rows(slopes, dim, lanes)))
    return out


def one_hot(slots, cells):
    lanes = slots.shape[1]
    return jnp.where(iota((cells, lanes), 0) == slots, 1.0, 0.0).astype(BF16)


def configured(product, config, nconf):
    rows = product.shape[0] // nconf
    chosen = product[:rows]
    for which in range(1, nconf):
        chosen = jnp.where(config == which, product[which * rows : (which + 1) * rows], chosen)
    return chosen


def tripled(high, low):
    return jnp.concatenate([high, low, high], axis=0)


def turned_parts(high, low):
    return jnp.concatenate([high, high, low], axis=0)


def constrain(matrix, columns, config_rows, store, nconf, comps, blocks, lanes):
    step = 2 if blocks % 2 == 0 else 1
    for k in range(comps):
        for first in range(0, blocks, step):
            values, parts = columns(k, range(first, first + step))
            product = dot(matrix, parts)
            for i in range(step):
                piece = product[:, i * lanes : (i + 1) * lanes]
                store(k, first + i, values[i] + configured(piece, config_rows[first + i], nconf))


def fetch(pairs, sems):
    copies = [pltpu.make_async_copy(src, dst, sems.at[i]) for i, (src, dst) in enumerate(pairs)]
    for copy in copies:
        copy.start()
    return copies


def plain_matrix(offsets):
    high, low = split(offsets)
    return jnp.concatenate([high, high, low], axis=1)


def turned_matrix(offsets, nconf, nodes):
    blocks = [offsets[w * nodes : (w + 1) * nodes, :] for w in range(nconf)]
    highs, lows = [], []
    for block in blocks:
        high = block.astype(BF16).astype(F32)
        both = jnp.concatenate([high, block - high], axis=0).T.astype(BF16)
        highs.append(both)
        lows.append(both[:, :nodes])
    return jnp.concatenate([jnp.concatenate(highs, axis=0), jnp.concatenate(lows, axis=0)], axis=1)


def begin(
    dims, axes, fast,
    v_hbm, config_hbm, offset_hbm, slot_hbm, xi_hbm, strain_hbm, motion_hbm, viscosity_hbm,
    talk_ref, self_ref, own_ref, split_ref, matrix_ref, target_ref, weight_ref, config_ref, offset_ref, viscosity_ref,
    v_ref, slot_ref, xi_ref, strain_ref, motion_ref, sems,
):
    comps, nodes, cx, cy, cz, nconf, slots, lanes = dims
    blocks = cx * cy
    cells = blocks * cz
    copies = fetch(
        [(v_hbm, v_ref), (offset_hbm, offset_ref), (slot_hbm, slot_ref), (config_hbm, config_ref), (xi_hbm, xi_ref),
         (strain_hbm, strain_ref), (motion_hbm, motion_ref), (viscosity_hbm, viscosity_ref)],
        sems,
    )

    for copy in copies:
        copy.wait()
    targets = jnp.concatenate([slot_ref[...]] * 2, axis=1)
    target_ref[...] = targets
    wide = 2 * blocks
    columns = pl.cdiv(slots + wide, 128) * 128
    lane = iota((1, columns), 1)
    both = jnp.concatenate([slot_ref[...], jnp.full((1, columns - slots), -1, jnp.int32)], axis=1)
    for y in range(blocks):
        both = jnp.where(lane == columns - wide + y, y * cz, both)
        both = jnp.where(lane == columns - blocks + y, (y + 1) * cz - 1, both)
    hot = one_hot(both, cells)
    config = jnp.concatenate([config_ref[y : y + 1, :] for y in range(blocks)], axis=1)
    config = dot(jnp.broadcast_to(config.astype(F32), (16, cells)).astype(BF16), hot)[0:1, :]

    half = iota((1, lanes), 1) < slots

    def twice(x):
        if 2 * slots == columns:
            return jnp.where(iota(x.shape, 1) < slots, x, pltpu.roll(x, slots, axis=1))
        return jnp.concatenate([x[:, :slots]] * 2, axis=1)

    config_twice = twice(config)
    xi = [jnp.concatenate([xi_ref[j]] * 2, axis=1) for j in range(3)]
    (px, dx), (py, dy), (pz, dz) = shapes_of(xi, lanes)
    basis = (jnp.where(half, px, dx) * (py * pz), px * jnp.where(half, dy * pz, py * dz))
    matrix = turned_matrix(offset_ref[...], nconf, nodes)
    matrix_ref[...] = matrix
    raw = []
    for k in range(comps):
        row = 2 * k * nodes
        for y in range(blocks):
            high, low = split(v_ref[pl.ds(k * nodes * blocks + y, nodes, stride=blocks), :])
            at = slice(y * cz, (y + 1) * cz)
            split_ref[row : row + nodes, at] = high
            split_ref[row + nodes : row + 2 * nodes, at] = low
        both = dot(split_ref[row : row + 2 * nodes, :], hot)
        raw.append(both[:nodes] + both[nodes:])
    product = dot(matrix, jnp.concatenate([turned_parts(*split(p)) for p in basis], axis=1))
    weights = []
    for j in range(2):
        weights.append(basis[j] + configured(product[:, j * lanes : (j + 1) * lanes], config_twice, nconf))
        weight_ref[j * nodes : (j + 1) * nodes, :] = weights[j]

    for k in range(comps):
        value = twice(raw[k])
        for j in range(2):
            sums = jnp.sum(value * weights[j], axis=0, keepdims=True)
            other = pltpu.roll(sums, slots, axis=1)
            left, right = ((k, 3 + 3 * k), (4 + 3 * k, 5 + 3 * k))[j]
            own_ref[left : left + 1, :] = jnp.where(half, sums, other)
            own_ref[right : right + 1, :] = jnp.where(half, other, sums)
    for i in range(9):
        own_ref[16 + i : 17 + i, :] = jnp.concatenate([strain_ref[i]] * 2, axis=1)
    for i in range(3):
        own_ref[25 + i : 26 + i, :] = jnp.concatenate([motion_ref[i]] * 2, axis=1)
    for i in (12, 28):
        own_ref[i : i + 4, :] = jnp.zeros((4, lanes), F32)

    count = comps * nodes // 16
    ends = jnp.concatenate([r[:, columns - 128 :] for r in raw], axis=0)
    lane = iota((16, 128), 1)
    at_end = 128 - wide
    packed = jnp.broadcast_to(pltpu.roll(config[:, columns - 128 :], (count * wide - at_end) % 128, axis=1), (16, 128))
    for g in range(count):
        group = pltpu.roll(ends[16 * g : 16 * (g + 1)], (g * wide - at_end) % 128, axis=1)
        packed = jnp.where((lane >= g * wide) & (lane < (g + 1) * wide), group, packed)
    talk_ref[talk_ref.shape[0] - 16 :, :] = packed
    if fast:
        parts = jnp.where(lane < slots, own_ref[0:16, :], own_ref[16:32, :])
        self_ref[...] = parts
        talk_ref[0:16, :] = jnp.where(lane & 8 == 0, pltpu.roll(parts, 120, axis=1), pltpu.roll(parts, 8, axis=1))
    else:
        self_ref[...] = jnp.zeros_like(self_ref)


def local(
    dims, axes,
    split_ref, offset_ref, config_ref,
    con_ref, xa_ref, xb_ref, ya_ref, yb_ref,
    field_ref,
):
    comps, nodes, cx, cy, cz, nconf, slots, lanes = dims
    blocks = cx * cy
    me_x, me_y = lax.axis_index(axes[0]), lax.axis_index(axes[1])
    even_x, even_y = me_x % 2 == 0, me_y % 2 == 0
    config_rows = [config_ref[y : y + 1, :] for y in range(blocks)]

    def columns(k, ys):
        at = slice(ys[0] * cz, (ys[-1] + 1) * cz)
        high = split_ref[2 * k * nodes : (2 * k + 1) * nodes, at]
        low = split_ref[(2 * k + 1) * nodes : (2 * k + 2) * nodes, at]
        value = high.astype(F32) + low.astype(F32)
        return [value[:, i * cz : (i + 1) * cz] for i in range(len(ys))], tripled(high, low)

    def store(k, y, value):
        field_ref[(y * comps + k) * nodes : (y * comps + k + 1) * nodes, :] = value
        part, rest = split(value)
        row = 2 * k * nodes
        con_ref[row : row + nodes, y * cz : (y + 1) * cz] = part
        con_ref[row + nodes : row + 2 * nodes, y * cz : (y + 1) * cz] = rest

    constrain(plain_matrix(offset_ref[...]), columns, config_rows, store, nconf, comps, blocks, cz)

    face = nodes // 4
    for k in range(comps):
        for y in range(cy):
            low_row = (y * comps + k) * nodes
            up_row = (((cx - 1) * cy + y) * comps + k + 1) * nodes
            lower = field_ref[low_row : low_row + face, :]
            upper = field_ref[up_row - face : up_row, :]
            cells = slice(y * cz, (y + 1) * cz)
            xa_ref[k * face : (k + 1) * face, cells] = jnp.where(even_x, upper, lower)
            xb_ref[k * face : (k + 1) * face, cells] = jnp.where(even_x, lower, upper)
        for a in range(4):
            into = k * face + a * 4
            for x in range(cx):
                first = (x * cy * comps + k) * nodes + a * face
                last = ((x * cy + cy - 1) * comps + k) * nodes + a * face
                lower = field_ref[first : first + 4, :]
                upper = field_ref[last + 12 : last + 16, :]
                ya_ref[into : into + 4, x * cz : (x + 1) * cz] = jnp.where(even_y, upper, lower)
                yb_ref[into : into + 4, x * cz : (x + 1) * cz] = jnp.where(even_y, lower, upper)


def solid(vel, grad, strain, motion):
    deform = [strain[3 * j + l] + (1.0 if j == l else 0.0) for j in range(3) for l in range(3)]
    moved = []
    for k in range(3):
        for l in range(3):
            change = sum(grad[3 * k + j] * deform[3 * j + l] for j in range(3))
            moved.append(deform[3 * k + l] + TIME_STEP * change)
    stress = [
        sum(moved[3 * k + l] * moved[3 * m + l] for l in range(3)) - (1.0 if k == m else 0.0)
        for k in range(3) for m in range(3)
    ]
    drag = [SPRING_RATE * (motion[k] - vel[k]) for k in range(3)]
    return moved, stress, drag


def node_tables():
    i, j = iota((64, 64), 0), iota((64, 64), 1)
    digits = [((i >> s) & 3, (j >> s) & 3) for s in (4, 2, 0)]
    same = [p == q for p, q in digits]
    lap = jnp.zeros((64, 64), F32)
    swaps = []
    for d in range(3):
        others = same[(d + 1) % 3] & same[(d + 2) % 3]
        p, q = digits[d]
        line = jnp.where(p == q, 2.0, jnp.where((p - q == 1) | (q - p == 1), -1.0, 0.0))
        lap = lap + jnp.where(others, line, 0.0)
        swaps.append(jnp.where(others & (((p == 0) & (q == 3)) | ((p == 3) & (q == 0))), 1.0, 0.0))
    return jnp.concatenate([lap, swaps[2], swaps[1]], axis=0).astype(BF16)


def sides(even, open_b, a, b):
    b = jnp.where(open_b, b, 0.0)
    return jnp.where(even, b, a), jnp.where(even, a, b)


def place(axis, n):
    index = lax.axis_index(axis)
    even = index % 2 == 0
    return even, jnp.where(even, index, n - 1 - index) > 0


def middle(
    dims, axes, sizes, fast,
    za_ref, con_ref, viscosity_ref, offset_ref, matrix_ref, config_ref, xa_ref, xb_ref, zb_ref, target_ref,
    total_ref, hot_ref,
):
    comps, nodes, cx, cy, cz, nconf, slots, lanes = dims
    blocks = cx * cy
    face = nodes // 4
    even_x, open_x = place(axes[0], sizes[0])
    even_z, open_z = place(axes[2], sizes[2])

    table = node_tables()
    table = jnp.concatenate([table, table], axis=1)
    row = iota((nodes, cz), 0)
    a, b, c = (row >> 4) & 3, (row >> 2) & 3, row & 3

    def ends(p):
        return jnp.where((p == 0) | (p == 3), PENALTY, 0.0)

    keep = 1.0 + ends(a) + ends(b) + ends(c)
    lane = iota((nodes, cz), 1)
    count = comps * nodes // 16
    wide = 2 * blocks
    plain = plain_matrix(offset_ref[...])
    hot_ref[...] = one_hot(jnp.concatenate([target_ref[...]] * 2, axis=1), blocks * cz)

    def ends_of(ref):
        packed = ref[ref.shape[0] - 16 :, :]
        config = pltpu.roll(packed, (128 - count * wide) % 128, axis=1)
        groups = [pltpu.roll(packed, (128 - g * wide) % 128, axis=1) for g in range(count)]
        rows = jnp.concatenate(groups, axis=0)
        raw = rows[:nodes]
        spread_config = config[0:1]
        for k in range(1, comps):
            here = lane >= k * wide
            raw = jnp.where(here, pltpu.roll(rows[k * nodes : (k + 1) * nodes], k * wide, axis=1), raw)
            spread_config = jnp.where(here[0:1], pltpu.roll(config, k * wide, axis=1)[0:1], spread_config)
        raw = jnp.where(lane < comps * wide, raw, 0.0)
        return raw + configured(dot(plain, tripled(*split(raw))), spread_config, nconf)

    z_a = ends_of(za_ref)
    z_low, z_up = sides(even_z, open_z, z_a, z_a if fast else ends_of(zb_ref))
    z_low, z_up = pltpu.roll(z_low, nodes - 3, axis=0), pltpu.roll(z_up, 3, axis=0)
    config_rows = [config_ref[y : y + 1, :] for y in range(blocks)]
    matrix = matrix_ref[...]

    for k in range(comps):
        pair = con_ref[2 * k * nodes : 2 * (k + 1) * nodes, :]
        ops = dot(table, pair)
        rows = slice(k * face, (k + 1) * face)
        x_low, x_up = sides(even_x, open_x, xa_ref[rows, :], xb_ref[rows, :])
        values = []
        for y in range(blocks):
            x_at, y_at = y // cy, y % cy
            cells = slice(y * cz, (y + 1) * cz)
            value = pair[:nodes, cells].astype(F32) + pair[nodes:, cells].astype(F32)
            total = keep * value + viscosity_ref[y : y + 1, :] * ops[0:nodes, cells]
            moved_z = ops[nodes : 2 * nodes, cells]
            below = jnp.where(lane == 0, pltpu.roll(z_low, cz - k * wide - blocks - y, axis=1), pltpu.roll(moved_z, 1, axis=1))
            above = jnp.where(
                lane == cz - 1, pltpu.roll(z_up, cz - 1 - k * wide - y, axis=1), pltpu.roll(moved_z, cz - 1, axis=1)
            )
            near = jnp.where(c == 0, below, jnp.where(c == 3, above, 0.0))
            if y_at > 0:
                near = near + jnp.where(b == 0, ops[2 * nodes : 3 * nodes, (y - 1) * cz : y * cz], 0.0)
            if y_at < cy - 1:
                near = near + jnp.where(b == 3, ops[2 * nodes : 3 * nodes, (y + 1) * cz : (y + 2) * cz], 0.0)
            total = total - PENALTY * near
            plane = slice(y_at * cz, (y_at + 1) * cz)
            if x_at > 0:
                other = slice((y - cy) * cz, (y - cy + 1) * cz)
                below = pair[nodes - face : nodes, other].astype(F32) + pair[2 * nodes - face :, other].astype(F32)
            else:
                below = x_low[:, plane]
            if x_at < cx - 1:
                other = slice((y + cy) * cz, (y + cy + 1) * cz)
                above = pair[:face, other].astype(F32) + pair[nodes : nodes + face, other].astype(F32)
            else:
                above = x_up[:, plane]
            total = jnp.concatenate(
                [total[:face] - PENALTY * below, total[face : nodes - face], total[nodes - face :] - PENALTY * above],
                axis=0,
            )
            values.append(total)
        inner = [y for y in range(blocks) if 0 < y % cy < cy - 1]
        if inner:
            product = dot(matrix, turned_parts(*split(jnp.concatenate([values[y] for y in inner], axis=1))))
            for i, y in enumerate(inner):
                values[y] = values[y] + configured(product[:, i * cz : (i + 1) * cz], config_rows[y], nconf)
        for y in range(blocks):
            total_ref[k * nodes : (k + 1) * nodes, y * cz : (y + 1) * cz] = values[y]


def outer_blocks(cx, cy):
    return [y for y in range(cx * cy) if y % cy in (0, cy - 1)]


def widen(face, nodes):
    return jnp.concatenate([face[4 * (i // 4) : 4 * (i // 4) + 4] for i in range(nodes // 4)], axis=0)


def gather_parts(refs, axes):
    me_y, me_s = lax.axis_index(axes[1]), lax.axis_index(axes[2])
    lane = iota((16, 128), 1)
    parts = jnp.zeros((16, 128), F32)
    for bits, ref in enumerate(refs):
        block = ref[0:16, :]
        if bits == 2:
            block = jnp.concatenate([block[8:], block[:8]], axis=0)
        for side in range(2):
            place = me_y * 2 + (me_s ^ side)
            source = (me_y ^ bits) * 2 + (me_s ^ side)
            moved = pltpu.roll(block, ((source - place) * 8) & 127, axis=1)
            parts = jnp.where((lane & 63) >> 3 == source, moved, parts)
    other = pltpu.roll(parts, 64, axis=1)
    return jnp.concatenate([jnp.where(lane < 64, parts, other), jnp.where(lane < 64, other, parts)], axis=0)


def rim(
    dims, axes, sizes, fast,
    total_ref, yb_ref, ya_ref, matrix_ref, config_ref,
    rim_ref,
):
    comps, nodes, cx, cy, cz, nconf, slots, lanes = dims
    face = nodes // 4
    even_y, open_y = place(axes[1], sizes[1])
    first = 16 if fast else 0
    b = (iota((nodes, cz), 0) >> 2) & 3
    matrix = matrix_ref[...]
    for k in range(comps):
        rows = slice(first + k * face, first + (k + 1) * face)
        y_low, y_up = sides(even_y, open_y, ya_ref[rows, :], yb_ref[rows, :])
        outer = outer_blocks(cx, cy)
        values = []
        for y in outer:
            plane = slice(y // cy * cz, (y // cy + 1) * cz)
            value = total_ref[k * nodes : (k + 1) * nodes, y * cz : (y + 1) * cz]
            if y % cy == 0:
                value = value - jnp.where(b == 0, PENALTY * widen(y_low[:, plane], nodes), 0.0)
            if y % cy == cy - 1:
                value = value - jnp.where(b == 3, PENALTY * widen(y_up[:, plane], nodes), 0.0)
            values.append(value)
        product = dot(matrix, turned_parts(*split(jnp.concatenate(values, axis=1))))
        for i, y in enumerate(outer):
            at = slice(i * cz, (i + 1) * cz)
            rim_ref[k * nodes : (k + 1) * nodes, at] = values[i] + configured(product[:, at], config_ref[y : y + 1, :], nconf)


def after(
    dims, axes, fast,
    total_ref, *refs,
):
    comps, nodes, cx, cy, cz, nconf, slots, lanes = dims
    blocks = cx * cy
    if fast:
        got_3, got_2, got_1, pair_ref, *refs = refs
        part_refs = (pair_ref, got_1, got_2, got_3)
    else:
        *part_refs, refs = refs[0], refs[1:]
    rim_ref, hot_ref, weight_ref, own_ref, out_hbm, deform_hbm, out_ref, deform_ref, sems = refs

    parts = gather_parts(part_refs, axes) if fast else part_refs[0][...]
    own = [own_ref[i : i + 1, :] for i in range(32)]
    got = [parts[i : i + 1, :] for i in range(32)]
    _, stress, drag = solid(own[0:3], own[3:12], got[16:25], got[25:28])
    moved, _, _ = solid(got[0:3], got[3:12], own[16:25], own[25:28])
    for i in range(9):
        deform_ref[i] = moved[i][:, :slots]
    copies = [pltpu.make_async_copy(deform_ref, deform_hbm, sems.at[comps])]
    copies[0].start()
    hot = hot_ref[...]
    half = iota((1, lanes), 1) < slots
    highs, lows = [], []
    for k in range(comps):
        force = jnp.where(half, drag[k], -stress[3 * k]) * weight_ref[:nodes, :]
        force = force - jnp.where(half, stress[3 * k + 1], stress[3 * k + 2]) * weight_ref[nodes:, :]
        high, low = split(force)
        highs.append(high)
        lows.append(low)
    pieces = jnp.concatenate([jnp.concatenate(highs, axis=0), jnp.concatenate(lows, axis=0)], axis=1)
    spreads = dot(pieces, hot, ((1,), (1,)))

    outer = outer_blocks(cx, cy)
    for k in range(comps):
        rows = slice(k * nodes, (k + 1) * nodes)
        for y in range(blocks):
            cells = slice(y * cz, (y + 1) * cz)
            if y in outer:
                value = rim_ref[rows, outer.index(y) * cz : (outer.index(y) + 1) * cz]
            else:
                value = total_ref[rows, cells]
            out_ref[pl.ds(k * nodes * blocks + y, nodes, stride=blocks), :] = value - spreads[rows, cells]
        done = slice(k * nodes * blocks, (k + 1) * nodes * blocks)
        copies.append(pltpu.make_async_copy(out_ref.at[done, :], out_hbm.at[done, :], sems.at[k]))
        copies[-1].start()
    for copy in copies:
        copy.wait()


def swap(x, axis, stage):
    n = lax.axis_size(axis)
    pairs = [(i, i + 1) for i in range(stage, n - 1, 2)]
    if not pairs:
        return jnp.zeros_like(x)
    return lax.ppermute(x, axis, pairs + [(j, i) for i, j in pairs])


def flip(x, axis, bits):
    return lax.ppermute(x, axis, [(i, i ^ bits) for i in range(lax.axis_size(axis))])


def shards(
    mesh_sizes,
    velocity,
    viscosity,
    cell_config,
    constraint_offsets,
    slot_cells,
    point_coords,
    strain_offsets,
    solid_velocity,
):
    axes = ("dx", "dy", "solid")
    comps, cx, cy, cz = velocity.shape[0], *velocity.shape[4:]
    nodes = velocity.shape[1] * velocity.shape[2] * velocity.shape[3]
    blocks = cx * cy
    nconf = constraint_offsets.shape[0]
    slots = slot_cells.shape[-1]
    n_dx, n_dy, n_solid = mesh_sizes
    face_rows = comps * nodes // 4
    lanes = 2 * slots
    dims = (comps, nodes, cx, cy, cz, nconf, slots, lanes)

    v = velocity.reshape(comps * nodes * blocks, cz)
    visc = viscosity.reshape(blocks, cz)
    config = cell_config.reshape(blocks, cz)
    offsets = constraint_offsets.reshape(nconf * nodes, nodes)
    targets = slot_cells.reshape(1, slots)
    xi = point_coords.reshape(3, 1, slots)
    strain = strain_offsets.reshape(9, 1, slots)
    motion = solid_velocity.reshape(3, 1, slots)

    vmem = pl.BlockSpec(memory_space=pltpu.VMEM)
    hbm = pl.BlockSpec(memory_space=pltpu.HBM)
    params = pltpu.CompilerParams(vmem_limit_bytes=VMEM_LIMIT)
    cells = blocks * cz
    face_y = jax.ShapeDtypeStruct((face_rows, cx * cz), F32)
    face_x = jax.ShapeDtypeStruct((face_rows, cy * cz), F32)
    def shape(*size, dtype=F32):
        return jax.ShapeDtypeStruct(size, dtype)

    def estimate(columns):
        return pl.CostEstimate(flops=2 * 6 * nconf * nodes * nodes * columns, bytes_accessed=1_000_000, transcendentals=0)

    fast = (n_dx, n_dy, n_solid, slots) == (4, 4, 2, 64)
    talk, mine, own, parted, matrix, targets, weights, config, offsets, visc = pl.pallas_call(
        functools.partial(begin, dims, axes, fast),
        out_shape=(
            shape(32 if fast else 16, 128),
            shape(16, 128),
            shape(32, lanes),
            shape(2 * comps * nodes, cells, dtype=BF16),
            shape(nconf * nodes, 3 * nodes, dtype=BF16),
            shape(1, lanes, dtype=targets.dtype),
            shape(2 * nodes, lanes),
            shape(*config.shape, dtype=config.dtype),
            shape(*offsets.shape),
            shape(*visc.shape),
        ),
        in_specs=[hbm] * 8,
        out_specs=(vmem,) * 10,
        scratch_shapes=[
            pltpu.VMEM(v.shape, F32),
            pltpu.VMEM(targets.shape, targets.dtype),
            pltpu.VMEM(xi.shape, F32),
            pltpu.VMEM(strain.shape, F32),
            pltpu.VMEM(motion.shape, F32),
            pltpu.SemaphoreType.DMA((8,)),
        ],
        compiler_params=params,
        name="begin",
    )(*(pltpu.with_memory_space_constraint(x, pltpu.HBM) for x in (v, config, offsets, targets, xi, strain, motion, visc)))

    con, xa, xb, ya, yb = pl.pallas_call(
        functools.partial(local, dims, axes),
        out_shape=(shape(2 * comps * nodes, cells, dtype=BF16), face_x, face_x, face_y, face_y),
        in_specs=[vmem] * 3,
        out_specs=(vmem,) * 5,
        scratch_shapes=[pltpu.VMEM((blocks * comps * nodes, cz), F32)],
        compiler_params=params,
        cost_estimate=estimate(comps * cells),
        name="local",
    )(parted, offsets, config)

    if fast:
        got_s = swap(talk, "solid", 0)
        got_xa = swap(xa, "dx", 0)
        got_xb = flip(xb, "dx", 3)
        own_side = (iota((16, 128), 1) >> 3) & 1 == lax.axis_index("solid")
        pair = jnp.where(own_side, mine, got_s[:16])
        got_3 = flip(jnp.concatenate([pair, yb], axis=0), "dy", 3)
        got_2 = flip(jnp.concatenate([pair[8:], pair[:8]], axis=0), "dy", 2)
        got_1 = flip(jnp.concatenate([pair, ya], axis=0), "dy", 1)
        parts = [got_3, got_2, got_1, pair]
        got_ya, got_yb = got_1, got_3
        got_za, got_zb = got_s, got_s
    else:
        got_xa, got_xb = swap(xa, "dx", 0), swap(xb, "dx", 1)
        got_ya, got_yb = swap(ya, "dy", 0), swap(yb, "dy", 1)
        got_za, got_zb = swap(talk, "solid", 0), swap(talk, "solid", 1)
        sent = jnp.concatenate([own[:12, :slots], own[16:28, :slots]], axis=0)
        got_parts = lax.all_to_all(sent, ("dy", "solid"), split_axis=1, concat_axis=1, tiled=True)
        got_parts = jnp.pad(got_parts.reshape(2, 12, slots), ((0, 0), (0, 4), (0, 0))).reshape(32, slots)
        parts = [jnp.concatenate([got_parts] * 2, axis=1)]

    total, hot = pl.pallas_call(
        functools.partial(middle, dims, axes, mesh_sizes, fast),
        out_shape=(shape(comps * nodes, cells), shape(cells, 2 * lanes, dtype=BF16)),
        in_specs=[vmem] * 10,
        out_specs=(vmem,) * 2,
        compiler_params=params,
        cost_estimate=estimate(comps * cells),
        name="middle",
    )(got_za, con, visc, offsets, matrix, config, got_xa, got_xb, got_zb, targets)

    rims = pl.pallas_call(
        functools.partial(rim, dims, axes, mesh_sizes, fast),
        out_shape=shape(comps * nodes, len(outer_blocks(cx, cy)) * cz),
        in_specs=[vmem] * 5,
        out_specs=vmem,
        compiler_params=params,
        cost_estimate=estimate(comps * cells),
        name="rim",
    )(total, got_yb, got_ya, matrix, config)

    out, deform = pl.pallas_call(
        functools.partial(after, dims, axes, fast),
        out_shape=(shape(*v.shape), shape(9, 1, slots)),
        in_specs=[vmem] * (5 + len(parts)),
        out_specs=(hbm, hbm),
        scratch_shapes=[
            pltpu.VMEM(v.shape, F32),
            pltpu.VMEM(strain.shape, F32),
            pltpu.SemaphoreType.DMA((comps + 1,)),
        ],
        compiler_params=params,
        name="after",
    )(total, *parts, rims, hot, weights, own)
    return out.reshape(velocity.shape), deform.reshape(strain_offsets.shape)


def solution(mesh):
    sizes = tuple(mesh.shape[a] for a in ("dx", "dy", "solid"))
    return jax.shard_map(
        functools.partial(shards, sizes),
        mesh=mesh,
        in_specs=(
            P(None, None, None, None, "dx", "dy", "solid"),
            P("dx", "dy", "solid"),
            P("dx", "dy", "solid"),
            P(),
            P("dx", ("dy", "solid"), None),
            P(None, "dx", ("dy", "solid"), None),
            P(None, None, "dx", ("dy", "solid"), None),
            P(None, "dx", ("dy", "solid"), None),
        ),
        out_specs=(
            P(None, None, None, None, "dx", "dy", "solid"),
            P(None, None, "dx", ("dy", "solid"), None),
        ),
        check_vma=False,
    )
```

```python
import functools

import jax
import jax.numpy as jnp
from jax import lax
from jax.experimental import pallas as pl
from jax.experimental.pallas import tpu as pltpu
from jax.sharding import PartitionSpec as P

TIME_STEP = 0.05
SPRING_RATE = 2.0
PENALTY = 4.0
NODE_POINTS = (0.0, 1.0 / 3.0, 2.0 / 3.0, 1.0)
F32, BF16 = jnp.float32, jnp.bfloat16
VMEM_LIMIT = 24 * 1024 * 1024


def iota(shape, dim):
    return lax.broadcasted_iota(jnp.int32, shape, dim)


def split(x):
    high = x.astype(BF16)
    low = (x - high.astype(F32)).astype(BF16)
    return high, low


def dot(a, b, dims=((1,), (0,))):
    return lax.dot_general(a, b, (dims, ((), ())), preferred_element_type=F32)


def lagrange(coord):
    values = []
    slopes = []
    for which in range(4):
        others = [NODE_POINTS[j] for j in range(4) if j != which]
        denom = 1.0
        for other in others:
            denom = denom * (NODE_POINTS[which] - other)
        scale = 1.0 / denom
        first = coord - others[0]
        second = coord - others[1]
        third = coord - others[2]
        values.append(first * second * third * scale)
        slopes.append((second * third + first * third + first * second) * scale)
    return values, slopes


def spread_rows(parts, dim, lanes):
    wide = [jnp.broadcast_to(p, (8, lanes)) for p in parts]
    if dim == 0:
        return jnp.concatenate([wide[a] for a in (0, 0, 1, 1, 2, 2, 3, 3)], axis=0)
    row = iota((8, lanes), 0)
    if dim == 1:
        even = jnp.where(row < 4, wide[0], wide[1])
        odd = jnp.where(row < 4, wide[2], wide[3])
        return jnp.concatenate([even, odd] * 4, axis=0)
    c = row & 3
    block = jnp.where(c == 0, wide[0], jnp.where(c == 1, wide[1], jnp.where(c == 2, wide[2], wide[3])))
    return jnp.concatenate([block] * 8, axis=0)


def shapes_of(xi, lanes):
    out = []
    for dim in range(3):
        values, slopes = lagrange(xi[dim])
        out.append((spread_rows(values, dim, lanes), spread_rows(slopes, dim, lanes)))
    return out


def one_hot(slots, cells):
    lanes = slots.shape[1]
    return jnp.where(iota((cells, lanes), 0) == slots, 1.0, 0.0).astype(BF16)


def configured(product, config, nconf):
    rows = product.shape[0] // nconf
    chosen = product[:rows]
    for which in range(1, nconf):
        chosen = jnp.where(config == which, product[which * rows : (which + 1) * rows], chosen)
    return chosen


def tripled(high, low):
    return jnp.concatenate([high, low, high], axis=0)


def turned_parts(high, low):
    return jnp.concatenate([high, high, low], axis=0)


def constrain(matrix, columns, config_rows, store, nconf, comps, blocks, lanes):
    step = 2 if blocks % 2 == 0 else 1
    for k in range(comps):
        for first in range(0, blocks, step):
            values, parts = columns(k, range(first, first + step))
            product = dot(matrix, parts)
            for i in range(step):
                piece = product[:, i * lanes : (i + 1) * lanes]
                store(k, first + i, values[i] + configured(piece, config_rows[first + i], nconf))


def fetch(pairs, sems):
    copies = [pltpu.make_async_copy(src, dst, sems.at[i]) for i, (src, dst) in enumerate(pairs)]
    for copy in copies:
        copy.start()
    return copies


def plain_matrix(offsets):
    high, low = split(offsets)
    return jnp.concatenate([high, high, low], axis=1)


def turned_matrix(offsets, nconf, nodes):
    blocks = [offsets[w * nodes : (w + 1) * nodes, :] for w in range(nconf)]
    highs, lows = [], []
    for block in blocks:
        high = block.astype(BF16).astype(F32)
        both = jnp.concatenate([high, block - high], axis=0).T.astype(BF16)
        highs.append(both)
        lows.append(both[:, :nodes])
    return jnp.concatenate([jnp.concatenate(highs, axis=0), jnp.concatenate(lows, axis=0)], axis=1)


def begin(
    dims, axes, fast,
    v_hbm, config_hbm, offset_hbm, slot_hbm, xi_hbm, strain_hbm, motion_hbm, viscosity_hbm,
    talk_ref, self_ref, own_ref, split_ref, matrix_ref, target_ref, weight_ref, config_ref, offset_ref, viscosity_ref,
    v_ref, slot_ref, xi_ref, strain_ref, motion_ref, hot_ref, parts_ref, basis_ref, sems,
):
    comps, nodes, cx, cy, cz, nconf, slots, lanes = dims
    blocks = cx * cy
    cells = blocks * cz
    copies = fetch(
        [(slot_hbm, slot_ref), (config_hbm, config_ref), (xi_hbm, xi_ref), (v_hbm, v_ref), (offset_hbm, offset_ref),
         (strain_hbm, strain_ref), (motion_hbm, motion_ref), (viscosity_hbm, viscosity_ref)],
        sems,
    )

    for copy in copies[:3]:
        copy.wait()
    targets = jnp.concatenate([slot_ref[...]] * 2, axis=1)
    target_ref[...] = targets
    wide = 2 * blocks
    columns = pl.cdiv(slots + wide, 128) * 128
    lane = iota((1, columns), 1)
    both = jnp.concatenate([slot_ref[...], jnp.full((1, columns - slots), -1, jnp.int32)], axis=1)
    for y in range(blocks):
        both = jnp.where(lane == columns - wide + y, y * cz, both)
        both = jnp.where(lane == columns - blocks + y, (y + 1) * cz - 1, both)
    hot = one_hot(both, cells)
    hot_ref[...] = hot
    config = jnp.concatenate([config_ref[y : y + 1, :] for y in range(blocks)], axis=1)
    config = dot(jnp.broadcast_to(config.astype(F32), (16, cells)).astype(BF16), hot)[0:1, :]

    half = iota((1, lanes), 1) < slots

    def twice(x):
        if 2 * slots == columns:
            return jnp.where(iota(x.shape, 1) < slots, x, pltpu.roll(x, slots, axis=1))
        return jnp.concatenate([x[:, :slots]] * 2, axis=1)

    config_twice = twice(config)
    xi = [jnp.concatenate([xi_ref[j]] * 2, axis=1) for j in range(3)]
    (px, dx), (py, dy), (pz, dz) = shapes_of(xi, lanes)
    basis = (jnp.where(half, px, dx) * (py * pz), px * jnp.where(half, dy * pz, py * dz))
    for j in range(2):
        basis_ref[j * nodes : (j + 1) * nodes, :] = basis[j]
        parts_ref[:, j * lanes : (j + 1) * lanes] = turned_parts(*split(basis[j]))
    for copy in copies[3:]:
        copy.wait()
    matrix = turned_matrix(offset_ref[...], nconf, nodes)
    matrix_ref[...] = matrix
    raw = []
    for k in range(comps):
        row = 2 * k * nodes
        for y in range(blocks):
            high, low = split(v_ref[pl.ds(k * nodes * blocks + y, nodes, stride=blocks), :])
            at = slice(y * cz, (y + 1) * cz)
            split_ref[row : row + nodes, at] = high
            split_ref[row + nodes : row + 2 * nodes, at] = low
        both = dot(split_ref[row : row + 2 * nodes, :], hot_ref[...])
        raw.append(both[:nodes] + both[nodes:])
    product = dot(matrix, parts_ref[...])
    weights = []
    for j in range(2):
        weights.append(basis_ref[j * nodes : (j + 1) * nodes, :] + configured(product[:, j * lanes : (j + 1) * lanes], config_twice, nconf))
        weight_ref[j * nodes : (j + 1) * nodes, :] = weights[j]

    for k in range(comps):
        value = twice(raw[k])
        for j in range(2):
            sums = jnp.sum(value * weights[j], axis=0, keepdims=True)
            other = pltpu.roll(sums, slots, axis=1)
            left, right = ((k, 3 + 3 * k), (4 + 3 * k, 5 + 3 * k))[j]
            own_ref[left : left + 1, :] = jnp.where(half, sums, other)
            own_ref[right : right + 1, :] = jnp.where(half, other, sums)
    for i in range(9):
        own_ref[16 + i : 17 + i, :] = jnp.concatenate([strain_ref[i]] * 2, axis=1)
    for i in range(3):
        own_ref[25 + i : 26 + i, :] = jnp.concatenate([motion_ref[i]] * 2, axis=1)
    for i in (12, 28):
        own_ref[i : i + 4, :] = jnp.zeros((4, lanes), F32)

    count = comps * nodes // 16
    ends = jnp.concatenate([r[:, columns - 128 :] for r in raw], axis=0)
    lane = iota((16, 128), 1)
    at_end = 128 - wide
    packed = jnp.broadcast_to(pltpu.roll(config[:, columns - 128 :], (count * wide - at_end) % 128, axis=1), (16, 128))
    for g in range(count):
        group = pltpu.roll(ends[16 * g : 16 * (g + 1)], (g * wide - at_end) % 128, axis=1)
        packed = jnp.where((lane >= g * wide) & (lane < (g + 1) * wide), group, packed)
    talk_ref[talk_ref.shape[0] - 16 :, :] = packed
    if fast:
        parts = jnp.where(lane < slots, own_ref[0:16, :], own_ref[16:32, :])
        self_ref[...] = parts
        talk_ref[0:16, :] = jnp.where(lane & 8 == 0, pltpu.roll(parts, 120, axis=1), pltpu.roll(parts, 8, axis=1))
    else:
        self_ref[...] = jnp.zeros_like(self_ref)


def local(
    dims, axes,
    split_ref, offset_ref, config_ref,
    con_ref, xa_ref, xb_ref, ya_ref, yb_ref,
    field_ref,
):
    comps, nodes, cx, cy, cz, nconf, slots, lanes = dims
    blocks = cx * cy
    me_x, me_y = lax.axis_index(axes[0]), lax.axis_index(axes[1])
    even_x, even_y = me_x % 2 == 0, me_y % 2 == 0
    config_rows = [config_ref[y : y + 1, :] for y in range(blocks)]

    def columns(k, ys):
        at = slice(ys[0] * cz, (ys[-1] + 1) * cz)
        high = split_ref[2 * k * nodes : (2 * k + 1) * nodes, at]
        low = split_ref[(2 * k + 1) * nodes : (2 * k + 2) * nodes, at]
        value = high.astype(F32) + low.astype(F32)
        return [value[:, i * cz : (i + 1) * cz] for i in range(len(ys))], tripled(high, low)

    def store(k, y, value):
        field_ref[(y * comps + k) * nodes : (y * comps + k + 1) * nodes, :] = value
        part, rest = split(value)
        row = 2 * k * nodes
        con_ref[row : row + nodes, y * cz : (y + 1) * cz] = part
        con_ref[row + nodes : row + 2 * nodes, y * cz : (y + 1) * cz] = rest

    constrain(plain_matrix(offset_ref[...]), columns, config_rows, store, nconf, comps, blocks, cz)

    face = nodes // 4
    for k in range(comps):
        for y in range(cy):
            low_row = (y * comps + k) * nodes
            up_row = (((cx - 1) * cy + y) * comps + k + 1) * nodes
            lower = field_ref[low_row : low_row + face, :]
            upper = field_ref[up_row - face : up_row, :]
            cells = slice(y * cz, (y + 1) * cz)
            xa_ref[k * face : (k + 1) * face, cells] = jnp.where(even_x, upper, lower)
            xb_ref[k * face : (k + 1) * face, cells] = jnp.where(even_x, lower, upper)
        for a in range(4):
            into = k * face + a * 4
            for x in range(cx):
                first = (x * cy * comps + k) * nodes + a * face
                last = ((x * cy + cy - 1) * comps + k) * nodes + a * face
                lower = field_ref[first : first + 4, :]
                upper = field_ref[last + 12 : last + 16, :]
                ya_ref[into : into + 4, x * cz : (x + 1) * cz] = jnp.where(even_y, upper, lower)
                yb_ref[into : into + 4, x * cz : (x + 1) * cz] = jnp.where(even_y, lower, upper)


def solid(vel, grad, strain, motion):
    deform = [strain[3 * j + l] + (1.0 if j == l else 0.0) for j in range(3) for l in range(3)]
    moved = []
    for k in range(3):
        for l in range(3):
            change = sum(grad[3 * k + j] * deform[3 * j + l] for j in range(3))
            moved.append(deform[3 * k + l] + TIME_STEP * change)
    stress = [
        sum(moved[3 * k + l] * moved[3 * m + l] for l in range(3)) - (1.0 if k == m else 0.0)
        for k in range(3) for m in range(3)
    ]
    drag = [SPRING_RATE * (motion[k] - vel[k]) for k in range(3)]
    return moved, stress, drag


def node_tables():
    i, j = iota((64, 64), 0), iota((64, 64), 1)
    digits = [((i >> s) & 3, (j >> s) & 3) for s in (4, 2, 0)]
    same = [p == q for p, q in digits]
    lap = jnp.zeros((64, 64), F32)
    swaps = []
    for d in range(3):
        others = same[(d + 1) % 3] & same[(d + 2) % 3]
        p, q = digits[d]
        line = jnp.where(p == q, 2.0, jnp.where((p - q == 1) | (q - p == 1), -1.0, 0.0))
        lap = lap + jnp.where(others, line, 0.0)
        swaps.append(jnp.where(others & (((p == 0) & (q == 3)) | ((p == 3) & (q == 0))), 1.0, 0.0))
    return jnp.concatenate([lap, swaps[2], swaps[1]], axis=0).astype(BF16)


def sides(even, open_b, a, b):
    b = jnp.where(open_b, b, 0.0)
    return jnp.where(even, b, a), jnp.where(even, a, b)


def place(axis, n):
    index = lax.axis_index(axis)
    even = index % 2 == 0
    return even, jnp.where(even, index, n - 1 - index) > 0


def middle(
    dims, axes, sizes, fast,
    za_ref, con_ref, viscosity_ref, offset_ref, matrix_ref, config_ref, xa_ref, xb_ref, zb_ref, target_ref,
    total_ref, hot_ref,
):
    comps, nodes, cx, cy, cz, nconf, slots, lanes = dims
    blocks = cx * cy
    face = nodes // 4
    even_x, open_x = place(axes[0], sizes[0])
    even_z, open_z = place(axes[2], sizes[2])

    table = node_tables()
    table = jnp.concatenate([table, table], axis=1)
    row = iota((nodes, cz), 0)
    a, b, c = (row >> 4) & 3, (row >> 2) & 3, row & 3

    def ends(p):
        return jnp.where((p == 0) | (p == 3), PENALTY, 0.0)

    keep = 1.0 + ends(a) + ends(b) + ends(c)
    lane = iota((nodes, cz), 1)
    count = comps * nodes // 16
    wide = 2 * blocks
    plain = plain_matrix(offset_ref[...])
    hot_ref[...] = one_hot(jnp.concatenate([target_ref[...]] * 2, axis=1), blocks * cz)

    def ends_of(ref):
        packed = ref[ref.shape[0] - 16 :, :]
        config = pltpu.roll(packed, (128 - count * wide) % 128, axis=1)
        groups = [pltpu.roll(packed, (128 - g * wide) % 128, axis=1) for g in range(count)]
        rows = jnp.concatenate(groups, axis=0)
        raw = rows[:nodes]
        spread_config = config[0:1]
        for k in range(1, comps):
            here = lane >= k * wide
            raw = jnp.where(here, pltpu.roll(rows[k * nodes : (k + 1) * nodes], k * wide, axis=1), raw)
            spread_config = jnp.where(here[0:1], pltpu.roll(config, k * wide, axis=1)[0:1], spread_config)
        raw = jnp.where(lane < comps * wide, raw, 0.0)
        return raw + configured(dot(plain, tripled(*split(raw))), spread_config, nconf)

    z_a = ends_of(za_ref)
    z_low, z_up = sides(even_z, open_z, z_a, z_a if fast else ends_of(zb_ref))
    z_low, z_up = pltpu.roll(z_low, nodes - 3, axis=0), pltpu.roll(z_up, 3, axis=0)
    config_rows = [config_ref[y : y + 1, :] for y in range(blocks)]
    matrix = matrix_ref[...]

    for k in range(comps):
        pair = con_ref[2 * k * nodes : 2 * (k + 1) * nodes, :]
        ops = dot(table, pair)
        rows = slice(k * face, (k + 1) * face)
        x_low, x_up = sides(even_x, open_x, xa_ref[rows, :], xb_ref[rows, :])
        values = []
        for y in range(blocks):
            x_at, y_at = y // cy, y % cy
            cells = slice(y * cz, (y + 1) * cz)
            value = pair[:nodes, cells].astype(F32) + pair[nodes:, cells].astype(F32)
            total = keep * value + viscosity_ref[y : y + 1, :] * ops[0:nodes, cells]
            moved_z = ops[nodes : 2 * nodes, cells]
            below = jnp.where(lane == 0, pltpu.roll(z_low, cz - k * wide - blocks - y, axis=1), pltpu.roll(moved_z, 1, axis=1))
            above = jnp.where(
                lane == cz - 1, pltpu.roll(z_up, cz - 1 - k * wide - y, axis=1), pltpu.roll(moved_z, cz - 1, axis=1)
            )
            near = jnp.where(c == 0, below, jnp.where(c == 3, above, 0.0))
            if y_at > 0:
                near = near + jnp.where(b == 0, ops[2 * nodes : 3 * nodes, (y - 1) * cz : y * cz], 0.0)
            if y_at < cy - 1:
                near = near + jnp.where(b == 3, ops[2 * nodes : 3 * nodes, (y + 1) * cz : (y + 2) * cz], 0.0)
            total = total - PENALTY * near
            plane = slice(y_at * cz, (y_at + 1) * cz)
            if x_at > 0:
                other = slice((y - cy) * cz, (y - cy + 1) * cz)
                below = pair[nodes - face : nodes, other].astype(F32) + pair[2 * nodes - face :, other].astype(F32)
            else:
                below = x_low[:, plane]
            if x_at < cx - 1:
                other = slice((y + cy) * cz, (y + cy + 1) * cz)
                above = pair[:face, other].astype(F32) + pair[nodes : nodes + face, other].astype(F32)
            else:
                above = x_up[:, plane]
            total = jnp.concatenate(
                [total[:face] - PENALTY * below, total[face : nodes - face], total[nodes - face :] - PENALTY * above],
                axis=0,
            )
            values.append(total)
        inner = [y for y in range(blocks) if 0 < y % cy < cy - 1]
        if inner:
            product = dot(matrix, turned_parts(*split(jnp.concatenate([values[y] for y in inner], axis=1))))
            for i, y in enumerate(inner):
                values[y] = values[y] + configured(product[:, i * cz : (i + 1) * cz], config_rows[y], nconf)
        for y in range(blocks):
            total_ref[k * nodes : (k + 1) * nodes, y * cz : (y + 1) * cz] = values[y]


def outer_blocks(cx, cy):
    return [y for y in range(cx * cy) if y % cy in (0, cy - 1)]


def widen(face, nodes):
    return jnp.concatenate([face[4 * (i // 4) : 4 * (i // 4) + 4] for i in range(nodes // 4)], axis=0)


def gather_parts(refs, axes):
    me_y, me_s = lax.axis_index(axes[1]), lax.axis_index(axes[2])
    lane = iota((16, 128), 1)
    parts = jnp.zeros((16, 128), F32)
    for bits, ref in enumerate(refs):
        block = ref[0:16, :]
        if bits == 2:
            block = jnp.concatenate([block[8:], block[:8]], axis=0)
        for side in range(2):
            place = me_y * 2 + (me_s ^ side)
            source = (me_y ^ bits) * 2 + (me_s ^ side)
            moved = pltpu.roll(block, ((source - place) * 8) & 127, axis=1)
            parts = jnp.where((lane & 63) >> 3 == source, moved, parts)
    other = pltpu.roll(parts, 64, axis=1)
    return jnp.concatenate([jnp.where(lane < 64, parts, other), jnp.where(lane < 64, other, parts)], axis=0)


def rim(
    dims, axes, sizes, fast,
    total_ref, yb_ref, ya_ref, matrix_ref, config_ref,
    rim_ref,
):
    comps, nodes, cx, cy, cz, nconf, slots, lanes = dims
    face = nodes // 4
    even_y, open_y = place(axes[1], sizes[1])
    first = 16 if fast else 0
    b = (iota((nodes, cz), 0) >> 2) & 3
    matrix = matrix_ref[...]
    for k in range(comps):
        rows = slice(first + k * face, first + (k + 1) * face)
        y_low, y_up = sides(even_y, open_y, ya_ref[rows, :], yb_ref[rows, :])
        outer = outer_blocks(cx, cy)
        values = []
        for y in outer:
            plane = slice(y // cy * cz, (y // cy + 1) * cz)
            value = total_ref[k * nodes : (k + 1) * nodes, y * cz : (y + 1) * cz]
            if y % cy == 0:
                value = value - jnp.where(b == 0, PENALTY * widen(y_low[:, plane], nodes), 0.0)
            if y % cy == cy - 1:
                value = value - jnp.where(b == 3, PENALTY * widen(y_up[:, plane], nodes), 0.0)
            values.append(value)
        product = dot(matrix, turned_parts(*split(jnp.concatenate(values, axis=1))))
        for i, y in enumerate(outer):
            at = slice(i * cz, (i + 1) * cz)
            rim_ref[k * nodes : (k + 1) * nodes, at] = values[i] + configured(product[:, at], config_ref[y : y + 1, :], nconf)


def after(
    dims, axes, fast,
    total_ref, *refs,
):
    comps, nodes, cx, cy, cz, nconf, slots, lanes = dims
    blocks = cx * cy
    if fast:
        got_3, got_2, got_1, pair_ref, *refs = refs
        part_refs = (pair_ref, got_1, got_2, got_3)
    else:
        *part_refs, refs = refs[0], refs[1:]
    rim_ref, hot_ref, weight_ref, own_ref, out_hbm, deform_hbm, out_ref, deform_ref, sems = refs

    parts = gather_parts(part_refs, axes) if fast else part_refs[0][...]
    own = [own_ref[i : i + 1, :] for i in range(32)]
    got = [parts[i : i + 1, :] for i in range(32)]
    _, stress, drag = solid(own[0:3], own[3:12], got[16:25], got[25:28])
    moved, _, _ = solid(got[0:3], got[3:12], own[16:25], own[25:28])
    for i in range(9):
        deform_ref[i] = moved[i][:, :slots]
    copies = [pltpu.make_async_copy(deform_ref, deform_hbm, sems.at[comps])]
    copies[0].start()
    hot = hot_ref[...]
    half = iota((1, lanes), 1) < slots
    highs, lows = [], []
    for k in range(comps):
        force = jnp.where(half, drag[k], -stress[3 * k]) * weight_ref[:nodes, :]
        force = force - jnp.where(half, stress[3 * k + 1], stress[3 * k + 2]) * weight_ref[nodes:, :]
        high, low = split(force)
        highs.append(high)
        lows.append(low)
    pieces = jnp.concatenate([jnp.concatenate(highs, axis=0), jnp.concatenate(lows, axis=0)], axis=1)
    spreads = dot(pieces, hot, ((1,), (1,)))

    outer = outer_blocks(cx, cy)
    for k in range(comps):
        rows = slice(k * nodes, (k + 1) * nodes)
        for y in range(blocks):
            cells = slice(y * cz, (y + 1) * cz)
            if y in outer:
                value = rim_ref[rows, outer.index(y) * cz : (outer.index(y) + 1) * cz]
            else:
                value = total_ref[rows, cells]
            out_ref[pl.ds(k * nodes * blocks + y, nodes, stride=blocks), :] = value - spreads[rows, cells]
        done = slice(k * nodes * blocks, (k + 1) * nodes * blocks)
        copies.append(pltpu.make_async_copy(out_ref.at[done, :], out_hbm.at[done, :], sems.at[k]))
        copies[-1].start()
    for copy in copies:
        copy.wait()


def swap(x, axis, stage):
    n = lax.axis_size(axis)
    pairs = [(i, i + 1) for i in range(stage, n - 1, 2)]
    if not pairs:
        return jnp.zeros_like(x)
    return lax.ppermute(x, axis, pairs + [(j, i) for i, j in pairs])


def flip(x, axis, bits):
    return lax.ppermute(x, axis, [(i, i ^ bits) for i in range(lax.axis_size(axis))])


def shards(
    mesh_sizes,
    velocity,
    viscosity,
    cell_config,
    constraint_offsets,
    slot_cells,
    point_coords,
    strain_offsets,
    solid_velocity,
):
    axes = ("dx", "dy", "solid")
    comps, cx, cy, cz = velocity.shape[0], *velocity.shape[4:]
    nodes = velocity.shape[1] * velocity.shape[2] * velocity.shape[3]
    blocks = cx * cy
    nconf = constraint_offsets.shape[0]
    slots = slot_cells.shape[-1]
    n_dx, n_dy, n_solid = mesh_sizes
    face_rows = comps * nodes // 4
    lanes = 2 * slots
    dims = (comps, nodes, cx, cy, cz, nconf, slots, lanes)

    v = velocity.reshape(comps * nodes * blocks, cz)
    visc = viscosity.reshape(blocks, cz)
    config = cell_config.reshape(blocks, cz)
    offsets = constraint_offsets.reshape(nconf * nodes, nodes)
    targets = slot_cells.reshape(1, slots)
    xi = point_coords.reshape(3, 1, slots)
    strain = strain_offsets.reshape(9, 1, slots)
    motion = solid_velocity.reshape(3, 1, slots)

    vmem = pl.BlockSpec(memory_space=pltpu.VMEM)
    hbm = pl.BlockSpec(memory_space=pltpu.HBM)
    params = pltpu.CompilerParams(vmem_limit_bytes=VMEM_LIMIT)
    cells = blocks * cz
    face_y = jax.ShapeDtypeStruct((face_rows, cx * cz), F32)
    face_x = jax.ShapeDtypeStruct((face_rows, cy * cz), F32)
    def shape(*size, dtype=F32):
        return jax.ShapeDtypeStruct(size, dtype)

    def estimate(columns):
        return pl.CostEstimate(flops=2 * 6 * nconf * nodes * nodes * columns, bytes_accessed=1_000_000, transcendentals=0)

    fast = (n_dx, n_dy, n_solid, slots) == (4, 4, 2, 64)
    talk, mine, own, parted, matrix, targets, weights, config, offsets, visc = pl.pallas_call(
        functools.partial(begin, dims, axes, fast),
        out_shape=(
            shape(32 if fast else 16, 128),
            shape(16, 128),
            shape(32, lanes),
            shape(2 * comps * nodes, cells, dtype=BF16),
            shape(nconf * nodes, 3 * nodes, dtype=BF16),
            shape(1, lanes, dtype=targets.dtype),
            shape(2 * nodes, lanes),
            shape(*config.shape, dtype=config.dtype),
            shape(*offsets.shape),
            shape(*visc.shape),
        ),
        in_specs=[hbm] * 8,
        out_specs=(vmem,) * 10,
        scratch_shapes=[
            pltpu.VMEM(v.shape, F32),
            pltpu.VMEM(targets.shape, targets.dtype),
            pltpu.VMEM(xi.shape, F32),
            pltpu.VMEM(strain.shape, F32),
            pltpu.VMEM(motion.shape, F32),
            pltpu.VMEM((cells, pl.cdiv(slots + 2 * blocks, 128) * 128), BF16),
            pltpu.VMEM((3 * nodes, 2 * lanes), BF16),
            pltpu.VMEM((2 * nodes, lanes), F32),
            pltpu.SemaphoreType.DMA((8,)),
        ],
        compiler_params=params,
        name="begin",
    )(*(pltpu.with_memory_space_constraint(x, pltpu.HBM) for x in (v, config, offsets, targets, xi, strain, motion, visc)))

    con, xa, xb, ya, yb = pl.pallas_call(
        functools.partial(local, dims, axes),
        out_shape=(shape(2 * comps * nodes, cells, dtype=BF16), face_x, face_x, face_y, face_y),
        in_specs=[vmem] * 3,
        out_specs=(vmem,) * 5,
        scratch_shapes=[pltpu.VMEM((blocks * comps * nodes, cz), F32)],
        compiler_params=params,
        cost_estimate=estimate(comps * cells),
        name="local",
    )(parted, offsets, config)

    if fast:
        got_s = swap(talk, "solid", 0)
        got_xa = swap(xa, "dx", 0)
        got_xb = flip(xb, "dx", 3)
        own_side = (iota((16, 128), 1) >> 3) & 1 == lax.axis_index("solid")
        pair = jnp.where(own_side, mine, got_s[:16])
        got_3 = flip(jnp.concatenate([pair, yb], axis=0), "dy", 3)
        got_2 = flip(jnp.concatenate([pair[8:], pair[:8]], axis=0), "dy", 2)
        got_1 = flip(jnp.concatenate([pair, ya], axis=0), "dy", 1)
        parts = [got_3, got_2, got_1, pair]
        got_ya, got_yb = got_1, got_3
        got_za, got_zb = got_s, got_s
    else:
        got_xa, got_xb = swap(xa, "dx", 0), swap(xb, "dx", 1)
        got_ya, got_yb = swap(ya, "dy", 0), swap(yb, "dy", 1)
        got_za, got_zb = swap(talk, "solid", 0), swap(talk, "solid", 1)
        sent = jnp.concatenate([own[:12, :slots], own[16:28, :slots]], axis=0)
        got_parts = lax.all_to_all(sent, ("dy", "solid"), split_axis=1, concat_axis=1, tiled=True)
        got_parts = jnp.pad(got_parts.reshape(2, 12, slots), ((0, 0), (0, 4), (0, 0))).reshape(32, slots)
        parts = [jnp.concatenate([got_parts] * 2, axis=1)]

    total, hot = pl.pallas_call(
        functools.partial(middle, dims, axes, mesh_sizes, fast),
        out_shape=(shape(comps * nodes, cells), shape(cells, 2 * lanes, dtype=BF16)),
        in_specs=[vmem] * 10,
        out_specs=(vmem,) * 2,
        compiler_params=params,
        cost_estimate=estimate(comps * cells),
        name="middle",
    )(got_za, con, visc, offsets, matrix, config, got_xa, got_xb, got_zb, targets)

    rims = pl.pallas_call(
        functools.partial(rim, dims, axes, mesh_sizes, fast),
        out_shape=shape(comps * nodes, len(outer_blocks(cx, cy)) * cz),
        in_specs=[vmem] * 5,
        out_specs=vmem,
        compiler_params=params,
        cost_estimate=estimate(comps * cells),
        name="rim",
    )(total, got_yb, got_ya, matrix, config)

    out, deform = pl.pallas_call(
        functools.partial(after, dims, axes, fast),
        out_shape=(shape(*v.shape), shape(9, 1, slots)),
        in_specs=[vmem] * (5 + len(parts)),
        out_specs=(hbm, hbm),
        scratch_shapes=[
            pltpu.VMEM(v.shape, F32),
            pltpu.VMEM(strain.shape, F32),
            pltpu.SemaphoreType.DMA((comps + 1,)),
        ],
        compiler_params=params,
        name="after",
    )(total, *parts, rims, hot, weights, own)
    return out.reshape(velocity.shape), deform.reshape(strain_offsets.shape)


def solution(mesh):
    sizes = tuple(mesh.shape[a] for a in ("dx", "dy", "solid"))
    return jax.shard_map(
        functools.partial(shards, sizes),
        mesh=mesh,
        in_specs=(
            P(None, None, None, None, "dx", "dy", "solid"),
            P("dx", "dy", "solid"),
            P("dx", "dy", "solid"),
            P(),
            P("dx", ("dy", "solid"), None),
            P(None, "dx", ("dy", "solid"), None),
            P(None, None, "dx", ("dy", "solid"), None),
            P(None, "dx", ("dy", "solid"), None),
        ),
        out_specs=(
            P(None, None, None, None, "dx", "dy", "solid"),
            P(None, None, "dx", ("dy", "solid"), None),
        ),
        check_vma=False,
    )
```

```python
import functools

import jax
import jax.numpy as jnp
from jax import lax
from jax.experimental import pallas as pl
from jax.experimental.pallas import tpu as pltpu
from jax.sharding import PartitionSpec as P

TIME_STEP = 0.05
SPRING_RATE = 2.0
PENALTY = 4.0
NODE_POINTS = (0.0, 1.0 / 3.0, 2.0 / 3.0, 1.0)
F32, BF16 = jnp.float32, jnp.bfloat16
VMEM_LIMIT = 24 * 1024 * 1024


def iota(shape, dim):
    return lax.broadcasted_iota(jnp.int32, shape, dim)


def split(x):
    high = x.astype(BF16)
    low = (x - high.astype(F32)).astype(BF16)
    return high, low


def dot(a, b, dims=((1,), (0,))):
    return lax.dot_general(a, b, (dims, ((), ())), preferred_element_type=F32)


def lagrange(coord):
    values = []
    slopes = []
    for which in range(4):
        others = [NODE_POINTS[j] for j in range(4) if j != which]
        denom = 1.0
        for other in others:
            denom = denom * (NODE_POINTS[which] - other)
        scale = 1.0 / denom
        first = coord - others[0]
        second = coord - others[1]
        third = coord - others[2]
        values.append(first * second * third * scale)
        slopes.append((second * third + first * third + first * second) * scale)
    return values, slopes


def spread_rows(parts, dim, lanes):
    wide = [jnp.broadcast_to(p, (8, lanes)) for p in parts]
    if dim == 0:
        return jnp.concatenate([wide[a] for a in (0, 0, 1, 1, 2, 2, 3, 3)], axis=0)
    row = iota((8, lanes), 0)
    if dim == 1:
        even = jnp.where(row < 4, wide[0], wide[1])
        odd = jnp.where(row < 4, wide[2], wide[3])
        return jnp.concatenate([even, odd] * 4, axis=0)
    c = row & 3
    block = jnp.where(c == 0, wide[0], jnp.where(c == 1, wide[1], jnp.where(c == 2, wide[2], wide[3])))
    return jnp.concatenate([block] * 8, axis=0)


def shapes_of(xi, lanes):
    out = []
    for dim in range(3):
        values, slopes = lagrange(xi[dim])
        out.append((spread_rows(values, dim, lanes), spread_rows(slopes, dim, lanes)))
    return out


def one_hot(slots, cells):
    lanes = slots.shape[1]
    return jnp.where(iota((cells, lanes), 0) == slots, 1.0, 0.0).astype(BF16)


def configured(product, config, nconf):
    rows = product.shape[0] // nconf
    chosen = product[:rows]
    for which in range(1, nconf):
        chosen = jnp.where(config == which, product[which * rows : (which + 1) * rows], chosen)
    return chosen


def tripled(high, low):
    return jnp.concatenate([high, low, high], axis=0)


def turned_parts(high, low):
    return jnp.concatenate([high, high, low], axis=0)


def constrain(matrix, columns, config_rows, store, nconf, comps, blocks, lanes):
    step = 2 if blocks % 2 == 0 else 1
    for k in range(comps):
        for first in range(0, blocks, step):
            values, parts = columns(k, range(first, first + step))
            product = dot(matrix, parts)
            for i in range(step):
                piece = product[:, i * lanes : (i + 1) * lanes]
                store(k, first + i, values[i] + configured(piece, config_rows[first + i], nconf))


def fetch(pairs, sems):
    copies = [pltpu.make_async_copy(src, dst, sems.at[i]) for i, (src, dst) in enumerate(pairs)]
    for copy in copies:
        copy.start()
    return copies


def plain_matrix(offsets):
    high, low = split(offsets)
    return jnp.concatenate([high, high, low], axis=1)


def turned_matrix(offsets, nconf, nodes):
    blocks = [offsets[w * nodes : (w + 1) * nodes, :] for w in range(nconf)]
    highs, lows = [], []
    for block in blocks:
        high = block.astype(BF16).astype(F32)
        both = jnp.concatenate([high, block - high], axis=0).T.astype(BF16)
        highs.append(both)
        lows.append(both[:, :nodes])
    return jnp.concatenate([jnp.concatenate(highs, axis=0), jnp.concatenate(lows, axis=0)], axis=1)


def begin(
    dims, axes, fast,
    v_hbm, config_hbm, offset_hbm, slot_hbm, xi_hbm, strain_hbm, motion_hbm,
    talk_ref, self_ref, own_ref, split_ref, matrix_ref, target_ref, weight_ref, config_ref, offset_ref,
    v_ref, slot_ref, xi_ref, strain_ref, motion_ref, sems,
):
    comps, nodes, cx, cy, cz, nconf, slots, lanes = dims
    blocks = cx * cy
    cells = blocks * cz
    copies = fetch(
        [(v_hbm, v_ref), (offset_hbm, offset_ref), (slot_hbm, slot_ref), (config_hbm, config_ref), (xi_hbm, xi_ref),
         (strain_hbm, strain_ref), (motion_hbm, motion_ref)],
        sems,
    )

    for copy in copies:
        copy.wait()
    targets = jnp.concatenate([slot_ref[...]] * 2, axis=1)
    target_ref[...] = targets
    wide = 2 * blocks
    columns = pl.cdiv(slots + wide, 128) * 128
    lane = iota((1, columns), 1)
    both = jnp.concatenate([slot_ref[...], jnp.full((1, columns - slots), -1, jnp.int32)], axis=1)
    for y in range(blocks):
        both = jnp.where(lane == columns - wide + y, y * cz, both)
        both = jnp.where(lane == columns - blocks + y, (y + 1) * cz - 1, both)
    hot = one_hot(both, cells)
    config = jnp.concatenate([config_ref[y : y + 1, :] for y in range(blocks)], axis=1)
    config = dot(jnp.broadcast_to(config.astype(F32), (16, cells)).astype(BF16), hot)[0:1, :]

    half = iota((1, lanes), 1) < slots

    def twice(x):
        if 2 * slots == columns:
            return jnp.where(iota(x.shape, 1) < slots, x, pltpu.roll(x, slots, axis=1))
        return jnp.concatenate([x[:, :slots]] * 2, axis=1)

    config_twice = twice(config)
    xi = [jnp.concatenate([xi_ref[j]] * 2, axis=1) for j in range(3)]
    (px, dx), (py, dy), (pz, dz) = shapes_of(xi, lanes)
    basis = (jnp.where(half, px, dx) * (py * pz), px * jnp.where(half, dy * pz, py * dz))
    matrix = turned_matrix(offset_ref[...], nconf, nodes)
    matrix_ref[...] = matrix
    raw = []
    for k in range(comps):
        row = 2 * k * nodes
        for y in range(blocks):
            high, low = split(v_ref[pl.ds(k * nodes * blocks + y, nodes, stride=blocks), :])
            at = slice(y * cz, (y + 1) * cz)
            split_ref[row : row + nodes, at] = high
            split_ref[row + nodes : row + 2 * nodes, at] = low
        both = dot(split_ref[row : row + 2 * nodes, :], hot)
        raw.append(both[:nodes] + both[nodes:])
    product = dot(matrix, jnp.concatenate([turned_parts(*split(p)) for p in basis], axis=1))
    weights = []
    for j in range(2):
        weights.append(basis[j] + configured(product[:, j * lanes : (j + 1) * lanes], config_twice, nconf))
        weight_ref[j * nodes : (j + 1) * nodes, :] = weights[j]

    for k in range(comps):
        value = twice(raw[k])
        for j in range(2):
            sums = jnp.sum(value * weights[j], axis=0, keepdims=True)
            other = pltpu.roll(sums, slots, axis=1)
            left, right = ((k, 3 + 3 * k), (4 + 3 * k, 5 + 3 * k))[j]
            own_ref[left : left + 1, :] = jnp.where(half, sums, other)
            own_ref[right : right + 1, :] = jnp.where(half, other, sums)
    for i in range(9):
        own_ref[16 + i : 17 + i, :] = jnp.concatenate([strain_ref[i]] * 2, axis=1)
    for i in range(3):
        own_ref[25 + i : 26 + i, :] = jnp.concatenate([motion_ref[i]] * 2, axis=1)
    for i in (12, 28):
        own_ref[i : i + 4, :] = jnp.zeros((4, lanes), F32)

    count = comps * nodes // 16
    ends = jnp.concatenate([r[:, columns - 128 :] for r in raw], axis=0)
    lane = iota((16, 128), 1)
    at_end = 128 - wide
    packed = jnp.broadcast_to(pltpu.roll(config[:, columns - 128 :], (count * wide - at_end) % 128, axis=1), (16, 128))
    for g in range(count):
        group = pltpu.roll(ends[16 * g : 16 * (g + 1)], (g * wide - at_end) % 128, axis=1)
        packed = jnp.where((lane >= g * wide) & (lane < (g + 1) * wide), group, packed)
    talk_ref[talk_ref.shape[0] - 16 :, :] = packed
    if fast:
        parts = jnp.where(lane < slots, own_ref[0:16, :], own_ref[16:32, :])
        self_ref[...] = parts
        talk_ref[0:16, :] = jnp.where(lane & 8 == 0, pltpu.roll(parts, 120, axis=1), pltpu.roll(parts, 8, axis=1))
    else:
        self_ref[...] = jnp.zeros_like(self_ref)


def local(
    dims, axes,
    split_ref, offset_ref, config_ref,
    con_ref, xa_ref, xb_ref, ya_ref, yb_ref,
    field_ref,
):
    comps, nodes, cx, cy, cz, nconf, slots, lanes = dims
    blocks = cx * cy
    me_x, me_y = lax.axis_index(axes[0]), lax.axis_index(axes[1])
    even_x, even_y = me_x % 2 == 0, me_y % 2 == 0
    config_rows = [config_ref[y : y + 1, :] for y in range(blocks)]

    def columns(k, ys):
        at = slice(ys[0] * cz, (ys[-1] + 1) * cz)
        high = split_ref[2 * k * nodes : (2 * k + 1) * nodes, at]
        low = split_ref[(2 * k + 1) * nodes : (2 * k + 2) * nodes, at]
        value = high.astype(F32) + low.astype(F32)
        return [value[:, i * cz : (i + 1) * cz] for i in range(len(ys))], tripled(high, low)

    def store(k, y, value):
        field_ref[(y * comps + k) * nodes : (y * comps + k + 1) * nodes, :] = value
        part, rest = split(value)
        row = 2 * k * nodes
        con_ref[row : row + nodes, y * cz : (y + 1) * cz] = part
        con_ref[row + nodes : row + 2 * nodes, y * cz : (y + 1) * cz] = rest

    constrain(plain_matrix(offset_ref[...]), columns, config_rows, store, nconf, comps, blocks, cz)

    face = nodes // 4
    for k in range(comps):
        for y in range(cy):
            low_row = (y * comps + k) * nodes
            up_row = (((cx - 1) * cy + y) * comps + k + 1) * nodes
            lower = field_ref[low_row : low_row + face, :]
            upper = field_ref[up_row - face : up_row, :]
            cells = slice(y * cz, (y + 1) * cz)
            xa_ref[k * face : (k + 1) * face, cells] = jnp.where(even_x, upper, lower)
            xb_ref[k * face : (k + 1) * face, cells] = jnp.where(even_x, lower, upper)
        for a in range(4):
            into = k * face + a * 4
            for x in range(cx):
                first = (x * cy * comps + k) * nodes + a * face
                last = ((x * cy + cy - 1) * comps + k) * nodes + a * face
                lower = field_ref[first : first + 4, :]
                upper = field_ref[last + 12 : last + 16, :]
                ya_ref[into : into + 4, x * cz : (x + 1) * cz] = jnp.where(even_y, upper, lower)
                yb_ref[into : into + 4, x * cz : (x + 1) * cz] = jnp.where(even_y, lower, upper)


def solid(vel, grad, strain, motion):
    deform = [strain[3 * j + l] + (1.0 if j == l else 0.0) for j in range(3) for l in range(3)]
    moved = []
    for k in range(3):
        for l in range(3):
            change = sum(grad[3 * k + j] * deform[3 * j + l] for j in range(3))
            moved.append(deform[3 * k + l] + TIME_STEP * change)
    stress = [
        sum(moved[3 * k + l] * moved[3 * m + l] for l in range(3)) - (1.0 if k == m else 0.0)
        for k in range(3) for m in range(3)
    ]
    drag = [SPRING_RATE * (motion[k] - vel[k]) for k in range(3)]
    return moved, stress, drag


def node_tables():
    i, j = iota((64, 64), 0), iota((64, 64), 1)
    digits = [((i >> s) & 3, (j >> s) & 3) for s in (4, 2, 0)]
    same = [p == q for p, q in digits]
    lap = jnp.zeros((64, 64), F32)
    swaps = []
    for d in range(3):
        others = same[(d + 1) % 3] & same[(d + 2) % 3]
        p, q = digits[d]
        line = jnp.where(p == q, 2.0, jnp.where((p - q == 1) | (q - p == 1), -1.0, 0.0))
        lap = lap + jnp.where(others, line, 0.0)
        swaps.append(jnp.where(others & (((p == 0) & (q == 3)) | ((p == 3) & (q == 0))), 1.0, 0.0))
    return jnp.concatenate([lap, swaps[2], swaps[1]], axis=0).astype(BF16)


def sides(even, open_b, a, b):
    b = jnp.where(open_b, b, 0.0)
    return jnp.where(even, b, a), jnp.where(even, a, b)


def place(axis, n):
    index = lax.axis_index(axis)
    even = index % 2 == 0
    return even, jnp.where(even, index, n - 1 - index) > 0


def middle(
    dims, axes, sizes, fast,
    za_ref, con_ref, viscosity_hbm, offset_ref, matrix_ref, config_ref, xa_ref, xb_ref, zb_ref, target_ref,
    total_ref, hot_ref,
    viscosity_ref, sems,
):
    copies = fetch([(viscosity_hbm, viscosity_ref)], sems)
    comps, nodes, cx, cy, cz, nconf, slots, lanes = dims
    blocks = cx * cy
    face = nodes // 4
    even_x, open_x = place(axes[0], sizes[0])
    even_z, open_z = place(axes[2], sizes[2])

    table = node_tables()
    table = jnp.concatenate([table, table], axis=1)
    row = iota((nodes, cz), 0)
    a, b, c = (row >> 4) & 3, (row >> 2) & 3, row & 3

    def ends(p):
        return jnp.where((p == 0) | (p == 3), PENALTY, 0.0)

    keep = 1.0 + ends(a) + ends(b) + ends(c)
    lane = iota((nodes, cz), 1)
    count = comps * nodes // 16
    wide = 2 * blocks
    plain = plain_matrix(offset_ref[...])
    hot_ref[...] = one_hot(jnp.concatenate([target_ref[...]] * 2, axis=1), blocks * cz)

    def ends_of(ref):
        packed = ref[ref.shape[0] - 16 :, :]
        config = pltpu.roll(packed, (128 - count * wide) % 128, axis=1)
        groups = [pltpu.roll(packed, (128 - g * wide) % 128, axis=1) for g in range(count)]
        rows = jnp.concatenate(groups, axis=0)
        raw = rows[:nodes]
        spread_config = config[0:1]
        for k in range(1, comps):
            here = lane >= k * wide
            raw = jnp.where(here, pltpu.roll(rows[k * nodes : (k + 1) * nodes], k * wide, axis=1), raw)
            spread_config = jnp.where(here[0:1], pltpu.roll(config, k * wide, axis=1)[0:1], spread_config)
        raw = jnp.where(lane < comps * wide, raw, 0.0)
        return raw + configured(dot(plain, tripled(*split(raw))), spread_config, nconf)

    z_a = ends_of(za_ref)
    z_low, z_up = sides(even_z, open_z, z_a, z_a if fast else ends_of(zb_ref))
    z_low, z_up = pltpu.roll(z_low, nodes - 3, axis=0), pltpu.roll(z_up, 3, axis=0)
    config_rows = [config_ref[y : y + 1, :] for y in range(blocks)]
    matrix = matrix_ref[...]

    copies[0].wait()
    for k in range(comps):
        pair = con_ref[2 * k * nodes : 2 * (k + 1) * nodes, :]
        ops = dot(table, pair)
        rows = slice(k * face, (k + 1) * face)
        x_low, x_up = sides(even_x, open_x, xa_ref[rows, :], xb_ref[rows, :])
        values = []
        for y in range(blocks):
            x_at, y_at = y // cy, y % cy
            cells = slice(y * cz, (y + 1) * cz)
            value = pair[:nodes, cells].astype(F32) + pair[nodes:, cells].astype(F32)
            total = keep * value + viscosity_ref[y : y + 1, :] * ops[0:nodes, cells]
            moved_z = ops[nodes : 2 * nodes, cells]
            below = jnp.where(lane == 0, pltpu.roll(z_low, cz - k * wide - blocks - y, axis=1), pltpu.roll(moved_z, 1, axis=1))
            above = jnp.where(
                lane == cz - 1, pltpu.roll(z_up, cz - 1 - k * wide - y, axis=1), pltpu.roll(moved_z, cz - 1, axis=1)
            )
            near = jnp.where(c == 0, below, jnp.where(c == 3, above, 0.0))
            if y_at > 0:
                near = near + jnp.where(b == 0, ops[2 * nodes : 3 * nodes, (y - 1) * cz : y * cz], 0.0)
            if y_at < cy - 1:
                near = near + jnp.where(b == 3, ops[2 * nodes : 3 * nodes, (y + 1) * cz : (y + 2) * cz], 0.0)
            total = total - PENALTY * near
            plane = slice(y_at * cz, (y_at + 1) * cz)
            if x_at > 0:
                other = slice((y - cy) * cz, (y - cy + 1) * cz)
                below = pair[nodes - face : nodes, other].astype(F32) + pair[2 * nodes - face :, other].astype(F32)
            else:
                below = x_low[:, plane]
            if x_at < cx - 1:
                other = slice((y + cy) * cz, (y + cy + 1) * cz)
                above = pair[:face, other].astype(F32) + pair[nodes : nodes + face, other].astype(F32)
            else:
                above = x_up[:, plane]
            total = jnp.concatenate(
                [total[:face] - PENALTY * below, total[face : nodes - face], total[nodes - face :] - PENALTY * above],
                axis=0,
            )
            values.append(total)
        inner = [y for y in range(blocks) if 0 < y % cy < cy - 1]
        if inner:
            product = dot(matrix, turned_parts(*split(jnp.concatenate([values[y] for y in inner], axis=1))))
            for i, y in enumerate(inner):
                values[y] = values[y] + configured(product[:, i * cz : (i + 1) * cz], config_rows[y], nconf)
        for y in range(blocks):
            total_ref[k * nodes : (k + 1) * nodes, y * cz : (y + 1) * cz] = values[y]


def outer_blocks(cx, cy):
    return [y for y in range(cx * cy) if y % cy in (0, cy - 1)]


def widen(face, nodes):
    return jnp.concatenate([face[4 * (i // 4) : 4 * (i // 4) + 4] for i in range(nodes // 4)], axis=0)


def gather_parts(refs, axes):
    me_y, me_s = lax.axis_index(axes[1]), lax.axis_index(axes[2])
    lane = iota((16, 128), 1)
    parts = jnp.zeros((16, 128), F32)
    for bits, ref in enumerate(refs):
        block = ref[0:16, :]
        if bits == 2:
            block = jnp.concatenate([block[8:], block[:8]], axis=0)
        for side in range(2):
            place = me_y * 2 + (me_s ^ side)
            source = (me_y ^ bits) * 2 + (me_s ^ side)
            moved = pltpu.roll(block, ((source - place) * 8) & 127, axis=1)
            parts = jnp.where((lane & 63) >> 3 == source, moved, parts)
    other = pltpu.roll(parts, 64, axis=1)
    return jnp.concatenate([jnp.where(lane < 64, parts, other), jnp.where(lane < 64, other, parts)], axis=0)


def rim(
    dims, axes, sizes, fast,
    total_ref, yb_ref, ya_ref, matrix_ref, config_ref,
    rim_ref,
):
    comps, nodes, cx, cy, cz, nconf, slots, lanes = dims
    face = nodes // 4
    even_y, open_y = place(axes[1], sizes[1])
    first = 16 if fast else 0
    b = (iota((nodes, cz), 0) >> 2) & 3
    matrix = matrix_ref[...]
    for k in range(comps):
        rows = slice(first + k * face, first + (k + 1) * face)
        y_low, y_up = sides(even_y, open_y, ya_ref[rows, :], yb_ref[rows, :])
        outer = outer_blocks(cx, cy)
        values = []
        for y in outer:
            plane = slice(y // cy * cz, (y // cy + 1) * cz)
            value = total_ref[k * nodes : (k + 1) * nodes, y * cz : (y + 1) * cz]
            if y % cy == 0:
                value = value - jnp.where(b == 0, PENALTY * widen(y_low[:, plane], nodes), 0.0)
            if y % cy == cy - 1:
                value = value - jnp.where(b == 3, PENALTY * widen(y_up[:, plane], nodes), 0.0)
            values.append(value)
        product = dot(matrix, turned_parts(*split(jnp.concatenate(values, axis=1))))
        for i, y in enumerate(outer):
            at = slice(i * cz, (i + 1) * cz)
            rim_ref[k * nodes : (k + 1) * nodes, at] = values[i] + configured(product[:, at], config_ref[y : y + 1, :], nconf)


def after(
    dims, axes, fast,
    total_ref, *refs,
):
    comps, nodes, cx, cy, cz, nconf, slots, lanes = dims
    blocks = cx * cy
    if fast:
        got_3, got_2, got_1, pair_ref, *refs = refs
        part_refs = (pair_ref, got_1, got_2, got_3)
    else:
        *part_refs, refs = refs[0], refs[1:]
    rim_ref, hot_ref, weight_ref, own_ref, out_hbm, deform_hbm, out_ref, deform_ref, sems = refs

    parts = gather_parts(part_refs, axes) if fast else part_refs[0][...]
    own = [own_ref[i : i + 1, :] for i in range(32)]
    got = [parts[i : i + 1, :] for i in range(32)]
    _, stress, drag = solid(own[0:3], own[3:12], got[16:25], got[25:28])
    moved, _, _ = solid(got[0:3], got[3:12], own[16:25], own[25:28])
    for i in range(9):
        deform_ref[i] = moved[i][:, :slots]
    copies = [pltpu.make_async_copy(deform_ref, deform_hbm, sems.at[comps])]
    copies[0].start()
    hot = hot_ref[...]
    half = iota((1, lanes), 1) < slots
    highs, lows = [], []
    for k in range(comps):
        force = jnp.where(half, drag[k], -stress[3 * k]) * weight_ref[:nodes, :]
        force = force - jnp.where(half, stress[3 * k + 1], stress[3 * k + 2]) * weight_ref[nodes:, :]
        high, low = split(force)
        highs.append(high)
        lows.append(low)
    pieces = jnp.concatenate([jnp.concatenate(highs, axis=0), jnp.concatenate(lows, axis=0)], axis=1)
    spreads = dot(pieces, hot, ((1,), (1,)))

    outer = outer_blocks(cx, cy)
    for k in range(comps):
        rows = slice(k * nodes, (k + 1) * nodes)
        for y in range(blocks):
            cells = slice(y * cz, (y + 1) * cz)
            if y in outer:
                value = rim_ref[rows, outer.index(y) * cz : (outer.index(y) + 1) * cz]
            else:
                value = total_ref[rows, cells]
            out_ref[pl.ds(k * nodes * blocks + y, nodes, stride=blocks), :] = value - spreads[rows, cells]
        done = slice(k * nodes * blocks, (k + 1) * nodes * blocks)
        copies.append(pltpu.make_async_copy(out_ref.at[done, :], out_hbm.at[done, :], sems.at[k]))
        copies[-1].start()
    for copy in copies:
        copy.wait()


def swap(x, axis, stage):
    n = lax.axis_size(axis)
    pairs = [(i, i + 1) for i in range(stage, n - 1, 2)]
    if not pairs:
        return jnp.zeros_like(x)
    return lax.ppermute(x, axis, pairs + [(j, i) for i, j in pairs])


def flip(x, axis, bits):
    return lax.ppermute(x, axis, [(i, i ^ bits) for i in range(lax.axis_size(axis))])


def shards(
    mesh_sizes,
    velocity,
    viscosity,
    cell_config,
    constraint_offsets,
    slot_cells,
    point_coords,
    strain_offsets,
    solid_velocity,
):
    axes = ("dx", "dy", "solid")
    comps, cx, cy, cz = velocity.shape[0], *velocity.shape[4:]
    nodes = velocity.shape[1] * velocity.shape[2] * velocity.shape[3]
    blocks = cx * cy
    nconf = constraint_offsets.shape[0]
    slots = slot_cells.shape[-1]
    n_dx, n_dy, n_solid = mesh_sizes
    face_rows = comps * nodes // 4
    lanes = 2 * slots
    dims = (comps, nodes, cx, cy, cz, nconf, slots, lanes)

    v = velocity.reshape(comps * nodes * blocks, cz)
    visc = viscosity.reshape(blocks, cz)
    config = cell_config.reshape(blocks, cz)
    offsets = constraint_offsets.reshape(nconf * nodes, nodes)
    targets = slot_cells.reshape(1, slots)
    xi = point_coords.reshape(3, 1, slots)
    strain = strain_offsets.reshape(9, 1, slots)
    motion = solid_velocity.reshape(3, 1, slots)

    vmem = pl.BlockSpec(memory_space=pltpu.VMEM)
    hbm = pl.BlockSpec(memory_space=pltpu.HBM)
    params = pltpu.CompilerParams(vmem_limit_bytes=VMEM_LIMIT)
    cells = blocks * cz
    face_y = jax.ShapeDtypeStruct((face_rows, cx * cz), F32)
    face_x = jax.ShapeDtypeStruct((face_rows, cy * cz), F32)
    def shape(*size, dtype=F32):
        return jax.ShapeDtypeStruct(size, dtype)

    def estimate(columns):
        return pl.CostEstimate(flops=2 * 6 * nconf * nodes * nodes * columns, bytes_accessed=1_000_000, transcendentals=0)

    fast = (n_dx, n_dy, n_solid, slots) == (4, 4, 2, 64)
    talk, mine, own, parted, matrix, targets, weights, config, offsets = pl.pallas_call(
        functools.partial(begin, dims, axes, fast),
        out_shape=(
            shape(32 if fast else 16, 128),
            shape(16, 128),
            shape(32, lanes),
            shape(2 * comps * nodes, cells, dtype=BF16),
            shape(nconf * nodes, 3 * nodes, dtype=BF16),
            shape(1, lanes, dtype=targets.dtype),
            shape(2 * nodes, lanes),
            shape(*config.shape, dtype=config.dtype),
            shape(*offsets.shape),
        ),
        in_specs=[hbm] * 7,
        out_specs=(vmem,) * 9,
        scratch_shapes=[
            pltpu.VMEM(v.shape, F32),
            pltpu.VMEM(targets.shape, targets.dtype),
            pltpu.VMEM(xi.shape, F32),
            pltpu.VMEM(strain.shape, F32),
            pltpu.VMEM(motion.shape, F32),
            pltpu.SemaphoreType.DMA((7,)),
        ],
        compiler_params=params,
        name="begin",
    )(*(pltpu.with_memory_space_constraint(x, pltpu.HBM) for x in (v, config, offsets, targets, xi, strain, motion)))

    con, xa, xb, ya, yb = pl.pallas_call(
        functools.partial(local, dims, axes),
        out_shape=(shape(2 * comps * nodes, cells, dtype=BF16), face_x, face_x, face_y, face_y),
        in_specs=[vmem] * 3,
        out_specs=(vmem,) * 5,
        scratch_shapes=[pltpu.VMEM((blocks * comps * nodes, cz), F32)],
        compiler_params=params,
        cost_estimate=estimate(comps * cells),
        name="local",
    )(parted, offsets, config)

    if fast:
        got_s = swap(talk, "solid", 0)
        got_xa = swap(xa, "dx", 0)
        got_xb = flip(xb, "dx", 3)
        own_side = (iota((16, 128), 1) >> 3) & 1 == lax.axis_index("solid")
        pair = jnp.where(own_side, mine, got_s[:16])
        got_3 = flip(jnp.concatenate([pair, yb], axis=0), "dy", 3)
        got_2 = flip(jnp.concatenate([pair[8:], pair[:8]], axis=0), "dy", 2)
        got_1 = flip(jnp.concatenate([pair, ya], axis=0), "dy", 1)
        parts = [got_3, got_2, got_1, pair]
        got_ya, got_yb = got_1, got_3
        got_za, got_zb = got_s, got_s
    else:
        got_xa, got_xb = swap(xa, "dx", 0), swap(xb, "dx", 1)
        got_ya, got_yb = swap(ya, "dy", 0), swap(yb, "dy", 1)
        got_za, got_zb = swap(talk, "solid", 0), swap(talk, "solid", 1)
        sent = jnp.concatenate([own[:12, :slots], own[16:28, :slots]], axis=0)
        got_parts = lax.all_to_all(sent, ("dy", "solid"), split_axis=1, concat_axis=1, tiled=True)
        got_parts = jnp.pad(got_parts.reshape(2, 12, slots), ((0, 0), (0, 4), (0, 0))).reshape(32, slots)
        parts = [jnp.concatenate([got_parts] * 2, axis=1)]

    total, hot = pl.pallas_call(
        functools.partial(middle, dims, axes, mesh_sizes, fast),
        out_shape=(shape(comps * nodes, cells), shape(cells, 2 * lanes, dtype=BF16)),
        in_specs=[vmem] * 2 + [hbm] + [vmem] * 7,
        scratch_shapes=[pltpu.VMEM(visc.shape, F32), pltpu.SemaphoreType.DMA((1,))],
        out_specs=(vmem,) * 2,
        compiler_params=params,
        cost_estimate=estimate(comps * cells),
        name="middle",
    )(got_za, con, pltpu.with_memory_space_constraint(visc, pltpu.HBM), offsets, matrix, config, got_xa, got_xb, got_zb, targets)

    rims = pl.pallas_call(
        functools.partial(rim, dims, axes, mesh_sizes, fast),
        out_shape=shape(comps * nodes, len(outer_blocks(cx, cy)) * cz),
        in_specs=[vmem] * 5,
        out_specs=vmem,
        compiler_params=params,
        cost_estimate=estimate(comps * cells),
        name="rim",
    )(total, got_yb, got_ya, matrix, config)

    out, deform = pl.pallas_call(
        functools.partial(after, dims, axes, fast),
        out_shape=(shape(*v.shape), shape(9, 1, slots)),
        in_specs=[vmem] * (5 + len(parts)),
        out_specs=(hbm, hbm),
        scratch_shapes=[
            pltpu.VMEM(v.shape, F32),
            pltpu.VMEM(strain.shape, F32),
            pltpu.SemaphoreType.DMA((comps + 1,)),
        ],
        compiler_params=params,
        name="after",
    )(total, *parts, rims, hot, weights, own)
    return out.reshape(velocity.shape), deform.reshape(strain_offsets.shape)


def solution(mesh):
    sizes = tuple(mesh.shape[a] for a in ("dx", "dy", "solid"))
    return jax.shard_map(
        functools.partial(shards, sizes),
        mesh=mesh,
        in_specs=(
            P(None, None, None, None, "dx", "dy", "solid"),
            P("dx", "dy", "solid"),
            P("dx", "dy", "solid"),
            P(),
            P("dx", ("dy", "solid"), None),
            P(None, "dx", ("dy", "solid"), None),
            P(None, None, "dx", ("dy", "solid"), None),
            P(None, "dx", ("dy", "solid"), None),
        ),
        out_specs=(
            P(None, None, None, None, "dx", "dy", "solid"),
            P(None, None, "dx", ("dy", "solid"), None),
        ),
        check_vma=False,
    )
```

```python
import functools

import jax
import jax.numpy as jnp
from jax import lax
from jax.experimental import pallas as pl
from jax.experimental.pallas import tpu as pltpu
from jax.sharding import PartitionSpec as P

TIME_STEP = 0.05
SPRING_RATE = 2.0
PENALTY = 4.0
NODE_POINTS = (0.0, 1.0 / 3.0, 2.0 / 3.0, 1.0)
F32, BF16 = jnp.float32, jnp.bfloat16
VMEM_LIMIT = 24 * 1024 * 1024


def iota(shape, dim):
    return lax.broadcasted_iota(jnp.int32, shape, dim)


def split(x):
    high = x.astype(BF16)
    low = (x - high.astype(F32)).astype(BF16)
    return high, low


def dot(a, b, dims=((1,), (0,))):
    return lax.dot_general(a, b, (dims, ((), ())), preferred_element_type=F32)


def lagrange(coord):
    values = []
    slopes = []
    for which in range(4):
        others = [NODE_POINTS[j] for j in range(4) if j != which]
        denom = 1.0
        for other in others:
            denom = denom * (NODE_POINTS[which] - other)
        scale = 1.0 / denom
        first = coord - others[0]
        second = coord - others[1]
        third = coord - others[2]
        values.append(first * second * third * scale)
        slopes.append((second * third + first * third + first * second) * scale)
    return values, slopes


def spread_rows(parts, dim, lanes):
    wide = [jnp.broadcast_to(p, (8, lanes)) for p in parts]
    if dim == 0:
        return jnp.concatenate([wide[a] for a in (0, 0, 1, 1, 2, 2, 3, 3)], axis=0)
    row = iota((8, lanes), 0)
    if dim == 1:
        even = jnp.where(row < 4, wide[0], wide[1])
        odd = jnp.where(row < 4, wide[2], wide[3])
        return jnp.concatenate([even, odd] * 4, axis=0)
    c = row & 3
    block = jnp.where(c == 0, wide[0], jnp.where(c == 1, wide[1], jnp.where(c == 2, wide[2], wide[3])))
    return jnp.concatenate([block] * 8, axis=0)


def shapes_of(xi, lanes):
    out = []
    for dim in range(3):
        values, slopes = lagrange(xi[dim])
        out.append((spread_rows(values, dim, lanes), spread_rows(slopes, dim, lanes)))
    return out


def one_hot(slots, cells):
    lanes = slots.shape[1]
    return jnp.where(iota((cells, lanes), 0) == slots, 1.0, 0.0).astype(BF16)


def configured(product, config, nconf):
    rows = product.shape[0] // nconf
    chosen = product[:rows]
    for which in range(1, nconf):
        chosen = jnp.where(config == which, product[which * rows : (which + 1) * rows], chosen)
    return chosen


def tripled(high, low):
    return jnp.concatenate([high, low, high], axis=0)


def turned_parts(high, low):
    return jnp.concatenate([high, high, low], axis=0)


def constrain(matrix, columns, config_rows, store, nconf, comps, blocks, lanes):
    step = 2 if blocks % 2 == 0 else 1
    for k in range(comps):
        for first in range(0, blocks, step):
            values, parts = columns(k, range(first, first + step))
            product = dot(matrix, parts)
            for i in range(step):
                piece = product[:, i * lanes : (i + 1) * lanes]
                store(k, first + i, values[i] + configured(piece, config_rows[first + i], nconf))


def fetch(pairs, sems):
    copies = [pltpu.make_async_copy(src, dst, sems.at[i]) for i, (src, dst) in enumerate(pairs)]
    for copy in copies:
        copy.start()
    return copies


def plain_matrix(offsets):
    high, low = split(offsets)
    return jnp.concatenate([high, high, low], axis=1)


def turned_matrix(offsets, nconf, nodes):
    blocks = [offsets[w * nodes : (w + 1) * nodes, :] for w in range(nconf)]
    highs, lows = [], []
    for block in blocks:
        high = block.astype(BF16).astype(F32)
        both = jnp.concatenate([high, block - high], axis=0).T.astype(BF16)
        highs.append(both)
        lows.append(both[:, :nodes])
    return jnp.concatenate([jnp.concatenate(highs, axis=0), jnp.concatenate(lows, axis=0)], axis=1)


def begin(
    dims, axes, fast,
    v_hbm, config_hbm, offset_hbm, slot_hbm, xi_hbm, strain_hbm, motion_hbm, viscosity_hbm,
    talk_ref, self_ref, own_ref, split_ref, matrix_ref, target_ref, weight_ref, config_ref, offset_ref, viscosity_ref,
    v_ref, slot_ref, xi_ref, strain_ref, motion_ref, sems,
):
    comps, nodes, cx, cy, cz, nconf, slots, lanes = dims
    blocks = cx * cy
    cells = blocks * cz
    copies = fetch(
        [(v_hbm, v_ref), (offset_hbm, offset_ref), (slot_hbm, slot_ref), (config_hbm, config_ref), (xi_hbm, xi_ref),
         (strain_hbm, strain_ref), (motion_hbm, motion_ref), (viscosity_hbm, viscosity_ref)],
        sems,
    )

    for copy in copies:
        copy.wait()
    targets = jnp.concatenate([slot_ref[...]] * 2, axis=1)
    target_ref[...] = targets
    wide = 2 * blocks
    columns = pl.cdiv(slots + wide, 128) * 128
    lane = iota((1, columns), 1)
    both = jnp.concatenate([slot_ref[...], jnp.full((1, columns - slots), -1, jnp.int32)], axis=1)
    for y in range(blocks):
        both = jnp.where(lane == columns - wide + y, y * cz, both)
        both = jnp.where(lane == columns - blocks + y, (y + 1) * cz - 1, both)
    hot = one_hot(both, cells)
    config = jnp.concatenate([config_ref[y : y + 1, :] for y in range(blocks)], axis=1)
    config = dot(jnp.broadcast_to(config.astype(F32), (16, cells)).astype(BF16), hot)[0:1, :]

    half = iota((1, lanes), 1) < slots

    def twice(x):
        if 2 * slots == columns:
            return jnp.where(iota(x.shape, 1) < slots, x, pltpu.roll(x, slots, axis=1))
        return jnp.concatenate([x[:, :slots]] * 2, axis=1)

    config_twice = twice(config)
    xi = [jnp.concatenate([xi_ref[j]] * 2, axis=1) for j in range(3)]
    (px, dx), (py, dy), (pz, dz) = shapes_of(xi, lanes)
    basis = (jnp.where(half, px, dx) * (py * pz), px * jnp.where(half, dy * pz, py * dz))
    matrix = turned_matrix(offset_ref[...], nconf, nodes)
    matrix_ref[...] = matrix
    raw = []
    for k in range(comps):
        row = 2 * k * nodes
        for y in range(blocks):
            high, low = split(v_ref[pl.ds(k * nodes * blocks + y, nodes, stride=blocks), :])
            at = slice(y * cz, (y + 1) * cz)
            split_ref[row : row + nodes, at] = high
            split_ref[row + nodes : row + 2 * nodes, at] = low
        both = dot(split_ref[row : row + 2 * nodes, :], hot)
        raw.append(both[:nodes] + both[nodes:])
    product = dot(matrix, jnp.concatenate([turned_parts(*split(p)) for p in basis], axis=1))
    weights = []
    for j in range(2):
        weights.append(basis[j] + configured(product[:, j * lanes : (j + 1) * lanes], config_twice, nconf))
        weight_ref[j * nodes : (j + 1) * nodes, :] = weights[j]

    count = comps * nodes // 16
    ends = jnp.concatenate([r[:, columns - 128 :] for r in raw], axis=0)
    lane = iota((16, 128), 1)
    at_end = 128 - wide
    packed = jnp.broadcast_to(pltpu.roll(config[:, columns - 128 :], (count * wide - at_end) % 128, axis=1), (16, 128))
    for g in range(count):
        group = pltpu.roll(ends[16 * g : 16 * (g + 1)], (g * wide - at_end) % 128, axis=1)
        packed = jnp.where((lane >= g * wide) & (lane < (g + 1) * wide), group, packed)
    talk_ref[talk_ref.shape[0] - 16 :, :] = packed
    for k in range(comps):
        value = twice(raw[k])
        for j in range(2):
            sums = jnp.sum(value * weights[j], axis=0, keepdims=True)
            other = pltpu.roll(sums, slots, axis=1)
            left, right = ((k, 3 + 3 * k), (4 + 3 * k, 5 + 3 * k))[j]
            own_ref[left : left + 1, :] = jnp.where(half, sums, other)
            own_ref[right : right + 1, :] = jnp.where(half, other, sums)
    for i in range(9):
        own_ref[16 + i : 17 + i, :] = jnp.concatenate([strain_ref[i]] * 2, axis=1)
    for i in range(3):
        own_ref[25 + i : 26 + i, :] = jnp.concatenate([motion_ref[i]] * 2, axis=1)
    for i in (12, 28):
        own_ref[i : i + 4, :] = jnp.zeros((4, lanes), F32)

    if fast:
        parts = jnp.where(lane < slots, own_ref[0:16, :], own_ref[16:32, :])
        self_ref[...] = parts
        talk_ref[0:16, :] = jnp.where(lane & 8 == 0, pltpu.roll(parts, 120, axis=1), pltpu.roll(parts, 8, axis=1))
    else:
        self_ref[...] = jnp.zeros_like(self_ref)


def local(
    dims, axes,
    split_ref, offset_ref, config_ref,
    con_ref, xa_ref, xb_ref, ya_ref, yb_ref,
    field_ref,
):
    comps, nodes, cx, cy, cz, nconf, slots, lanes = dims
    blocks = cx * cy
    me_x, me_y = lax.axis_index(axes[0]), lax.axis_index(axes[1])
    even_x, even_y = me_x % 2 == 0, me_y % 2 == 0
    config_rows = [config_ref[y : y + 1, :] for y in range(blocks)]

    def columns(k, ys):
        at = slice(ys[0] * cz, (ys[-1] + 1) * cz)
        high = split_ref[2 * k * nodes : (2 * k + 1) * nodes, at]
        low = split_ref[(2 * k + 1) * nodes : (2 * k + 2) * nodes, at]
        value = high.astype(F32) + low.astype(F32)
        return [value[:, i * cz : (i + 1) * cz] for i in range(len(ys))], tripled(high, low)

    def store(k, y, value):
        field_ref[(y * comps + k) * nodes : (y * comps + k + 1) * nodes, :] = value
        part, rest = split(value)
        row = 2 * k * nodes
        con_ref[row : row + nodes, y * cz : (y + 1) * cz] = part
        con_ref[row + nodes : row + 2 * nodes, y * cz : (y + 1) * cz] = rest

    constrain(plain_matrix(offset_ref[...]), columns, config_rows, store, nconf, comps, blocks, cz)

    face = nodes // 4
    for k in range(comps):
        for y in range(cy):
            low_row = (y * comps + k) * nodes
            up_row = (((cx - 1) * cy + y) * comps + k + 1) * nodes
            lower = field_ref[low_row : low_row + face, :]
            upper = field_ref[up_row - face : up_row, :]
            cells = slice(y * cz, (y + 1) * cz)
            xa_ref[k * face : (k + 1) * face, cells] = jnp.where(even_x, upper, lower)
            xb_ref[k * face : (k + 1) * face, cells] = jnp.where(even_x, lower, upper)
        for a in range(4):
            into = k * face + a * 4
            for x in range(cx):
                first = (x * cy * comps + k) * nodes + a * face
                last = ((x * cy + cy - 1) * comps + k) * nodes + a * face
                lower = field_ref[first : first + 4, :]
                upper = field_ref[last + 12 : last + 16, :]
                ya_ref[into : into + 4, x * cz : (x + 1) * cz] = jnp.where(even_y, upper, lower)
                yb_ref[into : into + 4, x * cz : (x + 1) * cz] = jnp.where(even_y, lower, upper)


def solid(vel, grad, strain, motion):
    deform = [strain[3 * j + l] + (1.0 if j == l else 0.0) for j in range(3) for l in range(3)]
    moved = []
    for k in range(3):
        for l in range(3):
            change = sum(grad[3 * k + j] * deform[3 * j + l] for j in range(3))
            moved.append(deform[3 * k + l] + TIME_STEP * change)
    stress = [
        sum(moved[3 * k + l] * moved[3 * m + l] for l in range(3)) - (1.0 if k == m else 0.0)
        for k in range(3) for m in range(3)
    ]
    drag = [SPRING_RATE * (motion[k] - vel[k]) for k in range(3)]
    return moved, stress, drag


def node_tables():
    i, j = iota((64, 64), 0), iota((64, 64), 1)
    digits = [((i >> s) & 3, (j >> s) & 3) for s in (4, 2, 0)]
    same = [p == q for p, q in digits]
    lap = jnp.zeros((64, 64), F32)
    swaps = []
    for d in range(3):
        others = same[(d + 1) % 3] & same[(d + 2) % 3]
        p, q = digits[d]
        line = jnp.where(p == q, 2.0, jnp.where((p - q == 1) | (q - p == 1), -1.0, 0.0))
        lap = lap + jnp.where(others, line, 0.0)
        swaps.append(jnp.where(others & (((p == 0) & (q == 3)) | ((p == 3) & (q == 0))), 1.0, 0.0))
    return jnp.concatenate([lap, swaps[2], swaps[1]], axis=0).astype(BF16)


def sides(even, open_b, a, b):
    b = jnp.where(open_b, b, 0.0)
    return jnp.where(even, b, a), jnp.where(even, a, b)


def place(axis, n):
    index = lax.axis_index(axis)
    even = index % 2 == 0
    return even, jnp.where(even, index, n - 1 - index) > 0


def middle(
    dims, axes, sizes, fast,
    za_ref, con_ref, viscosity_ref, offset_ref, matrix_ref, config_ref, xa_ref, xb_ref, zb_ref, target_ref,
    total_ref, hot_ref,
):
    comps, nodes, cx, cy, cz, nconf, slots, lanes = dims
    blocks = cx * cy
    face = nodes // 4
    even_x, open_x = place(axes[0], sizes[0])
    even_z, open_z = place(axes[2], sizes[2])

    table = node_tables()
    table = jnp.concatenate([table, table], axis=1)
    row = iota((nodes, cz), 0)
    a, b, c = (row >> 4) & 3, (row >> 2) & 3, row & 3

    def ends(p):
        return jnp.where((p == 0) | (p == 3), PENALTY, 0.0)

    keep = 1.0 + ends(a) + ends(b) + ends(c)
    lane = iota((nodes, cz), 1)
    count = comps * nodes // 16
    wide = 2 * blocks
    plain = plain_matrix(offset_ref[...])
    hot_ref[...] = one_hot(jnp.concatenate([target_ref[...]] * 2, axis=1), blocks * cz)

    def ends_of(ref):
        packed = ref[ref.shape[0] - 16 :, :]
        config = pltpu.roll(packed, (128 - count * wide) % 128, axis=1)
        groups = [pltpu.roll(packed, (128 - g * wide) % 128, axis=1) for g in range(count)]
        rows = jnp.concatenate(groups, axis=0)
        raw = rows[:nodes]
        spread_config = config[0:1]
        for k in range(1, comps):
            here = lane >= k * wide
            raw = jnp.where(here, pltpu.roll(rows[k * nodes : (k + 1) * nodes], k * wide, axis=1), raw)
            spread_config = jnp.where(here[0:1], pltpu.roll(config, k * wide, axis=1)[0:1], spread_config)
        raw = jnp.where(lane < comps * wide, raw, 0.0)
        return raw + configured(dot(plain, tripled(*split(raw))), spread_config, nconf)

    z_a = ends_of(za_ref)
    z_low, z_up = sides(even_z, open_z, z_a, z_a if fast else ends_of(zb_ref))
    z_low, z_up = pltpu.roll(z_low, nodes - 3, axis=0), pltpu.roll(z_up, 3, axis=0)
    config_rows = [config_ref[y : y + 1, :] for y in range(blocks)]
    matrix = matrix_ref[...]

    for k in range(comps):
        pair = con_ref[2 * k * nodes : 2 * (k + 1) * nodes, :]
        ops = dot(table, pair)
        rows = slice(k * face, (k + 1) * face)
        x_low, x_up = sides(even_x, open_x, xa_ref[rows, :], xb_ref[rows, :])
        values = []
        for y in range(blocks):
            x_at, y_at = y // cy, y % cy
            cells = slice(y * cz, (y + 1) * cz)
            value = pair[:nodes, cells].astype(F32) + pair[nodes:, cells].astype(F32)
            total = keep * value + viscosity_ref[y : y + 1, :] * ops[0:nodes, cells]
            moved_z = ops[nodes : 2 * nodes, cells]
            below = jnp.where(lane == 0, pltpu.roll(z_low, cz - k * wide - blocks - y, axis=1), pltpu.roll(moved_z, 1, axis=1))
            above = jnp.where(
                lane == cz - 1, pltpu.roll(z_up, cz - 1 - k * wide - y, axis=1), pltpu.roll(moved_z, cz - 1, axis=1)
            )
            near = jnp.where(c == 0, below, jnp.where(c == 3, above, 0.0))
            if y_at > 0:
                near = near + jnp.where(b == 0, ops[2 * nodes : 3 * nodes, (y - 1) * cz : y * cz], 0.0)
            if y_at < cy - 1:
                near = near + jnp.where(b == 3, ops[2 * nodes : 3 * nodes, (y + 1) * cz : (y + 2) * cz], 0.0)
            total = total - PENALTY * near
            plane = slice(y_at * cz, (y_at + 1) * cz)
            if x_at > 0:
                other = slice((y - cy) * cz, (y - cy + 1) * cz)
                below = pair[nodes - face : nodes, other].astype(F32) + pair[2 * nodes - face :, other].astype(F32)
            else:
                below = x_low[:, plane]
            if x_at < cx - 1:
                other = slice((y + cy) * cz, (y + cy + 1) * cz)
                above = pair[:face, other].astype(F32) + pair[nodes : nodes + face, other].astype(F32)
            else:
                above = x_up[:, plane]
            total = jnp.concatenate(
                [total[:face] - PENALTY * below, total[face : nodes - face], total[nodes - face :] - PENALTY * above],
                axis=0,
            )
            values.append(total)
        inner = [y for y in range(blocks) if 0 < y % cy < cy - 1]
        if inner:
            product = dot(matrix, turned_parts(*split(jnp.concatenate([values[y] for y in inner], axis=1))))
            for i, y in enumerate(inner):
                values[y] = values[y] + configured(product[:, i * cz : (i + 1) * cz], config_rows[y], nconf)
        for y in range(blocks):
            total_ref[k * nodes : (k + 1) * nodes, y * cz : (y + 1) * cz] = values[y]


def outer_blocks(cx, cy):
    return [y for y in range(cx * cy) if y % cy in (0, cy - 1)]


def widen(face, nodes):
    return jnp.concatenate([face[4 * (i // 4) : 4 * (i // 4) + 4] for i in range(nodes // 4)], axis=0)


def gather_parts(refs, axes):
    me_y, me_s = lax.axis_index(axes[1]), lax.axis_index(axes[2])
    lane = iota((16, 128), 1)
    parts = jnp.zeros((16, 128), F32)
    for bits, ref in enumerate(refs):
        block = ref[0:16, :]
        if bits == 2:
            block = jnp.concatenate([block[8:], block[:8]], axis=0)
        for side in range(2):
            place = me_y * 2 + (me_s ^ side)
            source = (me_y ^ bits) * 2 + (me_s ^ side)
            moved = pltpu.roll(block, ((source - place) * 8) & 127, axis=1)
            parts = jnp.where((lane & 63) >> 3 == source, moved, parts)
    other = pltpu.roll(parts, 64, axis=1)
    return jnp.concatenate([jnp.where(lane < 64, parts, other), jnp.where(lane < 64, other, parts)], axis=0)


def rim(
    dims, axes, sizes, fast,
    total_ref, yb_ref, ya_ref, matrix_ref, config_ref,
    rim_ref,
):
    comps, nodes, cx, cy, cz, nconf, slots, lanes = dims
    face = nodes // 4
    even_y, open_y = place(axes[1], sizes[1])
    first = 16 if fast else 0
    b = (iota((nodes, cz), 0) >> 2) & 3
    matrix = matrix_ref[...]
    for k in range(comps):
        rows = slice(first + k * face, first + (k + 1) * face)
        y_low, y_up = sides(even_y, open_y, ya_ref[rows, :], yb_ref[rows, :])
        outer = outer_blocks(cx, cy)
        values = []
        for y in outer:
            plane = slice(y // cy * cz, (y // cy + 1) * cz)
            value = total_ref[k * nodes : (k + 1) * nodes, y * cz : (y + 1) * cz]
            if y % cy == 0:
                value = value - jnp.where(b == 0, PENALTY * widen(y_low[:, plane], nodes), 0.0)
            if y % cy == cy - 1:
                value = value - jnp.where(b == 3, PENALTY * widen(y_up[:, plane], nodes), 0.0)
            values.append(value)
        product = dot(matrix, turned_parts(*split(jnp.concatenate(values, axis=1))))
        for i, y in enumerate(outer):
            at = slice(i * cz, (i + 1) * cz)
            rim_ref[k * nodes : (k + 1) * nodes, at] = values[i] + configured(product[:, at], config_ref[y : y + 1, :], nconf)


def after(
    dims, axes, fast,
    total_ref, *refs,
):
    comps, nodes, cx, cy, cz, nconf, slots, lanes = dims
    blocks = cx * cy
    if fast:
        got_3, got_2, got_1, pair_ref, *refs = refs
        part_refs = (pair_ref, got_1, got_2, got_3)
    else:
        *part_refs, refs = refs[0], refs[1:]
    rim_ref, hot_ref, weight_ref, own_ref, out_hbm, deform_hbm, out_ref, deform_ref, sems = refs

    parts = gather_parts(part_refs, axes) if fast else part_refs[0][...]
    own = [own_ref[i : i + 1, :] for i in range(32)]
    got = [parts[i : i + 1, :] for i in range(32)]
    _, stress, drag = solid(own[0:3], own[3:12], got[16:25], got[25:28])
    moved, _, _ = solid(got[0:3], got[3:12], own[16:25], own[25:28])
    for i in range(9):
        deform_ref[i] = moved[i][:, :slots]
    copies = [pltpu.make_async_copy(deform_ref, deform_hbm, sems.at[comps])]
    copies[0].start()
    hot = hot_ref[...]
    half = iota((1, lanes), 1) < slots
    highs, lows = [], []
    for k in range(comps):
        force = jnp.where(half, drag[k], -stress[3 * k]) * weight_ref[:nodes, :]
        force = force - jnp.where(half, stress[3 * k + 1], stress[3 * k + 2]) * weight_ref[nodes:, :]
        high, low = split(force)
        highs.append(high)
        lows.append(low)
    pieces = jnp.concatenate([jnp.concatenate(highs, axis=0), jnp.concatenate(lows, axis=0)], axis=1)
    spreads = dot(pieces, hot, ((1,), (1,)))

    outer = outer_blocks(cx, cy)
    for k in range(comps):
        rows = slice(k * nodes, (k + 1) * nodes)
        for y in range(blocks):
            cells = slice(y * cz, (y + 1) * cz)
            if y in outer:
                value = rim_ref[rows, outer.index(y) * cz : (outer.index(y) + 1) * cz]
            else:
                value = total_ref[rows, cells]
            out_ref[pl.ds(k * nodes * blocks + y, nodes, stride=blocks), :] = value - spreads[rows, cells]
        done = slice(k * nodes * blocks, (k + 1) * nodes * blocks)
        copies.append(pltpu.make_async_copy(out_ref.at[done, :], out_hbm.at[done, :], sems.at[k]))
        copies[-1].start()
    for copy in copies:
        copy.wait()


def swap(x, axis, stage):
    n = lax.axis_size(axis)
    pairs = [(i, i + 1) for i in range(stage, n - 1, 2)]
    if not pairs:
        return jnp.zeros_like(x)
    return lax.ppermute(x, axis, pairs + [(j, i) for i, j in pairs])


def flip(x, axis, bits):
    return lax.ppermute(x, axis, [(i, i ^ bits) for i in range(lax.axis_size(axis))])


def shards(
    mesh_sizes,
    velocity,
    viscosity,
    cell_config,
    constraint_offsets,
    slot_cells,
    point_coords,
    strain_offsets,
    solid_velocity,
):
    axes = ("dx", "dy", "solid")
    comps, cx, cy, cz = velocity.shape[0], *velocity.shape[4:]
    nodes = velocity.shape[1] * velocity.shape[2] * velocity.shape[3]
    blocks = cx * cy
    nconf = constraint_offsets.shape[0]
    slots = slot_cells.shape[-1]
    n_dx, n_dy, n_solid = mesh_sizes
    face_rows = comps * nodes // 4
    lanes = 2 * slots
    dims = (comps, nodes, cx, cy, cz, nconf, slots, lanes)

    v = velocity.reshape(comps * nodes * blocks, cz)
    visc = viscosity.reshape(blocks, cz)
    config = cell_config.reshape(blocks, cz)
    offsets = constraint_offsets.reshape(nconf * nodes, nodes)
    targets = slot_cells.reshape(1, slots)
    xi = point_coords.reshape(3, 1, slots)
    strain = strain_offsets.reshape(9, 1, slots)
    motion = solid_velocity.reshape(3, 1, slots)

    vmem = pl.BlockSpec(memory_space=pltpu.VMEM)
    hbm = pl.BlockSpec(memory_space=pltpu.HBM)
    params = pltpu.CompilerParams(vmem_limit_bytes=VMEM_LIMIT)
    cells = blocks * cz
    face_y = jax.ShapeDtypeStruct((face_rows, cx * cz), F32)
    face_x = jax.ShapeDtypeStruct((face_rows, cy * cz), F32)
    def shape(*size, dtype=F32):
        return jax.ShapeDtypeStruct(size, dtype)

    def estimate(columns):
        return pl.CostEstimate(flops=2 * 6 * nconf * nodes * nodes * columns, bytes_accessed=1_000_000, transcendentals=0)

    fast = (n_dx, n_dy, n_solid, slots) == (4, 4, 2, 64)
    talk, mine, own, parted, matrix, targets, weights, config, offsets, visc = pl.pallas_call(
        functools.partial(begin, dims, axes, fast),
        out_shape=(
            shape(32 if fast else 16, 128),
            shape(16, 128),
            shape(32, lanes),
            shape(2 * comps * nodes, cells, dtype=BF16),
            shape(nconf * nodes, 3 * nodes, dtype=BF16),
            shape(1, lanes, dtype=targets.dtype),
            shape(2 * nodes, lanes),
            shape(*config.shape, dtype=config.dtype),
            shape(*offsets.shape),
            shape(*visc.shape),
        ),
        in_specs=[hbm] * 8,
        out_specs=(vmem,) * 10,
        scratch_shapes=[
            pltpu.VMEM(v.shape, F32),
            pltpu.VMEM(targets.shape, targets.dtype),
            pltpu.VMEM(xi.shape, F32),
            pltpu.VMEM(strain.shape, F32),
            pltpu.VMEM(motion.shape, F32),
            pltpu.SemaphoreType.DMA((8,)),
        ],
        compiler_params=params,
        name="begin",
    )(*(pltpu.with_memory_space_constraint(x, pltpu.HBM) for x in (v, config, offsets, targets, xi, strain, motion, visc)))

    con, xa, xb, ya, yb = pl.pallas_call(
        functools.partial(local, dims, axes),
        out_shape=(shape(2 * comps * nodes, cells, dtype=BF16), face_x, face_x, face_y, face_y),
        in_specs=[vmem] * 3,
        out_specs=(vmem,) * 5,
        scratch_shapes=[pltpu.VMEM((blocks * comps * nodes, cz), F32)],
        compiler_params=params,
        cost_estimate=estimate(comps * cells),
        name="local",
    )(parted, offsets, config)

    if fast:
        got_s = swap(talk, "solid", 0)
        got_xa = swap(xa, "dx", 0)
        got_xb = flip(xb, "dx", 3)
        own_side = (iota((16, 128), 1) >> 3) & 1 == lax.axis_index("solid")
        pair = jnp.where(own_side, mine, got_s[:16])
        got_3 = flip(jnp.concatenate([pair, yb], axis=0), "dy", 3)
        got_2 = flip(jnp.concatenate([pair[8:], pair[:8]], axis=0), "dy", 2)
        got_1 = flip(jnp.concatenate([pair, ya], axis=0), "dy", 1)
        parts = [got_3, got_2, got_1, pair]
        got_ya, got_yb = got_1, got_3
        got_za, got_zb = got_s, got_s
    else:
        got_xa, got_xb = swap(xa, "dx", 0), swap(xb, "dx", 1)
        got_ya, got_yb = swap(ya, "dy", 0), swap(yb, "dy", 1)
        got_za, got_zb = swap(talk, "solid", 0), swap(talk, "solid", 1)
        sent = jnp.concatenate([own[:12, :slots], own[16:28, :slots]], axis=0)
        got_parts = lax.all_to_all(sent, ("dy", "solid"), split_axis=1, concat_axis=1, tiled=True)
        got_parts = jnp.pad(got_parts.reshape(2, 12, slots), ((0, 0), (0, 4), (0, 0))).reshape(32, slots)
        parts = [jnp.concatenate([got_parts] * 2, axis=1)]

    total, hot = pl.pallas_call(
        functools.partial(middle, dims, axes, mesh_sizes, fast),
        out_shape=(shape(comps * nodes, cells), shape(cells, 2 * lanes, dtype=BF16)),
        in_specs=[vmem] * 10,
        out_specs=(vmem,) * 2,
        compiler_params=params,
        cost_estimate=estimate(comps * cells),
        name="middle",
    )(got_za, con, visc, offsets, matrix, config, got_xa, got_xb, got_zb, targets)

    rims = pl.pallas_call(
        functools.partial(rim, dims, axes, mesh_sizes, fast),
        out_shape=shape(comps * nodes, len(outer_blocks(cx, cy)) * cz),
        in_specs=[vmem] * 5,
        out_specs=vmem,
        compiler_params=params,
        cost_estimate=estimate(comps * cells),
        name="rim",
    )(total, got_yb, got_ya, matrix, config)

    out, deform = pl.pallas_call(
        functools.partial(after, dims, axes, fast),
        out_shape=(shape(*v.shape), shape(9, 1, slots)),
        in_specs=[vmem] * (5 + len(parts)),
        out_specs=(hbm, hbm),
        scratch_shapes=[
            pltpu.VMEM(v.shape, F32),
            pltpu.VMEM(strain.shape, F32),
            pltpu.SemaphoreType.DMA((comps + 1,)),
        ],
        compiler_params=params,
        name="after",
    )(total, *parts, rims, hot, weights, own)
    return out.reshape(velocity.shape), deform.reshape(strain_offsets.shape)


def solution(mesh):
    sizes = tuple(mesh.shape[a] for a in ("dx", "dy", "solid"))
    return jax.shard_map(
        functools.partial(shards, sizes),
        mesh=mesh,
        in_specs=(
            P(None, None, None, None, "dx", "dy", "solid"),
            P("dx", "dy", "solid"),
            P("dx", "dy", "solid"),
            P(),
            P("dx", ("dy", "solid"), None),
            P(None, "dx", ("dy", "solid"), None),
            P(None, None, "dx", ("dy", "solid"), None),
            P(None, "dx", ("dy", "solid"), None),
        ),
        out_specs=(
            P(None, None, None, None, "dx", "dy", "solid"),
            P(None, None, "dx", ("dy", "solid"), None),
        ),
        check_vma=False,
    )
```
